256 devices in a mesh: lon: 64 (over z, y, x_lo), lat: 4 (over x_hi, core).
Axes of the slice: x: 4 (x_hi: 2, x_lo: 2; x = x_hi * 2 + x_lo), y: 4, z: 8, core: 2. Of those that a mesh axis runs over, the one named last changes fastest.
Arguments:
- tokens: bfloat16 [4, 72, 768, 192], P(None, 'lat', 'lon'), may hold values from -6 to 6
- cotangent: bfloat16 [4, 72, 768, 192], P(None, 'lat', 'lon'), may hold values from -6 to 6
- labels: int32 [4, 72, 768], P(None, 'lat', 'lon'), may hold values from 0 to 3
- w_qkv: bfloat16 [192, 576], replicated, may hold values from -0.4375 to 0.4375
- w_proj: bfloat16 [192, 192], replicated, may hold values from -0.4375 to 0.4375
- logit_scale: float32 [6], replicated, may hold values from 1 to 3.5
- bias_table: float32 [12, 2, 6, 3312], P('lat'), may hold values from -120 to 180
- bias_index: int32 [144, 144], replicated, may hold values from 0 to 3311
- norm_gain: float32 [192], replicated, may hold values from 0.5 to 1.5
Outputs:
- grad_tokens: bfloat16 [4, 72, 768, 192], P(None, 'lat', 'lon')
- grad_qkv: float32 [192, 576], replicated
- grad_proj: float32 [192, 192], replicated
- grad_scale: float32 [6], replicated
- grad_bias: float32 [12, 2, 6, 3312], P('lat')
- grad_gain: float32 [192], replicated
The draws below stay inside these ranges and needn't reach their ends.
All inputs are finite; a program needn't handle non-finite values.
Results may differ from the reference program's by a relative error of at most 0.012.
The reference program's roundings to bfloat16 on the way count: a program that leaves them out, or rounds other values in their place, can miss the bound.
Values may be sent and summed in bfloat16 or wider, within the bound.
No kernel may reach another device: no remote copies, remote signals or barrier semaphores. Data moves between devices by JAX's collectives and lax.ppermute only.
A program may use at most 256 MiB of HBM per device.

```python
import jax
import jax.numpy as jnp
from jax import lax

C = 192
HEADS = 6
WINDOW = 144
NB = 3312
ZL = 4
LAT = 72
LON = 768


def draw_bias_table(key, part):
    key = jax.random.fold_in(key, 11)
    second_key = jax.random.fold_in(key, 1)
    table_shape = (LAT // 6, ZL // 2, HEADS, NB)
    return jax.random.uniform(second_key, table_shape, jnp.float32, -2.0, 2.0)


def plant(drawn, key, least, top_value):
    index_at = [jax.random.randint(jax.random.fold_in(key, axis), (), 0, length) for axis, length in enumerate(drawn.shape)]
    longest = drawn.shape.index(max(drawn.shape))
    beside = index_at[:longest] + [(index_at[longest] + 1) % drawn.shape[longest]] + index_at[longest + 1:]
    return drawn.at[tuple(index_at)].set(least).at[tuple(beside)].set(top_value)


def block_scale(stream_key, shape, cuts, smallest, largest):
    level, own = 1.0, jax.random.fold_in(stream_key, 6)
    for axis_at, parts in cuts:
        draws = jnp.exp(jax.random.uniform(jax.random.fold_in(own, axis_at), (parts,), jnp.float32, smallest / len(cuts), largest / len(cuts)))
        level = level * jnp.repeat(draws, shape[axis_at] // parts).reshape([-1 if axis == axis_at else 1 for axis in range(len(shape))])
    return level


def scatter_about(rng, extent, scale, reach, pieces=(), kind=jnp.bfloat16):
    level = block_scale(rng, extent, pieces, -0.22, 0.18) if pieces else 1.0
    values = jax.random.normal(rng, extent, jnp.float32) * scale * level
    return jnp.minimum(jnp.maximum(values, -reach), reach).astype(kind)


def setup_inputs(seed: int = 0) -> dict:
    keys = jax.random.split(jax.random.key(seed), 10)
    return {
        "tokens": scatter_about(keys[0], (ZL, LAT, LON, C), 1.0, 6.0, ((1, 4), (2, 64))),
        "cotangent": scatter_about(keys[1], (ZL, LAT, LON, C), 1.0, 6.0, ((1, 4), (2, 64))),
        "labels": plant(jax.random.randint(keys[2], (ZL, LAT, LON), 0, 4), jax.random.fold_in(keys[2], 1), 0, 3).astype(jnp.int32),
        "w_qkv": scatter_about(keys[3], (C, 3 * C), C ** -0.5, 0.4375),
        "w_proj": scatter_about(keys[4], (C, C), C ** -0.5, 0.4375),
        "logit_scale": jnp.clip(jax.random.uniform(keys[5], (HEADS,), jnp.float32, 1.0, 3.5), 1.0, 3.5),
        "bias_table": draw_bias_table(jax.random.fold_in(keys[9], 71), 0),
        "bias_index": plant(jax.random.randint(keys[7], (WINDOW, WINDOW), 0, NB), jax.random.fold_in(keys[7], 1), 0, NB - 1).astype(jnp.int32),
        "norm_gain": jnp.clip(1.0 + 0.1 * jax.random.normal(keys[8], (C,), jnp.float32), 0.5, 1.5),
    }


NEG_FILL = -1e+30

def to_windows(field):
    levels_n, rows_n, cols_n = (field.shape[0], field.shape[1], field.shape[2])
    trailing = field.shape[3:]
    blocks = field.reshape((levels_n // 2, 2, rows_n // 6, 6, cols_n // 12, 12) + trailing)
    axes_order = (2, 0, 4, 1, 3, 5) + tuple(range(6, 6 + len(trailing)))
    blocks = blocks.transpose(axes_order)
    return blocks.reshape((rows_n // 6 * (levels_n // 2), cols_n // 12, 144) + trailing)

def from_windows(blocks, levels_n, rows_n, cols_n):
    trailing = blocks.shape[3:]
    field = blocks.reshape((rows_n // 6, levels_n // 2, cols_n // 12, 2, 6, 12) + trailing)
    axes_order = (1, 3, 0, 4, 2, 5) + tuple(range(6, 6 + len(trailing)))
    return field.transpose(axes_order).reshape((levels_n, rows_n, cols_n) + trailing)

def product(form, left, right):
    return jnp.einsum(form, left.astype(jnp.float32), right.astype(jnp.float32))

def attend_forward(windows, label_win, pair_bias, w_qkv, w_proj, logit_scale):
    groups, across, places, width = windows.shape
    heads_n = logit_scale.shape[0]
    head_width = width // heads_n
    projected = product('gwpc,cd->gwpd', windows, w_qkv).astype(jnp.bfloat16)
    projected = projected.reshape(groups, across, places, 3, heads_n, head_width)
    query_full = projected[:, :, :, 0].astype(jnp.float32)
    key_full = projected[:, :, :, 1].astype(jnp.float32)
    values = projected[:, :, :, 2]
    query_inv = lax.rsqrt(lax.optimization_barrier(jnp.sum(query_full * query_full, -1, keepdims=True)) + 1.0)
    key_inv = lax.rsqrt(lax.optimization_barrier(jnp.sum(key_full * key_full, -1, keepdims=True)) + 1.0)
    query_unit = (query_full * query_inv).astype(jnp.bfloat16)
    key_unit = (key_full * key_inv).astype(jnp.bfloat16)
    temper = jnp.exp(logit_scale)
    cosine = product('gwphd,gwqhd->gwhpq', query_unit, key_unit)
    same_label = (label_win[:, :, :, None] == label_win[:, :, None, :])[:, :, None]
    scores = cosine * temper[:, None, None] + pair_bias[:, None]
    scores = jnp.where(same_label, scores, NEG_FILL)
    row_top = lax.optimization_barrier(jnp.max(scores, -1, keepdims=True))
    weights = jnp.exp(scores - row_top)
    soft_probs = weights / lax.optimization_barrier(jnp.sum(weights, -1, keepdims=True))
    probs_half = soft_probs.astype(jnp.bfloat16)
    mixed_heads = product('gwhpq,gwqhd->gwphd', probs_half, values).astype(jnp.bfloat16)
    mixed_heads = mixed_heads.reshape(groups, across, places, width)
    attended = product('gwpc,cd->gwpd', mixed_heads, w_proj).astype(jnp.bfloat16)
    stash_fwd = (query_full, key_full, values, query_inv, key_inv, query_unit, key_unit, cosine, soft_probs, probs_half, mixed_heads, temper)
    return (attended, stash_fwd)

def attend_backward(windows, grad_out, stash_fwd, w_qkv, w_proj):
    query_full, key_full, values, query_inv, key_inv, query_unit, key_unit, cosine, soft_probs, probs_half, mixed_heads, temper = stash_fwd
    groups, across, places, width = windows.shape
    heads_n = temper.shape[0]
    head_width = width // heads_n
    grad_proj = product('gwpc,gwpd->cd', mixed_heads, grad_out)
    grad_mixed = product('gwpd,cd->gwpc', grad_out, w_proj).astype(jnp.bfloat16)
    grad_mixed = grad_mixed.reshape(groups, across, places, heads_n, head_width)
    grad_probs = product('gwphd,gwqhd->gwhpq', grad_mixed, values)
    grad_values = product('gwhpq,gwphd->gwqhd', probs_half, grad_mixed)
    grad_scores = soft_probs * (grad_probs - lax.optimization_barrier(jnp.sum(grad_probs * soft_probs, -1, keepdims=True)))
    grad_temper = lax.optimization_barrier(jnp.sum(grad_scores * cosine, axis=(0, 1, 3, 4))) * temper
    grad_pairs = lax.optimization_barrier(jnp.sum(grad_scores, axis=1))
    scores_half = grad_scores.astype(jnp.bfloat16)
    grad_qunit = product('gwhpq,gwqhd->gwphd', scores_half, key_unit) * temper[:, None]
    grad_kunit = product('gwhpq,gwphd->gwqhd', scores_half, query_unit) * temper[:, None]
    grad_query = query_inv * grad_qunit - query_full * query_inv ** 3 * lax.optimization_barrier(jnp.sum(query_full * grad_qunit, -1, keepdims=True))
    grad_key = key_inv * grad_kunit - key_full * key_inv ** 3 * lax.optimization_barrier(jnp.sum(key_full * grad_kunit, -1, keepdims=True))
    grad_all = jnp.stack([grad_query, grad_key, grad_values], axis=3)
    grad_all = grad_all.reshape(groups, across, places, 3 * width).astype(jnp.bfloat16)
    grad_qkv_w = product('gwpc,gwpd->cd', windows, grad_all)
    grad_windows = product('gwpd,cd->gwpc', grad_all, w_qkv).astype(jnp.bfloat16)
    return (grad_windows, grad_qkv_w, grad_proj, grad_temper, grad_pairs)

def table_grad(grad_pairs, bias_index, entries):
    groups, heads_n = (grad_pairs.shape[0], grad_pairs.shape[1])
    flat_pairs = grad_pairs.reshape(groups * heads_n, -1).T
    summed = jax.ops.segment_sum(flat_pairs, bias_index.reshape(-1), num_segments=entries)
    return summed.T.reshape(groups, heads_n, entries)

def norm_backward(attended, grad_in, norm_gain):
    full_att = attended.astype(jnp.float32)
    center = full_att - lax.optimization_barrier(jnp.mean(full_att, -1, keepdims=True))
    inv_std = lax.rsqrt(lax.optimization_barrier(jnp.mean(center * center, -1, keepdims=True)) + 1e-05)
    normed = center * inv_std
    grad_full = grad_in.astype(jnp.float32)
    grad_gain = lax.optimization_barrier(jnp.sum((grad_full * normed).reshape(-1, full_att.shape[-1]), 0))
    grad_norm = grad_full * norm_gain
    grad_att = inv_std * (grad_norm - lax.optimization_barrier(jnp.mean(grad_norm, -1, keepdims=True)) - normed * lax.optimization_barrier(jnp.mean(grad_norm * normed, -1, keepdims=True)))
    return (grad_att.astype(jnp.bfloat16), grad_gain)

def reference(tokens, cotangent, labels, w_qkv, w_proj, logit_scale, bias_table, bias_index, norm_gain):
    levels_n, rows_n, cols_n, width = tokens.shape
    entries = bias_table.shape[-1]
    shifted = jnp.roll(tokens, (-1, -3, -6), axis=(0, 1, 2))
    shifted_grad = jnp.roll(cotangent, (-1, -3, -6), axis=(0, 1, 2))

    def one_band(band_index):
        row_start = (band_index * 6).astype(jnp.int32)
        band_tokens = lax.dynamic_slice_in_dim(shifted, row_start, 6, 1)
        band_grad = lax.dynamic_slice_in_dim(shifted_grad, row_start, 6, 1)
        band_labels = lax.dynamic_slice_in_dim(labels, row_start, 6, 1)
        table_rows = lax.dynamic_index_in_dim(bias_table, band_index, 0, keepdims=False)
        pair_bias = table_rows[:, :, bias_index]
        windows = to_windows(band_tokens)
        attended, stash_fwd = attend_forward(windows, to_windows(band_labels), pair_bias, w_qkv, w_proj, logit_scale)
        grad_out, grad_gain = norm_backward(attended, to_windows(band_grad), norm_gain)
        grad_windows, grad_qkv_w, grad_proj, grad_temper, grad_pairs = attend_backward(windows, grad_out, stash_fwd, w_qkv, w_proj)
        grad_table = table_grad(grad_pairs, bias_index, entries)
        band_back = from_windows(grad_windows, levels_n, 6, cols_n)
        return (band_back, grad_qkv_w, grad_proj, grad_temper, grad_table, grad_gain)
    results = lax.map(one_band, jnp.arange(rows_n // 6, dtype=jnp.int32))
    grad_shifted = results[0].transpose(1, 0, 2, 3, 4).reshape(levels_n, rows_n, cols_n, width)
    returned = jnp.roll(grad_shifted, (1, 3, 6), axis=(0, 1, 2))
    grad_tokens = (cotangent.astype(jnp.float32) + returned.astype(jnp.float32)).astype(jnp.bfloat16)
    grad_qkv = lax.optimization_barrier(jnp.sum(results[1], 0))
    grad_proj = lax.optimization_barrier(jnp.sum(results[2], 0))
    grad_scale = lax.optimization_barrier(jnp.sum(results[3], 0))
    grad_bias = results[4]
    grad_gain = lax.optimization_barrier(jnp.sum(results[5], 0))
    return (grad_tokens, grad_qkv, grad_proj, grad_scale, grad_bias, grad_gain)
```

```python
import jax
import jax.numpy as jnp
from jax import lax
from jax.experimental import pallas as pl
from jax.experimental.pallas import tpu as pltpu
from jax.sharding import Mesh
from jax.sharding import PartitionSpec as P


F32 = jnp.float32
BF16 = jnp.bfloat16
NEG_FILL = -1e30
HEADS = 6
WIN = 144
LANES = 896
CHUNKS = 26
HI = 13
ROWS = 40
TILES = 162
AXES = ("z", "y", "xl", "xh", "core")
LAYER = ("y", "xl", "xh", "core")


def nt(left, right):
    return lax.dot_general(left, right, (((1,), (1,)), ((), ())), preferred_element_type=F32)


def tn(left, right):
    return lax.dot_general(left, right, (((0,), (0,)), ((), ())), preferred_element_type=F32)


def nn(left, right):
    return jnp.dot(left, right, preferred_element_type=F32)


def swap_blocks(x):
    sub = lax.broadcasted_iota(jnp.int32, x.shape, 0)
    block = lax.broadcasted_iota(jnp.int32, x.shape, 1) // 16
    for bit in (1, 2, 4):
        s_set = (sub & bit) != 0
        l_set = (block & bit) != 0
        up = pltpu.roll(pltpu.roll(x, bit, 0), 128 - 16 * bit, 1)
        down = pltpu.roll(pltpu.roll(x, 8 - bit, 0), 16 * bit, 1)
        x = jnp.where(s_set == l_set, x, jnp.where(s_set, up, down))
    return x


def bias_kernel(table_ref, index_ref, out_ref, rows_ref, left_ref):
    entries = table_ref.shape[2]
    rows_ref[...] = jnp.zeros_like(rows_ref)
    for w in range(6):
        rows_ref[w * HEADS : w * HEADS + HEADS, :entries] = table_ref[w]
    for k in range(HI):
        part = rows_ref[:, 256 * k : 256 * k + 256]
        high = part.astype(BF16).astype(F32)
        left_ref[k * ROWS : k * ROWS + ROWS, :256] = high
        left_ref[k * ROWS : k * ROWS + ROWS, 256:] = part - high
    left = left_ref[...].astype(BF16)
    places = lax.broadcasted_iota(jnp.int32, (256, 128), 0)

    def two(n):
        index = [index_ref[pl.ds(n + t, 1), :] for t in range(2)]
        picks = jnp.concatenate(
            [jnp.where(places == (i & 255), 1.0, 0.0).astype(BF16) for i in index], axis=1
        )
        got = nn(left, jnp.concatenate([picks, picks], axis=0))
        for t in range(2):
            high = index[t] >> 8
            total = got[:ROWS, 128 * t : 128 * t + 128]
            for k in range(1, HI):
                total = jnp.where(high == k, got[k * ROWS : k * ROWS + ROWS, 128 * t : 128 * t + 128], total)
            out_ref[pl.ds(pl.multiple_of((n + t) * ROWS, 8), ROWS), :] = total

    def step(n, carry):
        for u in range(9):
            two((n * 9 + u) * 2)
        return carry

    lax.fori_loop(0, TILES // 18, step, 0)


def pair_bias(table, index):
    return pl.pallas_call(
        bias_kernel,
        out_shape=jax.ShapeDtypeStruct((TILES * ROWS, 128), F32),
        in_specs=[pl.BlockSpec(memory_space=pltpu.VMEM)] * 2,
        out_specs=pl.BlockSpec(memory_space=pltpu.VMEM),
        scratch_shapes=[pltpu.VMEM((ROWS, HI * 256), F32), pltpu.VMEM((HI * ROWS, 512), F32)],
        compiler_params=pltpu.CompilerParams(vmem_limit_bytes=24 << 20),
        cost_estimate=pl.CostEstimate(flops=10_000_000_000, bytes_accessed=4_000_000, transcendentals=0),
        name="pair_bias",
    )(table, index)


def stack_heads(x, head_mask):
    main = [x[:128] * head_mask[h] for h in range(HEADS)]
    tail = [x[128:] * head_mask[h] for h in range(HEADS)]
    return jnp.concatenate(main + tail + [jnp.zeros((32, x.shape[1]), x.dtype)], axis=0)


def own_blocks(xt):
    main = jnp.concatenate(
        [xt[32 * h : 32 * h + 32, 128 * h : 128 * h + 128] for h in range(HEADS)], axis=0
    )
    tail = jnp.concatenate(
        [
            xt[32 * h : 32 * h + 32, 768:]
            if h == 0
            else pltpu.roll(xt[32 * h : 32 * h + 32, 768:], 128 - 16 * h, 1)
            for h in range(HEADS)
        ],
        axis=0,
    )
    return jnp.concatenate([main.T, tail.T[:16]], axis=0)


def layer_kernel(
    tok_ref,
    cot_ref,
    lon_ref,
    lat_ref,
    diag_ref,
    label_ref,
    wqkv_ref,
    proj_ref,
    gain_ref,
    scale_ref,
    bias_ref,
    own_out,
    lon_out,
    lat_out,
    diag_out,
    sums_out,
    pairs_out,
    x_ref,
    g_ref,
    xb_ref,
    gq_ref,
    gk_ref,
    gv_ref,
    mix_ref,
    att_ref,
    gwin_ref,
    w_ref,
):
    def places():
        for w in range(6):
            aw, zw = w // 2, w % 2
            for i in range(2):
                level = (2 * zw + i + 1) % 4
                for j in range(6):
                    yield w * WIN + (i * 6 + j) * 12, level, aw * 6 + j

    for base, level, row in places():
        for n, (own, to) in enumerate(((tok_ref, x_ref), (cot_ref, g_ref))):
            if row < 15:
                left = own[level, row + 3].astype(F32)[6:]
                right = lon_ref[n, level, row].astype(F32)
            else:
                left = lat_ref[n, level, row - 15].astype(F32)
                right = diag_ref[n, level, row - 15].astype(F32)
            to[base : base + 6, :] = left
            to[base + 6 : base + 12, :] = right

    width = 192
    for n in range(3):
        w_ref[n] = wqkv_ref[:, width * n : width * n + width]
    gain = gain_ref[...]
    row_head = lax.broadcasted_iota(jnp.int32, (width, width), 0) // 32
    column_head = lax.broadcasted_iota(jnp.int32, (width, width), 1) // 32
    ones = jnp.where(row_head == column_head, 1.0, 0.0).astype(BF16)
    head_mask = [jnp.where(column_head[:1] == h, 1.0, 0.0).astype(BF16) for h in range(HEADS)]
    temper = jnp.exp(scale_ref[...])
    lanes = lax.broadcasted_iota(jnp.int32, (1, LANES), 1)
    lane_head = jnp.where(lanes < 768, lanes // 128, (lanes - 768) // 16)
    temper_row = jnp.zeros((1, LANES), F32)
    temper_col = jnp.zeros((1, width), F32)
    for h in range(HEADS):
        temper_row = jnp.where(lane_head == h, temper[:, h : h + 1], temper_row)
        temper_col = jnp.where(column_head[:1] == h, temper[:, h : h + 1], temper_col)

    def head_sum(x):
        high = x.astype(BF16)
        low = (x - high.astype(F32)).astype(BF16)
        return nn(high, ones) + nn(low, ones)

    def window(w, carry):
        scale_sum, gain_sum = carry
        at = pl.ds(pl.multiple_of(w * WIN, 16), WIN)
        x = x_ref[at, :].astype(BF16)
        xb_ref[at, :] = x
        query = nn(x, w_ref[0]).astype(BF16).astype(F32)
        key = nn(x, w_ref[1]).astype(BF16).astype(F32)
        value = nn(x, w_ref[2]).astype(BF16)
        query_inv = lax.rsqrt(head_sum(query * query) + 1.0)
        key_inv = lax.rsqrt(head_sum(key * key) + 1.0)
        key_unit = (key * key_inv).astype(BF16)
        queries = stack_heads((query * query_inv).astype(BF16), head_mask)
        cosine = nt(key_unit, queries)
        bias = [bias_ref[pl.ds(w * HEADS + h, WIN, stride=ROWS), :] for h in range(HEADS)]
        tails = []
        for n in range(18):
            tail = bias_ref[pl.ds((WIN + n) * ROWS + w * HEADS, HEADS), :]
            tails.append(swap_blocks(jnp.concatenate([tail, jnp.zeros((2, 128), F32)], axis=0)))
        bias = jnp.concatenate(bias + [jnp.concatenate(tails, axis=0)], axis=1)
        scores = cosine * temper_row + bias
        label = label_ref[w]
        tail = jnp.concatenate([label[:, 128:]] * 8, axis=1)
        label_row = jnp.concatenate([label[:, :128]] * HEADS + [tail], axis=1)
        label_col = jnp.concatenate(
            [
                jnp.broadcast_to(label[:, :128], (8, 128)).T[:, :1],
                jnp.broadcast_to(tail, (8, 128)).T[:16, :1],
            ],
            axis=0,
        )
        scores = jnp.where(label_col == label_row, scores, NEG_FILL)
        weights = jnp.exp(scores - jnp.max(scores, axis=0, keepdims=True))
        probs = weights * (1.0 / jnp.sum(weights, axis=0, keepdims=True))
        probs_half = probs.astype(BF16)
        mixed = own_blocks(tn(value, probs_half)).astype(BF16)
        mix_ref[at, :] = mixed
        att = nn(mixed, proj_ref[...]).astype(BF16).astype(F32)
        center = att - jnp.sum(att, axis=1, keepdims=True) * (1.0 / width)
        inv_std = lax.rsqrt(jnp.sum(center * center, axis=1, keepdims=True) * (1.0 / width) + 1e-5)
        normed = center * inv_std
        grad = g_ref[at, :]
        gain_sum = gain_sum + jnp.sum(grad * normed, axis=0, keepdims=True)
        grad = grad * gain
        grad_mean = jnp.sum(grad, axis=1, keepdims=True) * (1.0 / width)
        both_mean = jnp.sum(grad * normed, axis=1, keepdims=True) * (1.0 / width)
        grad_att = (inv_std * (grad - grad_mean - normed * both_mean)).astype(BF16)
        att_ref[at, :] = grad_att
        grad_mixed = stack_heads(nt(grad_att, proj_ref[...]).astype(BF16), head_mask)
        grad_probs = nt(value, grad_mixed)
        grad_value = nn(probs_half, grad_mixed)
        along = jnp.sum(grad_probs * probs, axis=0, keepdims=True)
        grad_scores = probs * (grad_probs - along)
        scale_sum = scale_sum + jnp.sum(grad_scores * cosine, axis=0, keepdims=True)
        for h in range(HEADS):
            pairs_out[pl.ds(w * HEADS + h, WIN, stride=ROWS), :] = grad_scores[:, 128 * h : 128 * h + 128]
        for n in range(18):
            turned = swap_blocks(grad_scores[8 * n : 8 * n + 8, 768:])
            pairs_out[pl.ds((WIN + n) * ROWS + w * HEADS, HEADS), :] = turned[:HEADS]
        half = grad_scores.astype(BF16)
        grad_qunit = own_blocks(tn(key_unit, half)) * temper_col
        grad_kunit = nn(half, queries) * temper_col
        grad_query = query_inv * grad_qunit - query * (query_inv * query_inv * query_inv) * head_sum(
            query * grad_qunit
        )
        grad_key = key_inv * grad_kunit - key * (key_inv * key_inv * key_inv) * head_sum(key * grad_kunit)
        grad_query = grad_query.astype(BF16)
        grad_key = grad_key.astype(BF16)
        grad_value = grad_value.astype(BF16)
        gq_ref[at, :] = grad_query
        gk_ref[at, :] = grad_key
        gv_ref[at, :] = grad_value
        gwin = nt(grad_query, w_ref[0]) + nt(grad_key, w_ref[1]) + nt(grad_value, w_ref[2])
        gwin_ref[at, :] = gwin
        return (scale_sum, gain_sum)

    scale_sum, gain_sum = lax.fori_loop(
        0, 6, window, (jnp.zeros((1, LANES), F32), jnp.zeros((1, width), F32))
    )

    for base, level, row in places():
        left = gwin_ref[base : base + 6, :].astype(BF16)
        right = gwin_ref[base + 6 : base + 12, :].astype(BF16)
        if row < 15:
            own_out[level, row] = left
            lon_out[level, row] = right
        else:
            lat_out[level, row - 15] = left
            diag_out[level, row - 15] = right

    xb = xb_ref[...]
    grad_q = tn(xb, gq_ref[...])
    grad_k = tn(xb, gk_ref[...])
    grad_v = tn(xb, gv_ref[...])
    grad_p = tn(mix_ref[...], att_ref[...])
    k_turned = pltpu.roll(jnp.concatenate([grad_k, jnp.zeros((width, 64), F32)], axis=1), 64, 1)
    p_end = pltpu.roll(jnp.concatenate([grad_p[:, 128:], jnp.zeros((width, 64), F32)], axis=1), 64, 1)
    zero = jnp.zeros((width, 64), F32)
    columns = [
        grad_q[:, :128],
        jnp.concatenate([grad_q[:, 128:], zero], axis=1) + jnp.concatenate([zero, k_turned[:, 64:128]], axis=1),
        k_turned[:, 128:256],
        grad_v[:, :128],
        jnp.concatenate([grad_v[:, 128:], zero], axis=1) + p_end,
        grad_p[:, :128],
    ]
    sums_out[...] = jnp.zeros_like(sums_out)
    for c, column in enumerate(columns):
        for n in range(24):
            sums_out[n * 6 + c] = column[8 * n : 8 * n + 8]
    lane = lax.broadcasted_iota(jnp.int32, (1, 128), 1)
    scale_sum = scale_sum * temper_row
    scale_row = jnp.zeros((1, 128), F32)
    for h in range(HEADS):
        main = jnp.sum(scale_sum[:, 128 * h : 128 * h + 128], axis=1, keepdims=True)
        tail = jnp.where((lane >= 16 * h) & (lane < 16 * h + 16), scale_sum[:, 768:], 0.0)
        total = main + jnp.sum(tail, axis=1, keepdims=True)
        scale_row = scale_row + jnp.where(lane == h, total, 0.0)
    rest = jnp.concatenate(
        [
            gain_sum[:, :128],
            jnp.concatenate([gain_sum[:, 128:], jnp.zeros((1, 64), F32)], axis=1),
            scale_row,
            jnp.zeros((5, 128), F32),
        ],
        axis=0,
    )
    high = rest.astype(BF16).astype(F32)
    sums_out[150] = high
    sums_out[151] = rest - high


def sublayer(*args):
    vmem = pl.BlockSpec(memory_space=pltpu.VMEM)
    tokens_n = 6 * WIN
    return pl.pallas_call(
        layer_kernel,
        out_shape=(
            jax.ShapeDtypeStruct((4, 15, 6, 192), BF16),
            jax.ShapeDtypeStruct((4, 15, 6, 192), BF16),
            jax.ShapeDtypeStruct((4, 3, 6, 192), BF16),
            jax.ShapeDtypeStruct((4, 3, 6, 192), BF16),
            jax.ShapeDtypeStruct((160, 8, 128), F32),
            jax.ShapeDtypeStruct((TILES * ROWS, 128), F32),
        ),
        in_specs=[vmem] * len(args),
        out_specs=(vmem,) * 6,
        scratch_shapes=[pltpu.VMEM((tokens_n, 192), F32)] * 2
        + [pltpu.VMEM((tokens_n, 192), BF16)] * 6
        + [pltpu.VMEM((tokens_n, 192), F32), pltpu.VMEM((3, 192, 192), BF16)],
        compiler_params=pltpu.CompilerParams(vmem_limit_bytes=48 << 20),
        cost_estimate=pl.CostEstimate(flops=1_500_000_000, bytes_accessed=10_000_000, transcendentals=800_000),
        name="sublayer",
    )(*args)


def entry_kernel(pairs_ref, index_ref, out_ref, acc_ref):
    acc_ref[...] = jnp.zeros_like(acc_ref)
    places = lax.broadcasted_iota(jnp.int32, (256, 128), 0)

    def step(n, carry):
        lefts, rights = [], []
        for t in range(18):
            tile = n * 18 + t
            index = index_ref[pl.ds(tile, 1), :]
            low, high = index & 255, index >> 8
            rights.append(jnp.where(places == low, 1.0, 0.0).astype(BF16))
            pairs = pairs_ref[pl.ds(pl.multiple_of(tile * ROWS, 8), ROWS), :]
            lefts.append(
                jnp.concatenate([jnp.where(high == k, pairs, 0.0) for k in range(HI)], axis=0).astype(BF16)
            )
        acc_ref[...] += nt(jnp.concatenate(lefts, axis=1), jnp.concatenate(rights, axis=1))
        return carry

    lax.fori_loop(0, TILES // 18, step, 0)
    rows = [acc_ref[k * ROWS : k * ROWS + 36, :] for k in range(HI)]
    rows = jnp.concatenate(rows + [jnp.zeros((44, 256), F32)], axis=0)
    for n in range(64):
        out_ref[2 * n] = rows[8 * n : 8 * n + 8, :128]
        out_ref[2 * n + 1] = rows[8 * n : 8 * n + 8, 128:]


def by_entry(pairs, index):
    vmem = pl.BlockSpec(memory_space=pltpu.VMEM)
    return pl.pallas_call(
        entry_kernel,
        out_shape=jax.ShapeDtypeStruct((128, 8, 128), F32),
        in_specs=[vmem] * 2,
        out_specs=vmem,
        scratch_shapes=[pltpu.VMEM((HI * ROWS, 256), F32)],
        compiler_params=pltpu.CompilerParams(vmem_limit_bytes=32 << 20),
        cost_estimate=pl.CostEstimate(flops=5_000_000_000, bytes_accessed=4_000_000, transcendentals=0),
        name="by_entry",
    )(pairs, index)


def unpack_kernel(got_ref, qkv_out, proj_out, bias_out, gain_out, scale_out, flat_ref):
    def tile(n, slots, at):
        return got_ref[n // slots, at + n % slots].astype(F32)

    for n in range(24):
        rows = pl.ds(8 * n, 8)
        for c in range(4):
            qkv_out[rows, 128 * c : 128 * c + 128] = tile(n * 6 + c, 5, 0)
        mid = tile(n * 6 + 4, 5, 0)
        qkv_out[rows, 512:576] = mid[:, :64]
        proj_out[rows, :128] = tile(n * 6 + 5, 5, 0)
        proj_out[rows, 128:192] = pltpu.roll(mid, 64, 1)[:, :64]
    for n in range(59):
        flat_ref[8 * n : 8 * n + 8, :128] = tile(2 * n, 4, 5)
        flat_ref[8 * n : 8 * n + 8, 128:] = tile(2 * n + 1, 4, 5)
    for k in range(HI):
        size = min(256, 3312 - 256 * k)
        for w in range(6):
            part = flat_ref[36 * k + 6 * w : 36 * k + 6 * w + 6, :]
            bias_out[w, :, 256 * k : 256 * k + size] = part[:, :size]
    rest = tile(150, 5, 0) + tile(151, 5, 0)
    gain_out[:, :128] = rest[0:1]
    gain_out[:, 128:192] = rest[1:2, :64]
    scale_out[...] = rest[2:3]


def unpack(got):
    vmem = pl.BlockSpec(memory_space=pltpu.VMEM)
    return pl.pallas_call(
        unpack_kernel,
        out_shape=(
            jax.ShapeDtypeStruct((192, 576), F32),
            jax.ShapeDtypeStruct((192, 192), F32),
            jax.ShapeDtypeStruct((6, HEADS, 3312), F32),
            jax.ShapeDtypeStruct((1, 192), F32),
            jax.ShapeDtypeStruct((1, 128), F32),
        ),
        in_specs=[vmem],
        out_specs=(vmem,) * 5,
        scratch_shapes=[pltpu.VMEM((472, 256), F32)],
        compiler_params=pltpu.CompilerParams(vmem_limit_bytes=24 << 20),
        name="unpack",
    )(got)


def moved(value, lon_by, lat_by):
    lon_n, lat_n = 64, 4
    pairs = []
    for lon in range(lon_n):
        for lat in range(lat_n):
            to = (lon + lon_by) % lon_n * lat_n + (lat + lat_by) % lat_n
            pairs.append((lon * lat_n + lat, to))
    return lax.ppermute(value, AXES, pairs)


def half(x):
    return lax.reduce_precision(x, 8, 7)


def sum_everywhere(sums, entries, leaving):
    parts = jnp.concatenate([sums.reshape(32, 40, 128), entries.reshape(32, 32, 128)], axis=1).astype(BF16)
    parts = lax.all_to_all(parts, LAYER, 0, 0, tiled=True).astype(F32)
    mine = lax.axis_index(LAYER) == 30

    def rounded(x):
        both = x[:8] + x[8:16]
        high = half(both)
        split = jnp.concatenate([high, both - high, x[16:]], axis=0)
        return jnp.where(mine, split, x).astype(BF16)

    weights = jnp.sum(parts[:, :40], 0)
    bands = jnp.sum(parts[:, 40:].reshape(8, 4, 32, 128), 0).reshape(128, 128)
    layer = jnp.concatenate([rounded(weights), bands.astype(BF16)], axis=0)
    layer, leaving = lax.optimization_barrier((layer, leaving))
    layers = lax.all_to_all(jnp.broadcast_to(layer, (8, 168, 128)), "z", 0, 0, tiled=True)
    lon_out, lat_out, diag_out = leaving
    arrived = (moved(lon_out, 1, 0), moved(lat_out, 0, 1), moved(diag_out, 1, 1))
    layers, arrived = lax.optimization_barrier((layers, arrived))
    total = jnp.sum(layers.astype(F32), 0)
    weights = jnp.broadcast_to(rounded(total[:40]), (8, 4, 40, 128))
    bands = jnp.broadcast_to(total[40:].astype(BF16).reshape(4, 32, 128), (8, 4, 32, 128))
    parts = jnp.concatenate([weights, bands], axis=2).reshape(32, 72, 128)
    return lax.all_to_all(parts, LAYER, 0, 0, tiled=True), arrived


def on_device(tokens, cotangent, labels, w_qkv, w_proj, logit_scale, bias_table, bias_index, norm_gain):
    both = jnp.stack([tokens[:, :, :6], cotangent[:, :, :6]])
    lon_in = moved(both[:, :, 3:], -1, 0)
    diag_in = moved(both[:, :, :3], -1, -1)
    lat_in = moved(jnp.stack([tokens[:, :3, 6:], cotangent[:, :3, 6:]]), 0, -1)

    turned = bias_index.T
    index = jnp.concatenate([turned[:, :128], turned[:, 128:].reshape(18, 128)], axis=0)
    bias = pair_bias(bias_table.reshape(6, HEADS, -1), index)

    label_win = labels.reshape(2, 2, 3, 6, 12).transpose(2, 0, 1, 3, 4).reshape(6, 1, WIN).astype(F32)

    own, lon_out, lat_out, diag_out, sums, pairs = sublayer(
        tokens,
        cotangent,
        lon_in,
        lat_in,
        diag_in,
        label_win,
        w_qkv,
        w_proj,
        norm_gain[None],
        logit_scale[None],
        bias,
    )
    entries = by_entry(pairs, index)
    got, (lon_back, lat_back, diag_back) = sum_everywhere(sums, entries, (lon_out, lat_out, diag_out))
    grad_qkv, grad_proj, grad_bias, grad_gain, grad_scale = unpack(got.reshape(32, 9, 8, 128))
    returned = jnp.concatenate(
        [jnp.concatenate([diag_back, lat_back], axis=2), jnp.concatenate([lon_back, own], axis=2)], axis=1
    )
    grad_tokens = (cotangent.astype(F32) + returned.astype(F32)).astype(BF16)
    return (
        grad_tokens,
        grad_qkv,
        grad_proj,
        grad_scale[0, :HEADS],
        grad_bias.reshape(bias_table.shape),
        grad_gain[0],
    )


def solution(mesh):
    fine = Mesh(mesh.devices.reshape(8, 4, 2, 2, 2), AXES)
    lon, lat = ("z", "y", "xl"), ("xh", "core")
    placed = (
        P(None, lat, lon, None),
        P(None, lat, lon, None),
        P(None, lat, lon),
        P(),
        P(),
        P(),
        P(lat, None, None, None),
        P(),
        P(),
    )
    return jax.shard_map(
        on_device,
        mesh=fine,
        in_specs=placed,
        out_specs=(P(None, lat, lon, None), P(), P(), P(), P(lat, None, None, None), P()),
        check_vma=False,
    )
```

```python
import jax
import jax.numpy as jnp
from jax import lax
from jax.experimental import pallas as pl
from jax.experimental.pallas import tpu as pltpu
from jax.sharding import Mesh
from jax.sharding import PartitionSpec as P


F32 = jnp.float32
BF16 = jnp.bfloat16
NEG_FILL = -1e30
HEADS = 6
WIN = 144
LANES = 896
CHUNKS = 26
HI = 13
ROWS = 40
TOGETHER = 2
MANY = 4
TILES = 162
AXES = ("z", "y", "xl", "xh", "core")
LAYER = ("y", "xl", "xh", "core")


def nt(left, right):
    return lax.dot_general(left, right, (((1,), (1,)), ((), ())), preferred_element_type=F32)


def tn(left, right):
    return lax.dot_general(left, right, (((0,), (0,)), ((), ())), preferred_element_type=F32)


def nn(left, right):
    return jnp.dot(left, right, preferred_element_type=F32)


def swap_blocks(x):
    sub = lax.broadcasted_iota(jnp.int32, x.shape, 0)
    block = lax.broadcasted_iota(jnp.int32, x.shape, 1) // 16
    for bit in (1, 2, 4):
        s_set = (sub & bit) != 0
        l_set = (block & bit) != 0
        up = pltpu.roll(pltpu.roll(x, bit, 0), 128 - 16 * bit, 1)
        down = pltpu.roll(pltpu.roll(x, 8 - bit, 0), 16 * bit, 1)
        x = jnp.where(s_set == l_set, x, jnp.where(s_set, up, down))
    return x


def bias_kernel(table_ref, index_ref, many_out, few_out, tail_out, rows_ref, left_ref, *rest):
    blocks, sems = rest[:3], rest[3]
    entries = table_ref.shape[3]
    rows_ref[...] = jnp.zeros_like(rows_ref)
    for aw in range(3):
        for h in range(HEADS):
            for zw in range(2):
                row = (aw * 2 + zw) * HEADS + h
                rows_ref[row : row + 1, :entries] = table_ref[aw, h, zw : zw + 1, :]
    for k in range(HI):
        part = rows_ref[:, 256 * k : 256 * k + 256]
        high = part.astype(BF16).astype(F32)
        left_ref[0, k * ROWS : k * ROWS + ROWS, :] = high
        left_ref[1, k * ROWS : k * ROWS + ROWS, :] = part - high
    left = jnp.concatenate([left_ref[0], left_ref[1]], axis=0).astype(BF16)
    fewer = [
        left_ref[term, k * ROWS + HEADS * w : k * ROWS + HEADS * w + MANY, :]
        for term in range(2)
        for k in range(HI)
        for w in range(6)
    ]
    fewer = jnp.concatenate(fewer, axis=0).astype(BF16)
    places = lax.broadcasted_iota(jnp.int32, (256, 128), 0)

    def two(at, rows, left, block_ref, slot, to):
        index = [index_ref[pl.ds(at + t, 1), :] for t in range(2)]
        picks = jnp.concatenate(
            [jnp.where(places == (i & 255), 1.0, 0.0).astype(BF16) for i in index], axis=1
        )
        got = nn(left, picks)
        for t in range(2):
            high = index[t] >> 8
            lane = slice(128 * t, 128 * t + 128)
            total = None
            for k in range(HI):
                value = got[k * rows : k * rows + rows, lane] + got[(HI + k) * rows : (HI + k + 1) * rows, lane]
                total = value if total is None else jnp.where(high == k, value, total)
            block_ref[slot, (to + t) * rows : (to + t) * rows + rows, :] = total

    def pick(row, index):
        low = index & 127
        got = []
        for c in range(CHUNKS):
            source = jnp.broadcast_to(rows_ref[row : row + 1, c * 128 : c * 128 + 128], (8, 128))
            got.append(jnp.take_along_axis(source, low, axis=1, mode="promise_in_bounds"))
        bit = 128
        while len(got) > 1:
            odd = (index & bit) != 0
            got = [
                jnp.where(odd, got[i + 1], got[i]) if i + 1 < len(got) else got[i]
                for i in range(0, len(got), 2)
            ]
            bit *= 2
        return got[0]

    def leave(n):
        slot = n % 2
        outs = (
            many_out.at[pl.ds(pl.multiple_of(n * 16 * 6 * MANY, 8), 16 * 6 * MANY), :],
            few_out.at[:, pl.ds(pl.multiple_of(n * 16, 8), 16), :],
            tail_out.at[pl.ds(pl.multiple_of(n * 2 * ROWS, 8), 2 * ROWS), :],
        )
        return [
            pltpu.make_async_copy(block.at[slot], out, sems.at[slot, i])
            for i, (block, out) in enumerate(zip(blocks, outs))
        ]

    def step(n, carry):
        @pl.when(n >= 2)
        def _():
            for copy in leave(n - 2):
                copy.wait()

        slot = n % 2
        for u in range(8):
            two(n * 16 + 2 * u, 6 * MANY, fewer, blocks[0], slot, 2 * u)
            for v in range(3 * u, 3 * u + 3):
                w, h, b = v // 4, MANY + v // 2 % 2, v % 2
                index = index_ref[pl.ds(pl.multiple_of(n * 16 + 8 * b, 8), 8), :]
                blocks[1][slot, w * 2 + h - MANY, 8 * b : 8 * b + 8, :] = pick(w * HEADS + h, index)
        two(WIN + n * 2, ROWS, left, blocks[2], slot, 0)
        for copy in leave(n):
            copy.start()
        return carry

    lax.fori_loop(0, 9, step, 0)
    for n in (7, 8):
        for copy in leave(n):
            copy.wait()


def pair_bias(table, index):
    return pl.pallas_call(
        bias_kernel,
        out_shape=(
            jax.ShapeDtypeStruct((WIN * 6 * MANY, 128), F32),
            jax.ShapeDtypeStruct((12, WIN, 128), F32),
            jax.ShapeDtypeStruct((18 * ROWS, 128), F32),
        ),
        in_specs=[pl.BlockSpec(memory_space=pltpu.VMEM)] * 2,
        out_specs=(pl.BlockSpec(memory_space=pltpu.HBM),) * 3,
        scratch_shapes=[
            pltpu.VMEM((ROWS, HI * 256), F32),
            pltpu.VMEM((2, HI * ROWS, 256), F32),
            pltpu.VMEM((2, 16 * 6 * MANY, 128), F32),
            pltpu.VMEM((2, 12, 16, 128), F32),
            pltpu.VMEM((2, 2 * ROWS, 128), F32),
            pltpu.SemaphoreType.DMA((2, 3)),
        ],
        compiler_params=pltpu.CompilerParams(vmem_limit_bytes=20 << 20),
        cost_estimate=pl.CostEstimate(flops=10_000_000_000, bytes_accessed=4_000_000, transcendentals=0),
        name="pair_bias",
    )(table, index)


def wide(x):
    return x[:, :128], jnp.concatenate([x[:, 128:WIN], jnp.zeros((x.shape[0], 112), x.dtype)], axis=1)


def turned(x):
    main, tail = wide(x)
    return jnp.concatenate([main.T, tail.T[:16]], axis=0)


def spread(xt, tail_mask):
    main, tail = wide(xt)
    for by in (16, 32, 64):
        tail = tail + pltpu.roll(tail, by, 1)
    tail = jnp.where(tail_mask, tail, 0.0).astype(BF16)
    main = main.astype(BF16)
    zero = jnp.zeros((32, 128), BF16)
    pairs = []
    for j in range(3):
        top = jnp.concatenate([main[64 * j : 64 * j + 32], zero], axis=1)
        low = jnp.concatenate([zero, main[64 * j + 32 : 64 * j + 64]], axis=1)
        pairs.append(jnp.concatenate([top, low], axis=0))
    return pairs, tail


def across(left, right, take):
    pairs, tail = right
    for j in range(3):
        part = nn(left[:, 64 * j : 64 * j + 64], pairs[j])
        yield
        take(2 * j, part[:, :128])
        yield
        take(2 * j + 1, part[:, 128:])
    part = nn(left, tail)
    yield
    take(HEADS, part)


def gather_heads(left, right):
    main = []
    for j in range(3):
        part = nn(left[64 * j : 64 * j + 64], right[:, 256 * j : 256 * j + 256])
        main += [part[:32, :128], part[32:, 128:]]
    tail = nn(left, right[:, 768:])
    tails = [tail[:32]] + [pltpu.roll(tail[32 * h : 32 * h + 32], 128 - 16 * h, 1) for h in range(1, HEADS)]
    return jnp.concatenate([jnp.concatenate(main, axis=0), jnp.concatenate(tails, axis=0)[:, :16]], axis=1)


def gather_keys(left, right):
    pairs, tail = left
    main = [nt(pairs[j], right[:, 256 * j : 256 * j + 256]) for j in range(3)]
    return jnp.concatenate(main, axis=0) + nt(tail, right[:, 768:])


def head_sum(x):
    sums = [jnp.sum(x[32 * h : 32 * h + 32], axis=0, keepdims=True) for h in range(HEADS)]
    return jnp.concatenate([jnp.broadcast_to(t, (32, WIN)) for t in sums], axis=0)


def column(row):
    return jnp.broadcast_to(row, (8, row.shape[1])).T[:, :1]


def pack(x, n, halfway, ref):
    ref[6 * n : 6 * n + 6, :] = x[:, :128]
    rest = x[:, 128:]
    at = 12 * halfway + 6 * (n % halfway)
    if n < halfway:
        ref[at : at + 6, :64] = rest
    else:
        ref[at : at + 6, 64:] = rest


def unpacked(dense, levels, rows):
    n = levels * rows * 6
    rest = jnp.concatenate([dense[n:, :64], dense[n:, 64:]], axis=0)
    return jnp.concatenate([dense[:n], rest], axis=1).reshape(levels, rows, 6, 192)


def layer_kernel(
    tok_ref,
    cot_ref,
    lon_ref,
    lat_ref,
    diag_ref,
    label_ref,
    wqkv_ref,
    proj_ref,
    gain_ref,
    scale_ref,
    many_hbm,
    few_hbm,
    tail_hbm,
    own_out,
    lon_out,
    lat_out,
    diag_out,
    sums_out,
    pairs_out,
    x_ref,
    g_ref,
    gwin_ref,
    wt_ref,
    projt_ref,
    sum_w_ref,
    sum_p_ref,
    sum_g_ref,
    sum_s_ref,
    lon_ref32,
    lat_ref32,
    diag_ref32,
    many_ref,
    few_ref,
    tail_ref,
    bias_sems,
    *slots,
):
    arriving = [
        pltpu.make_async_copy(source, to, bias_sems.at[i])
        for i, (source, to) in enumerate(
            ((many_hbm, many_ref), (few_hbm, few_ref), (tail_hbm, tail_ref))
        )
    ]
    for copy in arriving:
        copy.start()

    def places():
        for w in range(6):
            aw, zw = w // 2, w % 2
            for i in range(2):
                level = (2 * zw + i + 1) % 4
                for j in range(6):
                    yield w * WIN + (i * 6 + j) * 12, level, aw * 6 + j

    for base, level, row in places():
        for n, (own, to) in enumerate(((tok_ref, x_ref), (cot_ref, g_ref))):
            if row < 15:
                left = own[level, row + 3].astype(F32)[6:]
                right = lon_ref[n, level, row].astype(F32)
            else:
                left = lat_ref[n, level, row - 15].astype(F32)
                right = diag_ref[n, level, row - 15].astype(F32)
            to[base : base + 6, :] = left
            to[base + 6 : base + 12, :] = right

    width = 192
    for n in range(3):
        wt_ref[width * n : width * n + width, :] = (
            wqkv_ref[:, width * n : width * n + width].astype(F32).T.astype(BF16)
        )
    projt_ref[...] = proj_ref[...].astype(F32).T.astype(BF16)
    for ref in (sum_w_ref, sum_p_ref, sum_g_ref, sum_s_ref):
        ref[...] = jnp.zeros_like(ref)
    gain = column(gain_ref[...])
    temper = jnp.exp(scale_ref[...])
    lanes = lax.broadcasted_iota(jnp.int32, (1, LANES), 1)
    lane_head = jnp.where(lanes < 768, lanes // 128, (lanes - 768) // 16)
    row_head = lax.broadcasted_iota(jnp.int32, (width, 128), 0) // 32
    tail_mask = row_head == lax.broadcasted_iota(jnp.int32, (width, 128), 1) // 16
    temper_row = jnp.zeros((1, LANES), F32)
    temper_col = jnp.zeros((width, 1), F32)
    for h in range(HEADS):
        temper_row = jnp.where(lane_head == h, temper[:, h : h + 1], temper_row)
        temper_col = jnp.where(row_head[:, :1] == h, temper[:, h : h + 1], temper_col)

    def window(w, slot):
        cosine_ref, probs_ref, half_ref, column_ref = (ref.at[slot] for ref in slots)
        at = pl.ds(pl.multiple_of(w * WIN, 16), WIN)
        x = x_ref[at, :].astype(BF16)
        projected = nt(wt_ref[...], x).astype(BF16).astype(F32)
        yield
        query, key, value = (projected[width * n : width * n + width] for n in range(3))
        query_inv = lax.rsqrt(head_sum(query * query) + 1.0)
        key_inv = lax.rsqrt(head_sum(key * key) + 1.0)
        yield
        key_unit = (key * key_inv).astype(BF16).astype(F32)
        yield
        queries = spread((query * query_inv).astype(BF16).astype(F32), tail_mask)
        label = label_ref[w]
        tail = jnp.concatenate([label[:, 128:]] * 8, axis=1)
        label_col = jnp.concatenate([column(label[:, :128]), column(tail)[:16]], axis=0)
        column_ref[...] = jnp.broadcast_to(label_col, (WIN, 128))

        def soften(t, cosine):
            lane = slice(128 * t, 128 * t + 128)
            cosine_ref[:, lane] = cosine
            if t < MANY:
                bias = many_ref[pl.ds(w * MANY + t, WIN, stride=6 * MANY), :]
            elif t < HEADS:
                bias = few_ref[w * 2 + t - MANY]
            else:
                bias = []
                for n in range(18):
                    part = tail_ref[pl.ds(n * ROWS + w * HEADS, HEADS), :]
                    bias.append(swap_blocks(jnp.concatenate([part, jnp.zeros((2, 128), F32)], axis=0)))
                bias = jnp.concatenate(bias, axis=0)
            scores = cosine * temper_row[:, lane] + bias
            same = column_ref[...] == (label[:, :128] if t < HEADS else tail)
            scores = jnp.where(same, scores, NEG_FILL)
            weights = jnp.exp(scores - jnp.max(scores, axis=0, keepdims=True))
            probs = weights * (1.0 / jnp.sum(weights, axis=0, keepdims=True))
            probs_ref[:, lane] = probs
            half_ref[:, lane] = probs.astype(BF16)

        yield from across(turned(key_unit).astype(BF16), queries, soften)
        yield
        probs_half = half_ref[...]
        yield
        mixed = gather_heads(value.astype(BF16), probs_half).astype(BF16)
        yield
        att = nn(projt_ref[...], mixed).astype(BF16).astype(F32)
        yield
        center = att - jnp.sum(att, axis=0, keepdims=True) * (1.0 / width)
        inv_std = lax.rsqrt(jnp.sum(center * center, axis=0, keepdims=True) * (1.0 / width) + 1e-5)
        yield
        normed = center * inv_std
        yield
        grad = g_ref[at, :]
        grad = jnp.concatenate([grad[:128].T, jnp.concatenate([grad[128:], grad[:112]], axis=0).T[:, :16]], axis=1)
        yield
        sum_g_ref[...] += grad * normed
        grad = grad * gain
        yield
        grad_mean = jnp.sum(grad, axis=0, keepdims=True) * (1.0 / width)
        both_mean = jnp.sum(grad * normed, axis=0, keepdims=True) * (1.0 / width)
        grad_att = (inv_std * (grad - grad_mean - normed * both_mean)).astype(BF16)
        yield
        sum_p_ref[...] += nt(mixed, grad_att)
        yield
        grad_mixed = spread(nn(proj_ref[...], grad_att).astype(BF16).astype(F32), tail_mask)
        yield
        grad_value = gather_keys(grad_mixed, probs_half)

        def harden(t, grad_probs):
            lane = slice(128 * t, 128 * t + 128)
            probs = probs_ref[:, lane]
            along = jnp.sum(grad_probs * probs, axis=0, keepdims=True)
            grad_scores = probs * (grad_probs - along)
            sum_s_ref[:, lane] += jnp.sum(grad_scores * cosine_ref[:, lane], axis=0, keepdims=True)
            half_ref[:, lane] = grad_scores.astype(BF16)
            if t < HEADS:
                pairs_out[pl.ds(w * HEADS + t, WIN, stride=ROWS), :] = grad_scores
            else:
                for n in range(18):
                    block = swap_blocks(grad_scores[8 * n : 8 * n + 8])
                    pairs_out[pl.ds((WIN + n) * ROWS + w * HEADS, HEADS), :] = block[:HEADS]

        yield from across(turned(value).astype(BF16), grad_mixed, harden)
        yield
        scores_half = half_ref[...]
        grad_qunit = gather_heads(key_unit.astype(BF16), scores_half) * temper_col
        yield
        grad_kunit = gather_keys(queries, scores_half) * temper_col
        yield
        grad_query = query_inv * grad_qunit - query * (query_inv * query_inv * query_inv) * head_sum(
            query * grad_qunit
        )
        yield
        grad_key = key_inv * grad_kunit - key * (key_inv * key_inv * key_inv) * head_sum(key * grad_kunit)
        yield
        grad_all = jnp.concatenate([grad_query, grad_key, grad_value], axis=0).astype(BF16)
        yield
        sum_w_ref[...] += nn(grad_all, x)
        yield
        gwin_ref[at, :] = turned(nn(wqkv_ref[...], grad_all))

    def group(n, carry):
        going = [window(n * TOGETHER + slot, slot) for slot in range(TOGETHER)]
        while going:
            going = [one for one in going if next(one, going) is None]
        return carry

    for copy in arriving:
        copy.wait()
    lax.fori_loop(0, 6 // TOGETHER, group, 0)

    for base, level, row in places():
        left = gwin_ref[base : base + 6, :]
        right = gwin_ref[base + 6 : base + 12, :]
        if row < 15:
            own_out[level, row] = left.astype(BF16)
            pack(right, level * 15 + row, 30, lon_ref32)
        else:
            pack(left, level * 3 + row - 15, 6, lat_ref32)
            pack(right, level * 3 + row - 15, 6, diag_ref32)
    lon_out[...] = lon_ref32[...].astype(BF16)
    lat_out[...] = lat_ref32[...].astype(BF16)
    diag_out[...] = diag_ref32[...].astype(BF16)

    grad_q, grad_k, grad_v = (sum_w_ref[width * n : width * n + width, :].T for n in range(3))
    grad_p = sum_p_ref[...]
    gain_sum = jnp.sum(sum_g_ref[...], axis=1, keepdims=True)
    gain_sum = jnp.broadcast_to(gain_sum, (width, 128)).T[:1]
    k_turned = pltpu.roll(jnp.concatenate([grad_k, jnp.zeros((width, 64), F32)], axis=1), 64, 1)
    p_end = pltpu.roll(jnp.concatenate([grad_p[:, 128:], jnp.zeros((width, 64), F32)], axis=1), 64, 1)
    zero = jnp.zeros((width, 64), F32)
    columns = [
        grad_q[:, :128],
        jnp.concatenate([grad_q[:, 128:], zero], axis=1) + jnp.concatenate([zero, k_turned[:, 64:128]], axis=1),
        k_turned[:, 128:256],
        grad_v[:, :128],
        jnp.concatenate([grad_v[:, 128:], zero], axis=1) + p_end,
        grad_p[:, :128],
    ]
    sums_out[...] = jnp.zeros_like(sums_out)
    for c, tiles in enumerate(columns):
        for n in range(24):
            sums_out[n * 6 + c] = tiles[8 * n : 8 * n + 8]
    lane = lax.broadcasted_iota(jnp.int32, (1, 128), 1)
    scale_sum = sum_s_ref[...] * temper_row
    scale_row = jnp.zeros((1, 128), F32)
    for h in range(HEADS):
        main = jnp.sum(scale_sum[:, 128 * h : 128 * h + 128], axis=1, keepdims=True)
        tail = jnp.where((lane >= 16 * h) & (lane < 16 * h + 16), scale_sum[:, 768:], 0.0)
        total = main + jnp.sum(tail, axis=1, keepdims=True)
        scale_row = scale_row + jnp.where(lane == h, total, 0.0)
    rest = jnp.concatenate(
        [
            gain_sum[:, :128],
            jnp.concatenate([gain_sum[:, 128:], jnp.zeros((1, 64), F32)], axis=1),
            scale_row,
            jnp.zeros((5, 128), F32),
        ],
        axis=0,
    )
    high = rest.astype(BF16).astype(F32)
    sums_out[150] = high
    sums_out[151] = rest - high


def sublayer(*args):
    vmem = pl.BlockSpec(memory_space=pltpu.VMEM)
    tokens_n = 6 * WIN
    return pl.pallas_call(
        layer_kernel,
        out_shape=(
            jax.ShapeDtypeStruct((4, 15, 6, 192), BF16),
            jax.ShapeDtypeStruct((540, 128), BF16),
            jax.ShapeDtypeStruct((108, 128), BF16),
            jax.ShapeDtypeStruct((108, 128), BF16),
            jax.ShapeDtypeStruct((160, 8, 128), F32),
            jax.ShapeDtypeStruct((TILES * ROWS, 128), F32),
        ),
        in_specs=[vmem] * (len(args) - 3) + [pl.BlockSpec(memory_space=pltpu.HBM)] * 3,
        out_specs=(vmem,) * 6,
        scratch_shapes=[pltpu.VMEM((tokens_n, 192), F32)] * 3
        + [pltpu.VMEM((576, 192), BF16), pltpu.VMEM((192, 192), BF16)]
        + [pltpu.VMEM((576, 192), F32), pltpu.VMEM((192, 192), F32), pltpu.VMEM((192, WIN), F32), pltpu.VMEM((1, LANES), F32)]
        + [pltpu.VMEM((540, 128), F32), pltpu.VMEM((108, 128), F32), pltpu.VMEM((108, 128), F32)]
        + [pltpu.VMEM((WIN * 6 * MANY, 128), F32), pltpu.VMEM((12, WIN, 128), F32)]
        + [pltpu.VMEM((18 * ROWS, 128), F32), pltpu.SemaphoreType.DMA((3,))]
        + [pltpu.VMEM((TOGETHER, WIN, LANES), F32)] * 2
        + [pltpu.VMEM((TOGETHER, WIN, LANES), BF16), pltpu.VMEM((TOGETHER, WIN, 128), F32)],
        compiler_params=pltpu.CompilerParams(vmem_limit_bytes=20 << 20),
        cost_estimate=pl.CostEstimate(flops=1_500_000_000, bytes_accessed=10_000_000, transcendentals=800_000),
        name="sublayer",
    )(*args)


def entry_kernel(pairs_ref, index_ref, out_ref, acc_ref):
    acc_ref[...] = jnp.zeros_like(acc_ref)
    places = lax.broadcasted_iota(jnp.int32, (256, 128), 0)

    def step(n, carry):
        lefts, rights = [], []
        for t in range(18):
            tile = n * 18 + t
            index = index_ref[pl.ds(tile, 1), :]
            low, high = index & 255, index >> 8
            rights.append(jnp.where(places == low, 1.0, 0.0).astype(BF16))
            pairs = pairs_ref[pl.ds(pl.multiple_of(tile * ROWS, 8), ROWS), :]
            lefts.append(
                jnp.concatenate([jnp.where(high == k, pairs, 0.0) for k in range(HI)], axis=0).astype(BF16)
            )
        acc_ref[...] += nt(jnp.concatenate(lefts, axis=1), jnp.concatenate(rights, axis=1))
        return carry

    lax.fori_loop(0, TILES // 18, step, 0)
    rows = [acc_ref[k * ROWS : k * ROWS + 36, :] for k in range(HI)]
    rows = jnp.concatenate(rows + [jnp.zeros((44, 256), F32)], axis=0)
    for n in range(64):
        out_ref[2 * n] = rows[8 * n : 8 * n + 8, :128]
        out_ref[2 * n + 1] = rows[8 * n : 8 * n + 8, 128:]


def by_entry(pairs, index):
    vmem = pl.BlockSpec(memory_space=pltpu.VMEM)
    return pl.pallas_call(
        entry_kernel,
        out_shape=jax.ShapeDtypeStruct((128, 8, 128), F32),
        in_specs=[vmem] * 2,
        out_specs=vmem,
        scratch_shapes=[pltpu.VMEM((HI * ROWS, 256), F32)],
        compiler_params=pltpu.CompilerParams(vmem_limit_bytes=20 << 20),
        cost_estimate=pl.CostEstimate(flops=5_000_000_000, bytes_accessed=4_000_000, transcendentals=0),
        name="by_entry",
    )(pairs, index)


def unpack_kernel(got_ref, qkv_out, proj_out, bias_out, gain_out, scale_out, flat_ref):
    def tile(n, slots, at):
        return got_ref[n // slots, at + n % slots].astype(F32)

    for n in range(24):
        rows = pl.ds(8 * n, 8)
        for c in range(4):
            qkv_out[rows, 128 * c : 128 * c + 128] = tile(n * 6 + c, 5, 0)
        mid = tile(n * 6 + 4, 5, 0)
        qkv_out[rows, 512:576] = mid[:, :64]
        proj_out[rows, :128] = tile(n * 6 + 5, 5, 0)
        proj_out[rows, 128:192] = pltpu.roll(mid, 64, 1)[:, :64]
    for n in range(59):
        flat_ref[8 * n : 8 * n + 8, :] = tile(2 * n, 4, 5)
        flat_ref[472 + 8 * n : 480 + 8 * n, :] = tile(2 * n + 1, 4, 5)
    for k in range(2 * HI):
        size = min(128, 3312 - 128 * k)
        for aw in range(3):
            for h in range(HEADS):
                part = flat_ref[pl.ds(472 * (k % 2) + 36 * (k // 2) + 12 * aw + h, 2, stride=HEADS), :]
                bias_out[aw, h, :, 128 * k : 128 * k + size] = part[:, :size]
    rest = tile(150, 5, 0) + tile(151, 5, 0)
    gain_out[:, :128] = rest[0:1]
    gain_out[:, 128:192] = rest[1:2, :64]
    scale_out[...] = rest[2:3]


def unpack(got):
    vmem = pl.BlockSpec(memory_space=pltpu.VMEM)
    return pl.pallas_call(
        unpack_kernel,
        out_shape=(
            jax.ShapeDtypeStruct((192, 576), F32),
            jax.ShapeDtypeStruct((192, 192), F32),
            jax.ShapeDtypeStruct((3, HEADS, 2, 3312), F32),
            jax.ShapeDtypeStruct((1, 192), F32),
            jax.ShapeDtypeStruct((1, 128), F32),
        ),
        in_specs=[vmem],
        out_specs=(vmem,) * 5,
        scratch_shapes=[pltpu.VMEM((944, 128), F32)],
        compiler_params=pltpu.CompilerParams(vmem_limit_bytes=20 << 20),
        name="unpack",
    )(got)


def moved(value, lon_by, lat_by):
    lon_n, lat_n = 64, 4
    pairs = []
    for lon in range(lon_n):
        for lat in range(lat_n):
            to = (lon + lon_by) % lon_n * lat_n + (lat + lat_by) % lat_n
            pairs.append((lon * lat_n + lat, to))
    return lax.ppermute(value, AXES, pairs)


def half(x):
    return lax.reduce_precision(x, 8, 7)


def sum_everywhere(sums, entries, leaving):
    parts = jnp.concatenate([sums.reshape(32, 40, 128), entries.reshape(32, 32, 128)], axis=1).astype(BF16)
    parts = lax.all_to_all(parts, LAYER, 0, 0, tiled=True).astype(F32)
    mine = lax.axis_index(LAYER) == 30

    def rounded(x):
        both = x[:8] + x[8:16]
        high = half(both)
        split = jnp.concatenate([high, both - high, x[16:]], axis=0)
        return jnp.where(mine, split, x).astype(BF16)

    weights = jnp.sum(parts[:, :40], 0)
    bands = jnp.sum(parts[:, 40:].reshape(8, 4, 32, 128), 0).reshape(128, 128)
    layer = jnp.concatenate([rounded(weights), bands.astype(BF16)], axis=0)
    layer, leaving = lax.optimization_barrier((layer, leaving))
    layers = lax.all_to_all(jnp.broadcast_to(layer, (8, 168, 128)), "z", 0, 0, tiled=True)
    lon_out, lat_out, diag_out = leaving
    arrived = (moved(lon_out, 1, 0), moved(lat_out, 0, 1), moved(diag_out, 1, 1))
    layers, arrived = lax.optimization_barrier((layers, arrived))
    total = jnp.sum(layers.astype(F32), 0)
    weights = jnp.broadcast_to(rounded(total[:40]), (8, 4, 40, 128))
    bands = jnp.broadcast_to(total[40:].astype(BF16).reshape(4, 32, 128), (8, 4, 32, 128))
    parts = jnp.concatenate([weights, bands], axis=2).reshape(32, 72, 128)
    return lax.all_to_all(parts, LAYER, 0, 0, tiled=True), arrived


def on_device(tokens, cotangent, labels, w_qkv, w_proj, logit_scale, bias_table, bias_index, norm_gain):
    both = jnp.stack([tokens[:, :, :6], cotangent[:, :, :6]])
    lon_in = moved(both[:, :, 3:], -1, 0)
    diag_in = moved(both[:, :, :3], -1, -1)
    lat_in = moved(jnp.stack([tokens[:, :3, 6:], cotangent[:, :3, 6:]]), 0, -1)

    turned = bias_index.T
    index = jnp.concatenate([turned[:, :128], turned[:, 128:].reshape(18, 128)], axis=0)
    bias = pair_bias(bias_table.transpose(0, 2, 1, 3), index)

    label_win = labels.reshape(2, 2, 3, 6, 12).transpose(2, 0, 1, 3, 4).reshape(6, 1, WIN).astype(F32)

    own, lon_out, lat_out, diag_out, sums, pairs = sublayer(
        tokens,
        cotangent,
        lon_in,
        lat_in,
        diag_in,
        label_win,
        w_qkv,
        w_proj,
        norm_gain[None],
        logit_scale[None],
        *bias,
    )
    entries = by_entry(pairs, index)
    got, (lon_back, lat_back, diag_back) = sum_everywhere(sums, entries, (lon_out, lat_out, diag_out))
    grad_qkv, grad_proj, grad_bias, grad_gain, grad_scale = unpack(got.reshape(32, 9, 8, 128))
    lon_back, lat_back, diag_back = unpacked(lon_back, 4, 15), unpacked(lat_back, 4, 3), unpacked(diag_back, 4, 3)
    returned = jnp.concatenate(
        [jnp.concatenate([diag_back, lat_back], axis=2), jnp.concatenate([lon_back, own], axis=2)], axis=1
    )
    grad_tokens = (cotangent.astype(F32) + returned.astype(F32)).astype(BF16)
    return (
        grad_tokens,
        grad_qkv,
        grad_proj,
        grad_scale[0, :HEADS],
        grad_bias.transpose(0, 2, 1, 3),
        grad_gain[0],
    )


def solution(mesh):
    fine = Mesh(mesh.devices.reshape(8, 4, 2, 2, 2), AXES)
    lon, lat = ("z", "y", "xl"), ("xh", "core")
    placed = (
        P(None, lat, lon, None),
        P(None, lat, lon, None),
        P(None, lat, lon),
        P(),
        P(),
        P(),
        P(lat, None, None, None),
        P(),
        P(),
    )
    return jax.shard_map(
        on_device,
        mesh=fine,
        in_specs=placed,
        out_specs=(P(None, lat, lon, None), P(), P(), P(), P(lat, None, None, None), P()),
        check_vma=False,
    )
```

```python
import jax
import jax.numpy as jnp
from jax import lax
from jax.experimental import pallas as pl
from jax.experimental.pallas import tpu as pltpu
from jax.sharding import Mesh
from jax.sharding import PartitionSpec as P


F32 = jnp.float32
BF16 = jnp.bfloat16
NEG_FILL = -1e30
HEADS = 6
WIN = 144
LANES = 896
CHUNKS = 26
HI = 13
ROWS = 40
LEAD = 2
TOGETHER = 3
MANY = 4
TILES = 162
AXES = ("z", "y", "xl", "xh", "core")
LAYER = ("y", "xl", "xh", "core")


def nt(left, right):
    return lax.dot_general(left, right, (((1,), (1,)), ((), ())), preferred_element_type=F32)


def tn(left, right):
    return lax.dot_general(left, right, (((0,), (0,)), ((), ())), preferred_element_type=F32)


def nn(left, right):
    return jnp.dot(left, right, preferred_element_type=F32)


def swap_blocks(x):
    sub = lax.broadcasted_iota(jnp.int32, x.shape, 0)
    block = lax.broadcasted_iota(jnp.int32, x.shape, 1) // 16
    for bit in (1, 2, 4):
        s_set = (sub & bit) != 0
        l_set = (block & bit) != 0
        up = pltpu.roll(pltpu.roll(x, bit, 0), 128 - 16 * bit, 1)
        down = pltpu.roll(pltpu.roll(x, 8 - bit, 0), 16 * bit, 1)
        x = jnp.where(s_set == l_set, x, jnp.where(s_set, up, down))
    return x


def bias_kernel(table_ref, given_ref, many_out, few_out, tail_out, index_ref, rows_ref, left_ref, *rest):
    given = given_ref[...].astype(F32)
    rest_q = jnp.concatenate([given[:, 128:], jnp.zeros((WIN, 112), F32)], axis=1)
    index_ref[:128, :] = given[:128, :128].T.astype(jnp.int32)
    index_ref[128:WIN, :] = rest_q[:128].T[:16].astype(jnp.int32)
    ends = jnp.concatenate([given[128:], jnp.zeros((112, WIN), F32)], axis=0)
    ends = jnp.concatenate(
        [ends[:, :128].T, jnp.concatenate([ends[:, 128:], jnp.zeros((128, 112), F32)], axis=1).T[:16]], axis=0
    )
    for by in (16, 32, 64):
        ends = ends + pltpu.roll(ends, by, 1)
    sub = lax.broadcasted_iota(jnp.int32, (WIN, 128), 0) % 8
    block = lax.broadcasted_iota(jnp.int32, (WIN, 128), 1) // 16
    ends = jnp.where(sub == block, ends, 0.0)
    for n in range(18):
        row = jnp.sum(ends[8 * n : 8 * n + 8], axis=0, keepdims=True)
        index_ref[WIN + n : WIN + n + 1, :] = row.astype(jnp.int32)
    blocks, sems = rest[:3], rest[3]
    entries = table_ref.shape[3]
    rows_ref[...] = jnp.zeros_like(rows_ref)
    for aw in range(3):
        for h in range(HEADS):
            for zw in range(2):
                row = (aw * 2 + zw) * HEADS + h
                rows_ref[row : row + 1, :entries] = table_ref[aw, h, zw : zw + 1, :]
    for k in range(HI):
        part = rows_ref[:, 256 * k : 256 * k + 256]
        high = part.astype(BF16).astype(F32)
        left_ref[0, k * ROWS : k * ROWS + ROWS, :] = high
        left_ref[1, k * ROWS : k * ROWS + ROWS, :] = part - high
    left = jnp.concatenate([left_ref[0], left_ref[1]], axis=0).astype(BF16)
    fewer = [
        left_ref[term, k * ROWS + HEADS * w : k * ROWS + HEADS * w + MANY, :]
        for term in range(2)
        for k in range(HI)
        for w in range(6)
    ]
    fewer = jnp.concatenate(fewer, axis=0).astype(BF16)
    places = lax.broadcasted_iota(jnp.int32, (256, 128), 0)

    def two(at, rows, left, block_ref, slot, to):
        index = [index_ref[pl.ds(at + t, 1), :] for t in range(2)]
        picks = jnp.concatenate(
            [jnp.where(places == (i & 255), 1.0, 0.0).astype(BF16) for i in index], axis=1
        )
        got = nn(left, picks)
        for t in range(2):
            high = index[t] >> 8
            lane = slice(128 * t, 128 * t + 128)
            total = None
            for k in range(HI):
                value = got[k * rows : k * rows + rows, lane] + got[(HI + k) * rows : (HI + k + 1) * rows, lane]
                total = value if total is None else jnp.where(high == k, value, total)
            block_ref[slot, (to + t) * rows : (to + t) * rows + rows, :] = total

    def pick(row, index):
        low = index & 127
        got = []
        for c in range(CHUNKS):
            source = jnp.broadcast_to(rows_ref[row : row + 1, c * 128 : c * 128 + 128], (8, 128))
            got.append(jnp.take_along_axis(source, low, axis=1, mode="promise_in_bounds"))
        bit = 128
        while len(got) > 1:
            odd = (index & bit) != 0
            got = [
                jnp.where(odd, got[i + 1], got[i]) if i + 1 < len(got) else got[i]
                for i in range(0, len(got), 2)
            ]
            bit *= 2
        return got[0]

    def leave(n):
        slot = n % 2
        outs = (
            many_out.at[pl.ds(pl.multiple_of(n * 16 * 6 * MANY, 8), 16 * 6 * MANY), :],
            few_out.at[:, pl.ds(pl.multiple_of(n * 16, 8), 16), :],
            tail_out.at[pl.ds(pl.multiple_of(n * 2 * ROWS, 8), 2 * ROWS), :],
        )
        return [
            pltpu.make_async_copy(block.at[slot], out, sems.at[slot, i])
            for i, (block, out) in enumerate(zip(blocks, outs))
        ]

    def step(n, carry):
        @pl.when(n >= 2)
        def _():
            for copy in leave(n - 2):
                copy.wait()

        slot = n % 2
        for u in range(8):
            two(n * 16 + 2 * u, 6 * MANY, fewer, blocks[0], slot, 2 * u)
            for v in range(3 * u, 3 * u + 3):
                w, h, b = v // 4, MANY + v // 2 % 2, v % 2
                index = index_ref[pl.ds(pl.multiple_of(n * 16 + 8 * b, 8), 8), :]
                blocks[1][slot, w * 2 + h - MANY, 8 * b : 8 * b + 8, :] = pick(w * HEADS + h, index)
        two(WIN + n * 2, ROWS, left, blocks[2], slot, 0)
        for copy in leave(n):
            copy.start()
        return carry

    lax.fori_loop(0, 9, step, 0)
    for n in (7, 8):
        for copy in leave(n):
            copy.wait()


def pair_bias(table, index):
    return pl.pallas_call(
        bias_kernel,
        out_shape=(
            pltpu.HBM((WIN * 6 * MANY, 128), F32),
            pltpu.HBM((12, WIN, 128), F32),
            pltpu.HBM((18 * ROWS, 128), F32),
            jax.ShapeDtypeStruct((TILES, 128), jnp.int32),
        ),
        in_specs=[pl.BlockSpec(memory_space=pltpu.VMEM)] * 2,
        out_specs=(pl.BlockSpec(memory_space=pltpu.HBM),) * 3 + (pl.BlockSpec(memory_space=pltpu.VMEM),),
        scratch_shapes=[
            pltpu.VMEM((ROWS, HI * 256), F32),
            pltpu.VMEM((2, HI * ROWS, 256), F32),
            pltpu.VMEM((2, 16 * 6 * MANY, 128), F32),
            pltpu.VMEM((2, 12, 16, 128), F32),
            pltpu.VMEM((2, 2 * ROWS, 128), F32),
            pltpu.SemaphoreType.DMA((2, 3)),
        ],
        compiler_params=pltpu.CompilerParams(vmem_limit_bytes=20 << 20),
        cost_estimate=pl.CostEstimate(flops=10_000_000_000, bytes_accessed=4_000_000, transcendentals=0),
        name="pair_bias",
    )(table, index)


def wide(x):
    return x[:, :128], jnp.concatenate([x[:, 128:WIN], jnp.zeros((x.shape[0], 112), x.dtype)], axis=1)


def turned(x):
    main, tail = wide(x)
    return jnp.concatenate([main.T, tail.T[:16]], axis=0)


def spread(xt, tail_mask):
    main, tail = wide(xt)
    for by in (16, 32, 64):
        tail = tail + pltpu.roll(tail, by, 1)
    tail = jnp.where(tail_mask, tail, 0.0).astype(BF16)
    main = main.astype(BF16)
    zero = jnp.zeros((32, 128), BF16)
    pairs = []
    for j in range(3):
        top = jnp.concatenate([main[64 * j : 64 * j + 32], zero], axis=1)
        low = jnp.concatenate([zero, main[64 * j + 32 : 64 * j + 64]], axis=1)
        pairs.append(jnp.concatenate([top, low], axis=0))
    return pairs, tail


def across(left, right, take):
    pairs, tail = right
    for j in range(3):
        part = nn(left[:, 64 * j : 64 * j + 64], pairs[j])
        yield
        take(2 * j, part[:, :128])
        yield
        take(2 * j + 1, part[:, 128:])
    part = nn(left, tail)
    yield
    take(HEADS, part)


def gather_heads(left, right):
    main = []
    for j in range(3):
        part = nn(left[64 * j : 64 * j + 64], right[:, 256 * j : 256 * j + 256])
        main += [part[:32, :128], part[32:, 128:]]
    tail = nn(left, right[:, 768:])
    tails = [tail[:32]] + [pltpu.roll(tail[32 * h : 32 * h + 32], 128 - 16 * h, 1) for h in range(1, HEADS)]
    return jnp.concatenate([jnp.concatenate(main, axis=0), jnp.concatenate(tails, axis=0)[:, :16]], axis=1)


def gather_keys(left, right):
    pairs, tail = left
    main = [nt(pairs[j], right[:, 256 * j : 256 * j + 256]) for j in range(3)]
    return jnp.concatenate(main, axis=0) + nt(tail, right[:, 768:])


def head_sum(x):
    sums = [jnp.sum(x[32 * h : 32 * h + 32], axis=0, keepdims=True) for h in range(HEADS)]
    return jnp.concatenate([jnp.broadcast_to(t, (32, WIN)) for t in sums], axis=0)


def column(row):
    return jnp.broadcast_to(row, (8, row.shape[1])).T[:, :1]


def pack(x, n, halfway, ref):
    ref[6 * n : 6 * n + 6, :] = x[:, :128]
    rest = x[:, 128:]
    at = 12 * halfway + 6 * (n % halfway)
    if n < halfway:
        ref[at : at + 6, :64] = rest
    else:
        ref[at : at + 6, 64:] = rest


def unpacked(dense, levels, rows):
    n = levels * rows * 6
    rest = jnp.concatenate([dense[n:, :64], dense[n:, 64:]], axis=0)
    return jnp.concatenate([dense[:n], rest], axis=1).reshape(levels, rows, 6, 192)


def places():
    for w in range(6):
        aw, zw = w // 2, w % 2
        for i in range(2):
            level = (2 * zw + i + 1) % 4
            for j in range(6):
                yield w * WIN + (i * 6 + j) * 12, level, aw * 6 + j


def layer_kernel(
    tok_ref,
    cot_ref,
    lon_ref,
    lat_ref,
    diag_ref,
    label_ref,
    wqkv_ref,
    proj_ref,
    gain_ref,
    scale_ref,
    many_hbm,
    few_hbm,
    tail_hbm,
    grads_out,
    sums_out,
    pairs_out,
    x_ref,
    g_ref,
    grads_ref,
    grads_sems,
    wt_ref,
    projt_ref,
    sum_w_ref,
    sum_p_ref,
    sum_g_ref,
    sum_s_ref,
    many_ref,
    few_ref,
    tail_ref,
    bias_sems,
    *slots,
):
    arriving = [
        pltpu.make_async_copy(source, to, bias_sems.at[i])
        for i, (source, to) in enumerate(
            ((many_hbm, many_ref), (few_hbm, few_ref), (tail_hbm, tail_ref))
        )
    ]
    for copy in arriving:
        copy.start()

    for base, level, row in places():
        for n, (own, to) in enumerate(((tok_ref, x_ref), (cot_ref, g_ref))):
            if row < 15:
                left = own[level, row + 3].astype(F32)[6:]
                right = lon_ref[n, level, row].astype(F32)
            else:
                left = lat_ref[n, level, row - 15].astype(F32)
                right = diag_ref[n, level, row - 15].astype(F32)
            to[base : base + 6, :] = left
            to[base + 6 : base + 12, :] = right

    width = 192
    for n in range(3):
        wt_ref[width * n : width * n + width, :] = (
            wqkv_ref[:, width * n : width * n + width].astype(F32).T.astype(BF16)
        )
    projt_ref[...] = proj_ref[...].astype(F32).T.astype(BF16)
    for ref in (sum_w_ref, sum_p_ref, sum_g_ref, sum_s_ref):
        ref[...] = jnp.zeros_like(ref)
    gain = column(gain_ref[...])
    temper = jnp.exp(scale_ref[...])
    lanes = lax.broadcasted_iota(jnp.int32, (1, LANES), 1)
    lane_head = jnp.where(lanes < 768, lanes // 128, (lanes - 768) // 16)
    row_head = lax.broadcasted_iota(jnp.int32, (width, 128), 0) // 32
    tail_mask = row_head == lax.broadcasted_iota(jnp.int32, (width, 128), 1) // 16
    temper_row = jnp.zeros((1, LANES), F32)
    temper_col = jnp.zeros((width, 1), F32)
    for h in range(HEADS):
        temper_row = jnp.where(lane_head == h, temper[:, h : h + 1], temper_row)
        temper_col = jnp.where(row_head[:, :1] == h, temper[:, h : h + 1], temper_col)

    def leave(w):
        return pltpu.make_async_copy(grads_ref.at[w], grads_out.at[w], grads_sems.at[w])

    def window(n, slot):
        w = n * TOGETHER + slot
        cosine_ref, probs_ref, half_ref, column_ref = (ref.at[slot] for ref in slots)
        at = pl.ds(pl.multiple_of(w * WIN, 16), WIN)
        x = x_ref[at, :].astype(BF16)
        projected = nt(wt_ref[...], x).astype(BF16).astype(F32)
        yield
        query, key, value = (projected[width * n : width * n + width] for n in range(3))
        query_inv = lax.rsqrt(head_sum(query * query) + 1.0)
        key_inv = lax.rsqrt(head_sum(key * key) + 1.0)
        yield
        key_unit = (key * key_inv).astype(BF16).astype(F32)
        yield
        queries = spread((query * query_inv).astype(BF16).astype(F32), tail_mask)
        label = label_ref[w]
        tail = jnp.concatenate([label[:, 128:]] * 8, axis=1)
        label_col = jnp.concatenate([column(label[:, :128]), column(tail)[:16]], axis=0)
        column_ref[...] = jnp.broadcast_to(label_col, (WIN, 128))

        def soften(t, cosine):
            lane = slice(128 * t, 128 * t + 128)
            cosine_ref[:, lane] = cosine
            if t < MANY:
                bias = many_ref[pl.ds(w * MANY + t, WIN, stride=6 * MANY), :]
            elif t < HEADS:
                bias = few_ref[w * 2 + t - MANY]
            else:
                bias = []
                for n in range(18):
                    part = tail_ref[pl.ds(n * ROWS + w * HEADS, HEADS), :]
                    bias.append(swap_blocks(jnp.concatenate([part, jnp.zeros((2, 128), F32)], axis=0)))
                bias = jnp.concatenate(bias, axis=0)
            scores = cosine * temper_row[:, lane] + bias
            same = column_ref[...] == (label[:, :128] if t < HEADS else tail)
            scores = jnp.where(same, scores, NEG_FILL)
            weights = jnp.exp(scores - jnp.max(scores, axis=0, keepdims=True))
            probs = weights * (1.0 / jnp.sum(weights, axis=0, keepdims=True))
            probs_ref[:, lane] = probs
            half_ref[:, lane] = probs.astype(BF16)

        key_turned = turned(key_unit).astype(BF16)
        yield
        if slot == 0:

            @pl.when(n == 0)
            def _():
                for copy in arriving:
                    copy.wait()

        yield from across(key_turned, queries, soften)
        yield
        probs_half = half_ref[...]
        yield
        mixed = gather_heads(value.astype(BF16), probs_half).astype(BF16)
        yield
        att = nn(projt_ref[...], mixed).astype(BF16).astype(F32)
        yield
        center = att - jnp.sum(att, axis=0, keepdims=True) * (1.0 / width)
        inv_std = lax.rsqrt(jnp.sum(center * center, axis=0, keepdims=True) * (1.0 / width) + 1e-5)
        yield
        normed = center * inv_std
        yield
        grad = g_ref[at, :]
        grad = jnp.concatenate([grad[:128].T, jnp.concatenate([grad[128:], grad[:112]], axis=0).T[:, :16]], axis=1)
        yield
        sum_g_ref[...] += grad * normed
        grad = grad * gain
        yield
        grad_mean = jnp.sum(grad, axis=0, keepdims=True) * (1.0 / width)
        both_mean = jnp.sum(grad * normed, axis=0, keepdims=True) * (1.0 / width)
        grad_att = (inv_std * (grad - grad_mean - normed * both_mean)).astype(BF16)
        yield
        sum_p_ref[...] += nt(mixed, grad_att)
        yield
        grad_mixed = spread(nn(proj_ref[...], grad_att).astype(BF16).astype(F32), tail_mask)
        yield
        grad_value = gather_keys(grad_mixed, probs_half)

        def harden(t, grad_probs):
            lane = slice(128 * t, 128 * t + 128)
            probs = probs_ref[:, lane]
            along = jnp.sum(grad_probs * probs, axis=0, keepdims=True)
            grad_scores = probs * (grad_probs - along)
            sum_s_ref[:, lane] += jnp.sum(grad_scores * cosine_ref[:, lane], axis=0, keepdims=True)
            half_ref[:, lane] = grad_scores.astype(BF16)
            if t < HEADS:
                pairs_out[pl.ds(w * HEADS + t, WIN, stride=ROWS), :] = grad_scores
            else:
                for n in range(18):
                    block = swap_blocks(grad_scores[8 * n : 8 * n + 8])
                    pairs_out[pl.ds((WIN + n) * ROWS + w * HEADS, HEADS), :] = block[:HEADS]

        yield from across(turned(value).astype(BF16), grad_mixed, harden)
        yield
        scores_half = half_ref[...]
        grad_qunit = gather_heads(key_unit.astype(BF16), scores_half) * temper_col
        yield
        grad_kunit = gather_keys(queries, scores_half) * temper_col
        yield
        grad_query = query_inv * grad_qunit - query * (query_inv * query_inv * query_inv) * head_sum(
            query * grad_qunit
        )
        yield
        grad_key = key_inv * grad_kunit - key * (key_inv * key_inv * key_inv) * head_sum(key * grad_kunit)
        yield
        grad_all = jnp.concatenate([grad_query, grad_key, grad_value], axis=0).astype(BF16)
        yield
        sum_w_ref[...] += nn(grad_all, x)
        grads_ref[w] = grad_all
        leave(w).start()

    def group(n, carry):
        going = [window(n, slot) for slot in range(TOGETHER)]
        for slot, one in enumerate(going):
            for _ in range(LEAD * (TOGETHER - 1 - slot)):
                next(one)
        while going:
            going = [one for one in going if next(one, going) is None]
        return carry

    lax.fori_loop(0, 6 // TOGETHER, group, 0)

    grad_q, grad_k, grad_v = (sum_w_ref[width * n : width * n + width, :].T for n in range(3))
    grad_p = sum_p_ref[...]
    gain_sum = jnp.sum(sum_g_ref[...], axis=1, keepdims=True)
    gain_sum = jnp.broadcast_to(gain_sum, (width, 128)).T[:1]
    k_turned = pltpu.roll(jnp.concatenate([grad_k, jnp.zeros((width, 64), F32)], axis=1), 64, 1)
    p_end = pltpu.roll(jnp.concatenate([grad_p[:, 128:], jnp.zeros((width, 64), F32)], axis=1), 64, 1)
    zero = jnp.zeros((width, 64), F32)
    columns = [
        grad_q[:, :128],
        jnp.concatenate([grad_q[:, 128:], zero], axis=1) + jnp.concatenate([zero, k_turned[:, 64:128]], axis=1),
        k_turned[:, 128:256],
        grad_v[:, :128],
        jnp.concatenate([grad_v[:, 128:], zero], axis=1) + p_end,
        grad_p[:, :128],
    ]
    sums_out[...] = jnp.zeros_like(sums_out)
    for c, tiles in enumerate(columns):
        for n in range(24):
            sums_out[n * 6 + c] = tiles[8 * n : 8 * n + 8]
    lane = lax.broadcasted_iota(jnp.int32, (1, 128), 1)
    for w in range(6):
        leave(w).wait()
    scale_sum = sum_s_ref[...] * temper_row
    scale_row = jnp.zeros((1, 128), F32)
    for h in range(HEADS):
        main = jnp.sum(scale_sum[:, 128 * h : 128 * h + 128], axis=1, keepdims=True)
        tail = jnp.where((lane >= 16 * h) & (lane < 16 * h + 16), scale_sum[:, 768:], 0.0)
        total = main + jnp.sum(tail, axis=1, keepdims=True)
        scale_row = scale_row + jnp.where(lane == h, total, 0.0)
    rest = jnp.concatenate(
        [
            gain_sum[:, :128],
            jnp.concatenate([gain_sum[:, 128:], jnp.zeros((1, 64), F32)], axis=1),
            scale_row,
            jnp.zeros((5, 128), F32),
        ],
        axis=0,
    )
    high = rest.astype(BF16).astype(F32)
    sums_out[150] = high
    sums_out[151] = rest - high


def sublayer(*args):
    vmem = pl.BlockSpec(memory_space=pltpu.VMEM)
    tokens_n = 6 * WIN
    return pl.pallas_call(
        layer_kernel,
        out_shape=(
            pltpu.HBM((6, 576, WIN), BF16),
            jax.ShapeDtypeStruct((160, 8, 128), F32),
            jax.ShapeDtypeStruct((TILES * ROWS, 128), F32),
        ),
        in_specs=[vmem] * (len(args) - 3) + [pl.BlockSpec(memory_space=pltpu.HBM)] * 3,
        out_specs=(pl.BlockSpec(memory_space=pltpu.HBM), vmem, vmem),
        scratch_shapes=[pltpu.VMEM((tokens_n, 192), F32)] * 2
        + [pltpu.VMEM((6, 576, WIN), BF16), pltpu.SemaphoreType.DMA((6,))]
        + [pltpu.VMEM((576, 192), BF16), pltpu.VMEM((192, 192), BF16)]
        + [pltpu.VMEM((576, 192), F32), pltpu.VMEM((192, 192), F32), pltpu.VMEM((192, WIN), F32), pltpu.VMEM((1, LANES), F32)]
        + [pltpu.VMEM((WIN * 6 * MANY, 128), F32), pltpu.VMEM((12, WIN, 128), F32)]
        + [pltpu.VMEM((18 * ROWS, 128), F32), pltpu.SemaphoreType.DMA((3,))]
        + [pltpu.VMEM((TOGETHER, WIN, LANES), F32)] * 2
        + [pltpu.VMEM((TOGETHER, WIN, LANES), BF16), pltpu.VMEM((TOGETHER, WIN, 128), F32)],
        compiler_params=pltpu.CompilerParams(vmem_limit_bytes=20 << 20),
        cost_estimate=pl.CostEstimate(flops=1_500_000_000, bytes_accessed=10_000_000, transcendentals=800_000),
        name="sublayer",
    )(*args)


def return_kernel(
    grads_ref, wqkv_ref, own_out, lon_out, lat_out, diag_out, gwin_ref, lon_ref32, lat_ref32, diag_ref32
):
    for w in range(6):
        gwin_ref[w * WIN : w * WIN + WIN, :] = turned(nn(wqkv_ref[...], grads_ref[w]))
    for base, level, row in places():
        left = gwin_ref[base : base + 6, :]
        right = gwin_ref[base + 6 : base + 12, :]
        if row < 15:
            own_out[level, row] = left.astype(BF16)
            pack(right, level * 15 + row, 30, lon_ref32)
        else:
            pack(left, level * 3 + row - 15, 6, lat_ref32)
            pack(right, level * 3 + row - 15, 6, diag_ref32)
    lon_out[...] = lon_ref32[...].astype(BF16)
    lat_out[...] = lat_ref32[...].astype(BF16)
    diag_out[...] = diag_ref32[...].astype(BF16)


def returns(grads, w_qkv):
    vmem = pl.BlockSpec(memory_space=pltpu.VMEM)
    return pl.pallas_call(
        return_kernel,
        out_shape=(
            jax.ShapeDtypeStruct((4, 15, 6, 192), BF16),
            jax.ShapeDtypeStruct((540, 128), BF16),
            jax.ShapeDtypeStruct((108, 128), BF16),
            jax.ShapeDtypeStruct((108, 128), BF16),
        ),
        in_specs=[vmem] * 2,
        out_specs=(vmem,) * 4,
        scratch_shapes=[pltpu.VMEM((6 * WIN, 192), F32), pltpu.VMEM((540, 128), F32)]
        + [pltpu.VMEM((108, 128), F32)] * 2,
        compiler_params=pltpu.CompilerParams(vmem_limit_bytes=14 << 20),
        cost_estimate=pl.CostEstimate(flops=2_000_000_000, bytes_accessed=3_000_000, transcendentals=0),
        name="returns",
    )(grads, w_qkv)


def entry_kernel(pairs_ref, index_ref, sums_ref, out_ref, acc_ref):
    acc_ref[...] = jnp.zeros_like(acc_ref)
    places = lax.broadcasted_iota(jnp.int32, (256, 128), 0)

    def step(n, carry):
        lefts, rights = [], []
        for t in range(18):
            tile = n * 18 + t
            index = index_ref[pl.ds(tile, 1), :]
            low, high = index & 255, index >> 8
            rights.append(jnp.where(places == low, 1.0, 0.0).astype(BF16))
            pairs = pairs_ref[pl.ds(pl.multiple_of(tile * ROWS, 8), ROWS), :]
            lefts.append(
                jnp.concatenate([jnp.where(high == k, pairs, 0.0) for k in range(HI)], axis=0).astype(BF16)
            )
        acc_ref[...] += nt(jnp.concatenate(lefts, axis=1), jnp.concatenate(rights, axis=1))
        return carry

    lax.fori_loop(0, TILES // 18, step, 0)
    rows = [acc_ref[k * ROWS : k * ROWS + 36, :] for k in range(HI)]
    rows = jnp.concatenate(rows + [jnp.zeros((44, 256), F32)], axis=0)
    for c in range(32):
        tiles = [sums_ref[5 * c + n] for n in range(5)]
        for n in range(2 * c, 2 * c + 2):
            tiles += [rows[8 * n : 8 * n + 8, :128], rows[8 * n : 8 * n + 8, 128:]]
        out_ref[c] = jnp.concatenate(tiles, axis=0).astype(BF16)


def by_entry(pairs, index, sums):
    vmem = pl.BlockSpec(memory_space=pltpu.VMEM)
    return pl.pallas_call(
        entry_kernel,
        out_shape=jax.ShapeDtypeStruct((32, 72, 128), BF16),
        in_specs=[vmem] * 3,
        out_specs=vmem,
        scratch_shapes=[pltpu.VMEM((HI * ROWS, 256), F32)],
        compiler_params=pltpu.CompilerParams(vmem_limit_bytes=20 << 20),
        cost_estimate=pl.CostEstimate(flops=5_000_000_000, bytes_accessed=4_000_000, transcendentals=0),
        name="by_entry",
    )(pairs, index, sums)


def unpack_kernel(got_ref, qkv_out, proj_out, bias_out, gain_out, scale_out, flat_ref):
    def tile(n, slots, at):
        return got_ref[n // slots, at + n % slots].astype(F32)

    for n in range(24):
        rows = pl.ds(8 * n, 8)
        for c in range(4):
            qkv_out[rows, 128 * c : 128 * c + 128] = tile(n * 6 + c, 5, 0)
        mid = tile(n * 6 + 4, 5, 0)
        qkv_out[rows, 512:576] = mid[:, :64]
        proj_out[rows, :128] = tile(n * 6 + 5, 5, 0)
        proj_out[rows, 128:192] = pltpu.roll(mid, 64, 1)[:, :64]
    for n in range(59):
        flat_ref[8 * n : 8 * n + 8, :] = tile(2 * n, 4, 5)
        flat_ref[472 + 8 * n : 480 + 8 * n, :] = tile(2 * n + 1, 4, 5)
    for k in range(2 * HI):
        size = min(128, 3312 - 128 * k)
        for aw in range(3):
            for h in range(HEADS):
                part = flat_ref[pl.ds(472 * (k % 2) + 36 * (k // 2) + 12 * aw + h, 2, stride=HEADS), :]
                bias_out[aw, h, :, 128 * k : 128 * k + size] = part[:, :size]
    rest = tile(150, 5, 0) + tile(151, 5, 0)
    gain_out[:, :128] = rest[0:1]
    gain_out[:, 128:192] = rest[1:2, :64]
    scale_out[...] = rest[2:3, :HEADS]


def unpack(got):
    vmem = pl.BlockSpec(memory_space=pltpu.VMEM)
    return pl.pallas_call(
        unpack_kernel,
        out_shape=(
            jax.ShapeDtypeStruct((192, 576), F32),
            jax.ShapeDtypeStruct((192, 192), F32),
            jax.ShapeDtypeStruct((3, HEADS, 2, 3312), F32),
            jax.ShapeDtypeStruct((1, 192), F32),
            jax.ShapeDtypeStruct((1, HEADS), F32),
        ),
        in_specs=[vmem],
        out_specs=(vmem,) * 5,
        scratch_shapes=[pltpu.VMEM((944, 128), F32)],
        compiler_params=pltpu.CompilerParams(vmem_limit_bytes=20 << 20),
        name="unpack",
    )(got)


def moved(value, lon_by, lat_by):
    lon_n, lat_n = 64, 4
    pairs = []
    for lon in range(lon_n):
        for lat in range(lat_n):
            to = (lon + lon_by) % lon_n * lat_n + (lat + lat_by) % lat_n
            pairs.append((lon * lat_n + lat, to))
    return lax.ppermute(value, AXES, pairs)


def half(x):
    return lax.reduce_precision(x, 8, 7)


def sum_everywhere(parts, leaving):
    parts = lax.all_to_all(parts, LAYER, 0, 0, tiled=True).astype(F32)
    mine = lax.axis_index(LAYER) == 30

    def rounded(x):
        both = x[:8] + x[8:16]
        high = half(both)
        split = jnp.concatenate([high, both - high, x[16:]], axis=0)
        return jnp.where(mine, split, x).astype(BF16)

    weights = jnp.sum(parts[:, :40], 0)
    bands = jnp.sum(parts[:, 40:].reshape(8, 4, 32, 128), 0).reshape(128, 128)
    layer = jnp.concatenate([rounded(weights), bands.astype(BF16)], axis=0)
    layer, leaving = lax.optimization_barrier((layer, leaving))
    layers = lax.all_to_all(jnp.broadcast_to(layer, (8, 168, 128)), "z", 0, 0, tiled=True)
    lon_out, lat_out, diag_out = leaving
    arrived = (moved(lon_out, 1, 0), moved(lat_out, 0, 1), moved(diag_out, 1, 1))
    layers, arrived = lax.optimization_barrier((layers, arrived))
    total = jnp.sum(layers.astype(F32), 0)
    weights = jnp.broadcast_to(rounded(total[:40]), (8, 4, 40, 128))
    bands = jnp.broadcast_to(total[40:].astype(BF16).reshape(4, 32, 128), (8, 4, 32, 128))
    parts = jnp.concatenate([weights, bands], axis=2).reshape(32, 72, 128)
    return lax.all_to_all(parts, LAYER, 0, 0, tiled=True), arrived


def on_device(tokens, cotangent, labels, w_qkv, w_proj, logit_scale, bias_table, bias_index, norm_gain):
    both = jnp.stack([tokens[:, :, :6], cotangent[:, :, :6]])
    lon_in = moved(both[:, :, 3:], -1, 0)
    diag_in = moved(both[:, :, :3], -1, -1)
    lat_in = moved(jnp.stack([tokens[:, :3, 6:], cotangent[:, :3, 6:]]), 0, -1)

    *bias, index = pair_bias(bias_table.transpose(0, 2, 1, 3), bias_index)

    label_win = labels.reshape(2, 2, 3, 6, 12).transpose(2, 0, 1, 3, 4).reshape(6, 1, WIN).astype(F32)

    grads, sums, pairs = sublayer(
        tokens,
        cotangent,
        lon_in,
        lat_in,
        diag_in,
        label_win,
        w_qkv,
        w_proj,
        norm_gain[None],
        logit_scale[None],
        *(pltpu.with_memory_space_constraint(part, pltpu.HBM) for part in bias),
    )
    parts = by_entry(pairs, index, sums)
    own, *leaving = returns(grads, w_qkv)
    got, (lon_back, lat_back, diag_back) = sum_everywhere(parts, tuple(leaving))
    grad_qkv, grad_proj, grad_bias, grad_gain, grad_scale = unpack(got.reshape(32, 9, 8, 128))
    lon_back, lat_back, diag_back = unpacked(lon_back, 4, 15), unpacked(lat_back, 4, 3), unpacked(diag_back, 4, 3)
    returned = jnp.concatenate(
        [jnp.concatenate([diag_back, lat_back], axis=2), jnp.concatenate([lon_back, own], axis=2)], axis=1
    )
    grad_tokens = (cotangent.astype(F32) + returned.astype(F32)).astype(BF16)
    return (
        grad_tokens,
        grad_qkv,
        grad_proj,
        grad_scale[0],
        grad_bias.transpose(0, 2, 1, 3),
        grad_gain[0],
    )


def solution(mesh):
    fine = Mesh(mesh.devices.reshape(8, 4, 2, 2, 2), AXES)
    lon, lat = ("z", "y", "xl"), ("xh", "core")
    placed = (
        P(None, lat, lon, None),
        P(None, lat, lon, None),
        P(None, lat, lon),
        P(),
        P(),
        P(),
        P(lat, None, None, None),
        P(),
        P(),
    )
    return jax.shard_map(
        on_device,
        mesh=fine,
        in_specs=placed,
        out_specs=(P(None, lat, lon, None), P(), P(), P(), P(lat, None, None, None), P()),
        check_vma=False,
    )
```

```python
import jax
import jax.numpy as jnp
from jax import lax
from jax.experimental import pallas as pl
from jax.experimental.pallas import tpu as pltpu
from jax.sharding import Mesh
from jax.sharding import PartitionSpec as P


F32 = jnp.float32
BF16 = jnp.bfloat16
NEG_FILL = -1e30
HEADS = 6
WIN = 144
LANES = 896
CHUNKS = 26
HI = 13
ROWS = 40
LEAD = 2
TOGETHER = 3
MANY = 4
TILES = 162
AXES = ("z", "y", "xl", "xh", "core")
LAYER = ("y", "xl", "xh", "core")


def nt(left, right):
    return lax.dot_general(left, right, (((1,), (1,)), ((), ())), preferred_element_type=F32)


def tn(left, right):
    return lax.dot_general(left, right, (((0,), (0,)), ((), ())), preferred_element_type=F32)


def nn(left, right):
    return jnp.dot(left, right, preferred_element_type=F32)


def swap_blocks(x):
    sub = lax.broadcasted_iota(jnp.int32, x.shape, 0)
    block = lax.broadcasted_iota(jnp.int32, x.shape, 1) // 16
    for bit in (1, 2, 4):
        s_set = (sub & bit) != 0
        l_set = (block & bit) != 0
        up = pltpu.roll(pltpu.roll(x, bit, 0), 128 - 16 * bit, 1)
        down = pltpu.roll(pltpu.roll(x, 8 - bit, 0), 16 * bit, 1)
        x = jnp.where(s_set == l_set, x, jnp.where(s_set, up, down))
    return x


def bias_kernel(table_ref, given_ref, many_out, few_out, tail_out, index_ref, rows_ref, left_ref, *rest):
    given = given_ref[...].astype(F32)
    rest_q = jnp.concatenate([given[:, 128:], jnp.zeros((WIN, 112), F32)], axis=1)
    index_ref[:128, :] = given[:128, :128].T.astype(jnp.int32)
    index_ref[128:WIN, :] = rest_q[:128].T[:16].astype(jnp.int32)
    ends = jnp.concatenate([given[128:], jnp.zeros((112, WIN), F32)], axis=0)
    ends = jnp.concatenate(
        [ends[:, :128].T, jnp.concatenate([ends[:, 128:], jnp.zeros((128, 112), F32)], axis=1).T[:16]], axis=0
    )
    for by in (16, 32, 64):
        ends = ends + pltpu.roll(ends, by, 1)
    sub = lax.broadcasted_iota(jnp.int32, (WIN, 128), 0) % 8
    block = lax.broadcasted_iota(jnp.int32, (WIN, 128), 1) // 16
    ends = jnp.where(sub == block, ends, 0.0)
    for n in range(18):
        row = jnp.sum(ends[8 * n : 8 * n + 8], axis=0, keepdims=True)
        index_ref[WIN + n : WIN + n + 1, :] = row.astype(jnp.int32)
    blocks, sems = rest[:3], rest[3]
    entries = table_ref.shape[3]
    rows_ref[...] = jnp.zeros_like(rows_ref)
    for aw in range(3):
        for h in range(HEADS):
            for zw in range(2):
                row = (aw * 2 + zw) * HEADS + h
                rows_ref[row : row + 1, :entries] = table_ref[aw, h, zw : zw + 1, :]
    for k in range(HI):
        part = rows_ref[:, 256 * k : 256 * k + 256]
        high = part.astype(BF16).astype(F32)
        left_ref[0, k * ROWS : k * ROWS + ROWS, :] = high
        left_ref[1, k * ROWS : k * ROWS + ROWS, :] = part - high
    left = jnp.concatenate([left_ref[0], left_ref[1]], axis=0).astype(BF16)
    fewer = [
        left_ref[term, k * ROWS + HEADS * w : k * ROWS + HEADS * w + MANY, :]
        for term in range(2)
        for k in range(HI)
        for w in range(6)
    ]
    fewer = jnp.concatenate(fewer, axis=0).astype(BF16)
    places = lax.broadcasted_iota(jnp.int32, (256, 128), 0)

    def two(at, rows, left, block_ref, slot, to):
        index = [index_ref[pl.ds(at + t, 1), :] for t in range(2)]
        picks = jnp.concatenate(
            [jnp.where(places == (i & 255), 1.0, 0.0).astype(BF16) for i in index], axis=1
        )
        got = nn(left, picks)
        for t in range(2):
            high = index[t] >> 8
            lane = slice(128 * t, 128 * t + 128)
            total = None
            for k in range(HI):
                value = got[k * rows : k * rows + rows, lane] + got[(HI + k) * rows : (HI + k + 1) * rows, lane]
                total = value if total is None else jnp.where(high == k, value, total)
            block_ref[slot, (to + t) * rows : (to + t) * rows + rows, :] = total

    def pick(row, index):
        low = index & 127
        got = []
        for c in range(CHUNKS):
            source = jnp.broadcast_to(rows_ref[row : row + 1, c * 128 : c * 128 + 128], (8, 128))
            got.append(jnp.take_along_axis(source, low, axis=1, mode="promise_in_bounds"))
        bit = 128
        while len(got) > 1:
            odd = (index & bit) != 0
            got = [
                jnp.where(odd, got[i + 1], got[i]) if i + 1 < len(got) else got[i]
                for i in range(0, len(got), 2)
            ]
            bit *= 2
        return got[0]

    def leave(n):
        slot = n % 2
        outs = (
            many_out.at[pl.ds(pl.multiple_of(n * 16 * 6 * MANY, 8), 16 * 6 * MANY), :],
            few_out.at[:, pl.ds(pl.multiple_of(n * 16, 8), 16), :],
            tail_out.at[pl.ds(pl.multiple_of(n * 2 * ROWS, 8), 2 * ROWS), :],
        )
        return [
            pltpu.make_async_copy(block.at[slot], out, sems.at[slot, i])
            for i, (block, out) in enumerate(zip(blocks, outs))
        ]

    def step(n, carry):
        @pl.when(n >= 2)
        def _():
            for copy in leave(n - 2):
                copy.wait()

        slot = n % 2
        for u in range(8):
            two(n * 16 + 2 * u, 6 * MANY, fewer, blocks[0], slot, 2 * u)
            for v in range(3 * u, 3 * u + 3):
                w, h, b = v // 4, MANY + v // 2 % 2, v % 2
                index = index_ref[pl.ds(pl.multiple_of(n * 16 + 8 * b, 8), 8), :]
                blocks[1][slot, w * 2 + h - MANY, 8 * b : 8 * b + 8, :] = pick(w * HEADS + h, index)
        two(WIN + n * 2, ROWS, left, blocks[2], slot, 0)
        for copy in leave(n):
            copy.start()
        return carry

    lax.fori_loop(0, 9, step, 0)
    for n in (7, 8):
        for copy in leave(n):
            copy.wait()


def pair_bias(table, index):
    return pl.pallas_call(
        bias_kernel,
        out_shape=(
            pltpu.HBM((WIN * 6 * MANY, 128), F32),
            pltpu.HBM((12, WIN, 128), F32),
            pltpu.HBM((18 * ROWS, 128), F32),
            jax.ShapeDtypeStruct((TILES, 128), jnp.int32),
        ),
        in_specs=[pl.BlockSpec(memory_space=pltpu.VMEM)] * 2,
        out_specs=(pl.BlockSpec(memory_space=pltpu.HBM),) * 3 + (pl.BlockSpec(memory_space=pltpu.VMEM),),
        scratch_shapes=[
            pltpu.VMEM((ROWS, HI * 256), F32),
            pltpu.VMEM((2, HI * ROWS, 256), F32),
            pltpu.VMEM((2, 16 * 6 * MANY, 128), F32),
            pltpu.VMEM((2, 12, 16, 128), F32),
            pltpu.VMEM((2, 2 * ROWS, 128), F32),
            pltpu.SemaphoreType.DMA((2, 3)),
        ],
        compiler_params=pltpu.CompilerParams(vmem_limit_bytes=20 << 20),
        cost_estimate=pl.CostEstimate(flops=10_000_000_000, bytes_accessed=4_000_000, transcendentals=0),
        name="pair_bias",
    )(table, index)


def pack(x, n, halfway, ref):
    ref[6 * n : 6 * n + 6, :] = x[:, :128]
    rest = x[:, 128:]
    at = 12 * halfway + 6 * (n % halfway)
    if n < halfway:
        ref[at : at + 6, :64] = rest
    else:
        ref[at : at + 6, 64:] = rest


def spare(ref, n, halfway):
    at = 12 * halfway + 6 * (n % halfway)
    return ref[at : at + 6, :64] if n < halfway else ref[at : at + 6, 64:]


def leaving_kernel(tok_ref, cot_ref, lon_out, lat_out, diag_out, lon_ref, lat_ref, diag_ref):
    for n, ref in enumerate((tok_ref, cot_ref)):
        for level in range(4):
            for row in range(18):
                x = ref[level, row].astype(F32)
                if row < 3:
                    pack(x[:6], level * 3 + row, 6, diag_ref)
                    pack(x[6:], level * 3 + row, 6, lat_ref)
                else:
                    pack(x[:6], level * 15 + row - 3, 30, lon_ref)
        lon_out[n] = lon_ref[...].astype(BF16)
        lat_out[n] = lat_ref[...].astype(BF16)
        diag_out[n] = diag_ref[...].astype(BF16)


def leaving(tokens, cotangent):
    vmem = pl.BlockSpec(memory_space=pltpu.VMEM)
    shapes = ((540, 128), (108, 128), (108, 128))
    return pl.pallas_call(
        leaving_kernel,
        out_shape=tuple(jax.ShapeDtypeStruct((2,) + shape, BF16) for shape in shapes),
        in_specs=[vmem] * 2,
        out_specs=(vmem,) * 3,
        scratch_shapes=[pltpu.VMEM(shape, F32) for shape in shapes],
        compiler_params=pltpu.CompilerParams(vmem_limit_bytes=14 << 20),
        name="leaving",
    )(tokens, cotangent)


def wide(x):
    return x[:, :128], jnp.concatenate([x[:, 128:WIN], jnp.zeros((x.shape[0], 112), x.dtype)], axis=1)


def turned(x):
    main, tail = wide(x)
    return jnp.concatenate([main.T, tail.T[:16]], axis=0)


def spread(xt, tail_mask):
    main, tail = wide(xt)
    for by in (16, 32, 64):
        tail = tail + pltpu.roll(tail, by, 1)
    tail = jnp.where(tail_mask, tail, 0.0).astype(BF16)
    main = main.astype(BF16)
    zero = jnp.zeros((32, 128), BF16)
    pairs = []
    for j in range(3):
        top = jnp.concatenate([main[64 * j : 64 * j + 32], zero], axis=1)
        low = jnp.concatenate([zero, main[64 * j + 32 : 64 * j + 64]], axis=1)
        pairs.append(jnp.concatenate([top, low], axis=0))
    return pairs, tail


def across(left, right, take):
    pairs, tail = right
    for j in range(3):
        part = nn(left[:, 64 * j : 64 * j + 64], pairs[j])
        yield
        take(2 * j, part[:, :128])
        yield
        take(2 * j + 1, part[:, 128:])
    part = nn(left, tail)
    yield
    take(HEADS, part)


def gather_heads(left, right):
    main = []
    for j in range(3):
        part = nn(left[64 * j : 64 * j + 64], right[:, 256 * j : 256 * j + 256])
        main += [part[:32, :128], part[32:, 128:]]
    tail = nn(left, right[:, 768:])
    tails = [tail[:32]] + [pltpu.roll(tail[32 * h : 32 * h + 32], 128 - 16 * h, 1) for h in range(1, HEADS)]
    return jnp.concatenate([jnp.concatenate(main, axis=0), jnp.concatenate(tails, axis=0)[:, :16]], axis=1)


def gather_keys(left, right):
    pairs, tail = left
    main = [nt(pairs[j], right[:, 256 * j : 256 * j + 256]) for j in range(3)]
    return jnp.concatenate(main, axis=0) + nt(tail, right[:, 768:])


def head_sum(x):
    sums = [jnp.sum(x[32 * h : 32 * h + 32], axis=0, keepdims=True) for h in range(HEADS)]
    return jnp.concatenate([jnp.broadcast_to(t, (32, WIN)) for t in sums], axis=0)


def column(row):
    return jnp.broadcast_to(row, (8, row.shape[1])).T[:, :1]


def unpacked(dense, levels, rows):
    n = levels * rows * 6
    rest = jnp.concatenate([dense[n:, :64], dense[n:, 64:]], axis=0)
    return jnp.concatenate([dense[:n], rest], axis=1).reshape(levels, rows, 6, 192)


def places():
    for w in range(6):
        aw, zw = w // 2, w % 2
        for i in range(2):
            level = (2 * zw + i + 1) % 4
            for j in range(6):
                yield w * WIN + (i * 6 + j) * 12, level, aw * 6 + j


def layer_kernel(
    tok_ref,
    cot_ref,
    lon_ref,
    lat_ref,
    diag_ref,
    label_ref,
    wqkv_ref,
    proj_ref,
    gain_ref,
    scale_ref,
    many_hbm,
    few_hbm,
    tail_hbm,
    grads_out,
    sums_out,
    pairs_out,
    lon_wide,
    lat_wide,
    diag_wide,
    x_ref,
    g_ref,
    grads_ref,
    grads_sems,
    wt_ref,
    projt_ref,
    sum_w_ref,
    sum_p_ref,
    sum_g_ref,
    sum_s_ref,
    many_ref,
    few_ref,
    tail_ref,
    bias_sems,
    *slots,
):
    arriving = [
        pltpu.make_async_copy(source, to, bias_sems.at[i])
        for i, (source, to) in enumerate(
            ((many_hbm, many_ref), (few_hbm, few_ref), (tail_hbm, tail_ref))
        )
    ]
    for copy in arriving:
        copy.start()

    for wide_ref, ref in ((lon_wide, lon_ref), (lat_wide, lat_ref), (diag_wide, diag_ref)):
        wide_ref[...] = ref[...].astype(F32)

    def place(ref, n, halfway, to, at):
        to[at : at + 6, :128] = ref[6 * n : 6 * n + 6, :]
        to[at : at + 6, 128:] = spare(ref, n, halfway)

    for base, level, row in places():
        for n, (own, to) in enumerate(((tok_ref, x_ref), (cot_ref, g_ref))):
            if row < 15:
                to[base : base + 6, :] = own[level, row + 3].astype(F32)[6:]
            else:
                place(lat_wide.at[n], level * 3 + row - 15, 6, to, base)
            if row < 15:
                place(lon_wide.at[n], level * 15 + row, 30, to, base + 6)
            else:
                place(diag_wide.at[n], level * 3 + row - 15, 6, to, base + 6)

    width = 192
    for n in range(3):
        wt_ref[width * n : width * n + width, :] = (
            wqkv_ref[:, width * n : width * n + width].astype(F32).T.astype(BF16)
        )
    projt_ref[...] = proj_ref[...].astype(F32).T.astype(BF16)
    for ref in (sum_w_ref, sum_p_ref, sum_g_ref, sum_s_ref):
        ref[...] = jnp.zeros_like(ref)
    gain = column(gain_ref[...])
    temper = jnp.exp(scale_ref[...])
    lanes = lax.broadcasted_iota(jnp.int32, (1, LANES), 1)
    lane_head = jnp.where(lanes < 768, lanes // 128, (lanes - 768) // 16)
    row_head = lax.broadcasted_iota(jnp.int32, (width, 128), 0) // 32
    tail_mask = row_head == lax.broadcasted_iota(jnp.int32, (width, 128), 1) // 16
    temper_row = jnp.zeros((1, LANES), F32)
    temper_col = jnp.zeros((width, 1), F32)
    for h in range(HEADS):
        temper_row = jnp.where(lane_head == h, temper[:, h : h + 1], temper_row)
        temper_col = jnp.where(row_head[:, :1] == h, temper[:, h : h + 1], temper_col)

    def leave(w):
        return pltpu.make_async_copy(grads_ref.at[w], grads_out.at[w], grads_sems.at[w])

    def window(n, slot):
        w = n * TOGETHER + slot
        cosine_ref, probs_ref, half_ref, column_ref = (ref.at[slot] for ref in slots)
        at = pl.ds(pl.multiple_of(w * WIN, 16), WIN)
        x = x_ref[at, :].astype(BF16)
        projected = nt(wt_ref[...], x).astype(BF16).astype(F32)
        yield
        query, key, value = (projected[width * n : width * n + width] for n in range(3))
        query_inv = lax.rsqrt(head_sum(query * query) + 1.0)
        key_inv = lax.rsqrt(head_sum(key * key) + 1.0)
        yield
        key_unit = (key * key_inv).astype(BF16).astype(F32)
        yield
        queries = spread((query * query_inv).astype(BF16).astype(F32), tail_mask)
        label = label_ref[w]
        tail = jnp.concatenate([label[:, 128:]] * 8, axis=1)
        label_col = jnp.concatenate([column(label[:, :128]), column(tail)[:16]], axis=0)
        column_ref[...] = jnp.broadcast_to(label_col, (WIN, 128))

        def soften(t, cosine):
            lane = slice(128 * t, 128 * t + 128)
            cosine_ref[:, lane] = cosine
            if t < MANY:
                bias = many_ref[pl.ds(w * MANY + t, WIN, stride=6 * MANY), :]
            elif t < HEADS:
                bias = few_ref[w * 2 + t - MANY]
            else:
                bias = []
                for n in range(18):
                    part = tail_ref[pl.ds(n * ROWS + w * HEADS, HEADS), :]
                    bias.append(swap_blocks(jnp.concatenate([part, jnp.zeros((2, 128), F32)], axis=0)))
                bias = jnp.concatenate(bias, axis=0)
            scores = cosine * temper_row[:, lane] + bias
            same = column_ref[...] == (label[:, :128] if t < HEADS else tail)
            scores = jnp.where(same, scores, NEG_FILL)
            weights = jnp.exp(scores - jnp.max(scores, axis=0, keepdims=True))
            probs = weights * (1.0 / jnp.sum(weights, axis=0, keepdims=True))
            probs_ref[:, lane] = probs
            half_ref[:, lane] = probs.astype(BF16)

        key_turned = turned(key_unit).astype(BF16)
        yield
        if slot == 0:

            @pl.when(n == 0)
            def _():
                for copy in arriving:
                    copy.wait()

        yield from across(key_turned, queries, soften)
        yield
        probs_half = half_ref[...]
        yield
        mixed = gather_heads(value.astype(BF16), probs_half).astype(BF16)
        yield
        att = nn(projt_ref[...], mixed).astype(BF16).astype(F32)
        yield
        center = att - jnp.sum(att, axis=0, keepdims=True) * (1.0 / width)
        inv_std = lax.rsqrt(jnp.sum(center * center, axis=0, keepdims=True) * (1.0 / width) + 1e-5)
        yield
        normed = center * inv_std
        yield
        grad = g_ref[at, :]
        grad = jnp.concatenate([grad[:128].T, jnp.concatenate([grad[128:], grad[:112]], axis=0).T[:, :16]], axis=1)
        yield
        sum_g_ref[...] += grad * normed
        grad = grad * gain
        yield
        grad_mean = jnp.sum(grad, axis=0, keepdims=True) * (1.0 / width)
        both_mean = jnp.sum(grad * normed, axis=0, keepdims=True) * (1.0 / width)
        grad_att = (inv_std * (grad - grad_mean - normed * both_mean)).astype(BF16)
        yield
        sum_p_ref[...] += nt(mixed, grad_att)
        yield
        grad_mixed = spread(nn(proj_ref[...], grad_att).astype(BF16).astype(F32), tail_mask)
        yield
        grad_value = gather_keys(grad_mixed, probs_half)

        def harden(t, grad_probs):
            lane = slice(128 * t, 128 * t + 128)
            probs = probs_ref[:, lane]
            along = jnp.sum(grad_probs * probs, axis=0, keepdims=True)
            grad_scores = probs * (grad_probs - along)
            sum_s_ref[:, lane] += jnp.sum(grad_scores * cosine_ref[:, lane], axis=0, keepdims=True)
            half_ref[:, lane] = grad_scores.astype(BF16)
            if t < HEADS:
                pairs_out[pl.ds(w * HEADS + t, WIN, stride=ROWS), :] = grad_scores
            else:
                for n in range(18):
                    block = swap_blocks(grad_scores[8 * n : 8 * n + 8])
                    pairs_out[pl.ds((WIN + n) * ROWS + w * HEADS, HEADS), :] = block[:HEADS]

        yield from across(turned(value).astype(BF16), grad_mixed, harden)
        yield
        scores_half = half_ref[...]
        grad_qunit = gather_heads(key_unit.astype(BF16), scores_half) * temper_col
        yield
        grad_kunit = gather_keys(queries, scores_half) * temper_col
        yield
        grad_query = query_inv * grad_qunit - query * (query_inv * query_inv * query_inv) * head_sum(
            query * grad_qunit
        )
        yield
        grad_key = key_inv * grad_kunit - key * (key_inv * key_inv * key_inv) * head_sum(key * grad_kunit)
        yield
        grad_all = jnp.concatenate([grad_query, grad_key, grad_value], axis=0).astype(BF16)
        yield
        sum_w_ref[...] += nn(grad_all, x)
        grads_ref[w] = grad_all
        leave(w).start()

    def group(n, carry):
        going = [window(n, slot) for slot in range(TOGETHER)]
        for slot, one in enumerate(going):
            for _ in range(LEAD * (TOGETHER - 1 - slot)):
                next(one)
        while going:
            going = [one for one in going if next(one, going) is None]
        return carry

    lax.fori_loop(0, 6 // TOGETHER, group, 0)

    grad_q, grad_k, grad_v = (sum_w_ref[width * n : width * n + width, :].T for n in range(3))
    grad_p = sum_p_ref[...]
    gain_sum = jnp.sum(sum_g_ref[...], axis=1, keepdims=True)
    gain_sum = jnp.broadcast_to(gain_sum, (width, 128)).T[:1]
    k_turned = pltpu.roll(jnp.concatenate([grad_k, jnp.zeros((width, 64), F32)], axis=1), 64, 1)
    p_end = pltpu.roll(jnp.concatenate([grad_p[:, 128:], jnp.zeros((width, 64), F32)], axis=1), 64, 1)
    zero = jnp.zeros((width, 64), F32)
    columns = [
        grad_q[:, :128],
        jnp.concatenate([grad_q[:, 128:], zero], axis=1) + jnp.concatenate([zero, k_turned[:, 64:128]], axis=1),
        k_turned[:, 128:256],
        grad_v[:, :128],
        jnp.concatenate([grad_v[:, 128:], zero], axis=1) + p_end,
        grad_p[:, :128],
    ]
    sums_out[...] = jnp.zeros_like(sums_out)
    for c, tiles in enumerate(columns):
        for n in range(24):
            sums_out[n * 6 + c] = tiles[8 * n : 8 * n + 8]
    lane = lax.broadcasted_iota(jnp.int32, (1, 128), 1)
    for w in range(6):
        leave(w).wait()
    scale_sum = sum_s_ref[...] * temper_row
    scale_row = jnp.zeros((1, 128), F32)
    for h in range(HEADS):
        main = jnp.sum(scale_sum[:, 128 * h : 128 * h + 128], axis=1, keepdims=True)
        tail = jnp.where((lane >= 16 * h) & (lane < 16 * h + 16), scale_sum[:, 768:], 0.0)
        total = main + jnp.sum(tail, axis=1, keepdims=True)
        scale_row = scale_row + jnp.where(lane == h, total, 0.0)
    rest = jnp.concatenate(
        [
            gain_sum[:, :128],
            jnp.concatenate([gain_sum[:, 128:], jnp.zeros((1, 64), F32)], axis=1),
            scale_row,
            jnp.zeros((5, 128), F32),
        ],
        axis=0,
    )
    high = rest.astype(BF16).astype(F32)
    sums_out[150] = high
    sums_out[151] = rest - high


def sublayer(*args):
    vmem = pl.BlockSpec(memory_space=pltpu.VMEM)
    tokens_n = 6 * WIN
    return pl.pallas_call(
        layer_kernel,
        out_shape=(
            pltpu.HBM((6, 576, WIN), BF16),
            jax.ShapeDtypeStruct((160, 8, 128), F32),
            jax.ShapeDtypeStruct((TILES * ROWS, 128), F32),
        ),
        in_specs=[vmem] * (len(args) - 3) + [pl.BlockSpec(memory_space=pltpu.HBM)] * 3,
        out_specs=(pl.BlockSpec(memory_space=pltpu.HBM), vmem, vmem),
        scratch_shapes=[pltpu.VMEM((2, 540, 128), F32)]
        + [pltpu.VMEM((2, 108, 128), F32)] * 2
        + [pltpu.VMEM((tokens_n, 192), F32)] * 2
        + [pltpu.VMEM((6, 576, WIN), BF16), pltpu.SemaphoreType.DMA((6,))]
        + [pltpu.VMEM((576, 192), BF16), pltpu.VMEM((192, 192), BF16)]
        + [pltpu.VMEM((576, 192), F32), pltpu.VMEM((192, 192), F32), pltpu.VMEM((192, WIN), F32), pltpu.VMEM((1, LANES), F32)]
        + [pltpu.VMEM((WIN * 6 * MANY, 128), F32), pltpu.VMEM((12, WIN, 128), F32)]
        + [pltpu.VMEM((18 * ROWS, 128), F32), pltpu.SemaphoreType.DMA((3,))]
        + [pltpu.VMEM((TOGETHER, WIN, LANES), F32)] * 2
        + [pltpu.VMEM((TOGETHER, WIN, LANES), BF16), pltpu.VMEM((TOGETHER, WIN, 128), F32)],
        compiler_params=pltpu.CompilerParams(vmem_limit_bytes=20 << 20),
        cost_estimate=pl.CostEstimate(flops=1_500_000_000, bytes_accessed=10_000_000, transcendentals=800_000),
        name="sublayer",
    )(*args)


def return_kernel(
    grads_ref, wqkv_ref, own_out, lon_out, lat_out, diag_out, gwin_ref, lon_ref32, lat_ref32, diag_ref32
):
    for w in range(6):
        gwin_ref[w * WIN : w * WIN + WIN, :] = turned(nn(wqkv_ref[...], grads_ref[w]))
    for base, level, row in places():
        left = gwin_ref[base : base + 6, :]
        right = gwin_ref[base + 6 : base + 12, :]
        if row < 15:
            own_out[level, row] = left.astype(BF16)
            pack(right, level * 15 + row, 30, lon_ref32)
        else:
            pack(left, level * 3 + row - 15, 6, lat_ref32)
            pack(right, level * 3 + row - 15, 6, diag_ref32)
    lon_out[...] = lon_ref32[...].astype(BF16)
    lat_out[...] = lat_ref32[...].astype(BF16)
    diag_out[...] = diag_ref32[...].astype(BF16)


def returns(grads, w_qkv):
    vmem = pl.BlockSpec(memory_space=pltpu.VMEM)
    return pl.pallas_call(
        return_kernel,
        out_shape=(
            jax.ShapeDtypeStruct((4, 15, 6, 192), BF16),
            jax.ShapeDtypeStruct((540, 128), BF16),
            jax.ShapeDtypeStruct((108, 128), BF16),
            jax.ShapeDtypeStruct((108, 128), BF16),
        ),
        in_specs=[vmem] * 2,
        out_specs=(vmem,) * 4,
        scratch_shapes=[pltpu.VMEM((6 * WIN, 192), F32), pltpu.VMEM((540, 128), F32)]
        + [pltpu.VMEM((108, 128), F32)] * 2,
        compiler_params=pltpu.CompilerParams(vmem_limit_bytes=14 << 20),
        cost_estimate=pl.CostEstimate(flops=2_000_000_000, bytes_accessed=3_000_000, transcendentals=0),
        name="returns",
    )(grads, w_qkv)


def entry_kernel(pairs_ref, index_ref, sums_ref, out_ref, acc_ref):
    acc_ref[...] = jnp.zeros_like(acc_ref)
    places = lax.broadcasted_iota(jnp.int32, (256, 128), 0)

    def step(n, carry):
        lefts, rights = [], []
        for t in range(18):
            tile = n * 18 + t
            index = index_ref[pl.ds(tile, 1), :]
            low, high = index & 255, index >> 8
            rights.append(jnp.where(places == low, 1.0, 0.0).astype(BF16))
            pairs = pairs_ref[pl.ds(pl.multiple_of(tile * ROWS, 8), ROWS), :]
            lefts.append(
                jnp.concatenate([jnp.where(high == k, pairs, 0.0) for k in range(HI)], axis=0).astype(BF16)
            )
        acc_ref[...] += nt(jnp.concatenate(lefts, axis=1), jnp.concatenate(rights, axis=1))
        return carry

    lax.fori_loop(0, TILES // 18, step, 0)
    rows = [acc_ref[k * ROWS : k * ROWS + 36, :] for k in range(HI)]
    rows = jnp.concatenate(rows + [jnp.zeros((44, 256), F32)], axis=0)
    for c in range(32):
        tiles = [sums_ref[5 * c + n] for n in range(5)]
        for n in range(2 * c, 2 * c + 2):
            tiles += [rows[8 * n : 8 * n + 8, :128], rows[8 * n : 8 * n + 8, 128:]]
        out_ref[c] = jnp.concatenate(tiles, axis=0).astype(BF16)


def by_entry(pairs, index, sums):
    vmem = pl.BlockSpec(memory_space=pltpu.VMEM)
    return pl.pallas_call(
        entry_kernel,
        out_shape=jax.ShapeDtypeStruct((32, 72, 128), BF16),
        in_specs=[vmem] * 3,
        out_specs=vmem,
        scratch_shapes=[pltpu.VMEM((HI * ROWS, 256), F32)],
        compiler_params=pltpu.CompilerParams(vmem_limit_bytes=20 << 20),
        cost_estimate=pl.CostEstimate(flops=5_000_000_000, bytes_accessed=4_000_000, transcendentals=0),
        name="by_entry",
    )(pairs, index, sums)


def unpack_kernel(got_ref, qkv_out, proj_out, bias_out, gain_out, scale_out, flat_ref):
    def tile(n, slots, at):
        return got_ref[n // slots, at + n % slots].astype(F32)

    for n in range(24):
        rows = pl.ds(8 * n, 8)
        for c in range(4):
            qkv_out[rows, 128 * c : 128 * c + 128] = tile(n * 6 + c, 5, 0)
        mid = tile(n * 6 + 4, 5, 0)
        qkv_out[rows, 512:576] = mid[:, :64]
        proj_out[rows, :128] = tile(n * 6 + 5, 5, 0)
        proj_out[rows, 128:192] = pltpu.roll(mid, 64, 1)[:, :64]
    for n in range(59):
        flat_ref[8 * n : 8 * n + 8, :] = tile(2 * n, 4, 5)
        flat_ref[472 + 8 * n : 480 + 8 * n, :] = tile(2 * n + 1, 4, 5)
    for k in range(2 * HI):
        size = min(128, 3312 - 128 * k)
        for aw in range(3):
            for h in range(HEADS):
                part = flat_ref[pl.ds(472 * (k % 2) + 36 * (k // 2) + 12 * aw + h, 2, stride=HEADS), :]
                bias_out[aw, h, :, 128 * k : 128 * k + size] = part[:, :size]
    rest = tile(150, 5, 0) + tile(151, 5, 0)
    gain_out[:, :128] = rest[0:1]
    gain_out[:, 128:192] = rest[1:2, :64]
    scale_out[...] = rest[2:3, :HEADS]


def unpack(got):
    vmem = pl.BlockSpec(memory_space=pltpu.VMEM)
    return pl.pallas_call(
        unpack_kernel,
        out_shape=(
            jax.ShapeDtypeStruct((192, 576), F32),
            jax.ShapeDtypeStruct((192, 192), F32),
            jax.ShapeDtypeStruct((3, HEADS, 2, 3312), F32),
            jax.ShapeDtypeStruct((1, 192), F32),
            jax.ShapeDtypeStruct((1, HEADS), F32),
        ),
        in_specs=[vmem],
        out_specs=(vmem,) * 5,
        scratch_shapes=[pltpu.VMEM((944, 128), F32)],
        compiler_params=pltpu.CompilerParams(vmem_limit_bytes=20 << 20),
        name="unpack",
    )(got)


def moved(value, lon_by, lat_by):
    lon_n, lat_n = 64, 4
    pairs = []
    for lon in range(lon_n):
        for lat in range(lat_n):
            to = (lon + lon_by) % lon_n * lat_n + (lat + lat_by) % lat_n
            pairs.append((lon * lat_n + lat, to))
    return lax.ppermute(value, AXES, pairs)


def half(x):
    return lax.reduce_precision(x, 8, 7)


def sum_everywhere(parts, leaving):
    parts = lax.all_to_all(parts, LAYER, 0, 0, tiled=True).astype(F32)
    mine = lax.axis_index(LAYER) == 30

    def rounded(x):
        both = x[:8] + x[8:16]
        high = half(both)
        split = jnp.concatenate([high, both - high, x[16:]], axis=0)
        return jnp.where(mine, split, x).astype(BF16)

    weights = jnp.sum(parts[:, :40], 0)
    bands = jnp.sum(parts[:, 40:].reshape(8, 4, 32, 128), 0).reshape(128, 128)
    layer = jnp.concatenate([rounded(weights), bands.astype(BF16)], axis=0)
    layer, leaving = lax.optimization_barrier((layer, leaving))
    layers = lax.all_to_all(jnp.broadcast_to(layer, (8, 168, 128)), "z", 0, 0, tiled=True)
    lon_out, lat_out, diag_out = leaving
    arrived = (moved(lon_out, 1, 0), moved(lat_out, 0, 1), moved(diag_out, 1, 1))
    layers, arrived = lax.optimization_barrier((layers, arrived))
    total = jnp.sum(layers.astype(F32), 0)
    weights = jnp.broadcast_to(rounded(total[:40]), (8, 4, 40, 128))
    bands = jnp.broadcast_to(total[40:].astype(BF16).reshape(4, 32, 128), (8, 4, 32, 128))
    parts = jnp.concatenate([weights, bands], axis=2).reshape(32, 72, 128)
    return lax.all_to_all(parts, LAYER, 0, 0, tiled=True), arrived


def on_device(tokens, cotangent, labels, w_qkv, w_proj, logit_scale, bias_table, bias_index, norm_gain):
    lon_in, lat_in, diag_in = leaving(tokens, cotangent)
    lat_in = moved(lat_in, 0, -1)
    lon_in = moved(lon_in, -1, 0)
    diag_in = moved(diag_in, -1, -1)

    *bias, index = pair_bias(bias_table.transpose(0, 2, 1, 3), bias_index)

    label_win = labels.reshape(2, 2, 3, 6, 12).transpose(2, 0, 1, 3, 4).reshape(6, 1, WIN).astype(F32)

    grads, sums, pairs = sublayer(
        tokens,
        cotangent,
        lon_in,
        lat_in,
        diag_in,
        label_win,
        w_qkv,
        w_proj,
        norm_gain[None],
        logit_scale[None],
        *(pltpu.with_memory_space_constraint(part, pltpu.HBM) for part in bias),
    )
    parts = by_entry(pairs, index, sums)
    own, *back = returns(grads, w_qkv)
    got, (lon_back, lat_back, diag_back) = sum_everywhere(parts, tuple(back))
    grad_qkv, grad_proj, grad_bias, grad_gain, grad_scale = unpack(got.reshape(32, 9, 8, 128))
    lon_back, lat_back, diag_back = unpacked(lon_back, 4, 15), unpacked(lat_back, 4, 3), unpacked(diag_back, 4, 3)
    returned = jnp.concatenate(
        [jnp.concatenate([diag_back, lat_back], axis=2), jnp.concatenate([lon_back, own], axis=2)], axis=1
    )
    grad_tokens = (cotangent.astype(F32) + returned.astype(F32)).astype(BF16)
    return (
        grad_tokens,
        grad_qkv,
        grad_proj,
        grad_scale[0],
        grad_bias.transpose(0, 2, 1, 3),
        grad_gain[0],
    )


def solution(mesh):
    fine = Mesh(mesh.devices.reshape(8, 4, 2, 2, 2), AXES)
    lon, lat = ("z", "y", "xl"), ("xh", "core")
    placed = (
        P(None, lat, lon, None),
        P(None, lat, lon, None),
        P(None, lat, lon),
        P(),
        P(),
        P(),
        P(lat, None, None, None),
        P(),
        P(),
    )
    return jax.shard_map(
        on_device,
        mesh=fine,
        in_specs=placed,
        out_specs=(P(None, lat, lon, None), P(), P(), P(), P(lat, None, None, None), P()),
        check_vma=False,
    )
```

```python
import jax
import jax.numpy as jnp
from jax import lax
from jax.experimental import pallas as pl
from jax.experimental.pallas import tpu as pltpu
from jax.sharding import Mesh
from jax.sharding import PartitionSpec as P


F32 = jnp.float32
BF16 = jnp.bfloat16
NEG_FILL = -1e30
HEADS = 6
WIN = 144
LANES = 896
CHUNKS = 26
HI = 13
ROWS = 40
LEAD = 2
TOGETHER = 3
MANY = 4
TILES = 162
AXES = ("z", "y", "xl", "xh", "core")
LAYER = ("y", "xl", "xh", "core")


def nt(left, right):
    return lax.dot_general(left, right, (((1,), (1,)), ((), ())), preferred_element_type=F32)


def tn(left, right):
    return lax.dot_general(left, right, (((0,), (0,)), ((), ())), preferred_element_type=F32)


def nn(left, right):
    return jnp.dot(left, right, preferred_element_type=F32)


def swap_blocks(x):
    sub = lax.broadcasted_iota(jnp.int32, x.shape, 0)
    block = lax.broadcasted_iota(jnp.int32, x.shape, 1) // 16
    for bit in (1, 2, 4):
        s_set = (sub & bit) != 0
        l_set = (block & bit) != 0
        up = pltpu.roll(pltpu.roll(x, bit, 0), 128 - 16 * bit, 1)
        down = pltpu.roll(pltpu.roll(x, 8 - bit, 0), 16 * bit, 1)
        x = jnp.where(s_set == l_set, x, jnp.where(s_set, up, down))
    return x


def bias_kernel(table_ref, given_ref, many_out, few_out, tail_out, index_ref, rows_ref, left_ref, *rest):
    given = given_ref[...].astype(F32)
    rest_q = jnp.concatenate([given[:, 128:], jnp.zeros((WIN, 112), F32)], axis=1)
    index_ref[:128, :] = given[:128, :128].T.astype(jnp.int32)
    index_ref[128:WIN, :] = rest_q[:128].T[:16].astype(jnp.int32)
    ends = jnp.concatenate([given[128:], jnp.zeros((112, WIN), F32)], axis=0)
    ends = jnp.concatenate(
        [ends[:, :128].T, jnp.concatenate([ends[:, 128:], jnp.zeros((128, 112), F32)], axis=1).T[:16]], axis=0
    )
    for by in (16, 32, 64):
        ends = ends + pltpu.roll(ends, by, 1)
    sub = lax.broadcasted_iota(jnp.int32, (WIN, 128), 0) % 8
    block = lax.broadcasted_iota(jnp.int32, (WIN, 128), 1) // 16
    ends = jnp.where(sub == block, ends, 0.0)
    for n in range(18):
        row = jnp.sum(ends[8 * n : 8 * n + 8], axis=0, keepdims=True)
        index_ref[WIN + n : WIN + n + 1, :] = row.astype(jnp.int32)
    blocks, sems = rest[:3], rest[3]
    entries = table_ref.shape[3]
    rows_ref[...] = jnp.zeros_like(rows_ref)
    for aw in range(3):
        for h in range(HEADS):
            for zw in range(2):
                row = (aw * 2 + zw) * HEADS + h
                rows_ref[row : row + 1, :entries] = table_ref[aw, h, zw : zw + 1, :]
    for k in range(HI):
        part = rows_ref[:, 256 * k : 256 * k + 256]
        high = part.astype(BF16).astype(F32)
        left_ref[0, k * ROWS : k * ROWS + ROWS, :] = high
        left_ref[1, k * ROWS : k * ROWS + ROWS, :] = part - high
    left = jnp.concatenate([left_ref[0], left_ref[1]], axis=0).astype(BF16)
    fewer = [
        left_ref[term, k * ROWS + HEADS * w : k * ROWS + HEADS * w + MANY, :]
        for term in range(2)
        for k in range(HI)
        for w in range(6)
    ]
    fewer = jnp.concatenate(fewer, axis=0).astype(BF16)
    places = lax.broadcasted_iota(jnp.int32, (256, 128), 0)

    def two(at, rows, left, block_ref, slot, to):
        index = [index_ref[pl.ds(at + t, 1), :] for t in range(2)]
        picks = jnp.concatenate(
            [jnp.where(places == (i & 255), 1.0, 0.0).astype(BF16) for i in index], axis=1
        )
        got = nn(left, picks)
        for t in range(2):
            high = index[t] >> 8
            lane = slice(128 * t, 128 * t + 128)
            total = None
            for k in range(HI):
                value = got[k * rows : k * rows + rows, lane] + got[(HI + k) * rows : (HI + k + 1) * rows, lane]
                total = value if total is None else jnp.where(high == k, value, total)
            block_ref[slot, (to + t) * rows : (to + t) * rows + rows, :] = total

    def pick(row, index):
        low = index & 127
        got = []
        for c in range(CHUNKS):
            source = jnp.broadcast_to(rows_ref[row : row + 1, c * 128 : c * 128 + 128], (8, 128))
            got.append(jnp.take_along_axis(source, low, axis=1, mode="promise_in_bounds"))
        bit = 128
        while len(got) > 1:
            odd = (index & bit) != 0
            got = [
                jnp.where(odd, got[i + 1], got[i]) if i + 1 < len(got) else got[i]
                for i in range(0, len(got), 2)
            ]
            bit *= 2
        return got[0]

    def leave(n):
        slot = n % 2
        outs = (
            many_out.at[pl.ds(pl.multiple_of(n * 48 * 6 * MANY, 8), 48 * 6 * MANY), :],
            few_out.at[:, pl.ds(pl.multiple_of(n * 48, 8), 48), :],
            tail_out.at[pl.ds(pl.multiple_of(n * 6 * ROWS, 8), 6 * ROWS), :],
        )
        return [
            pltpu.make_async_copy(block.at[slot], out, sems.at[slot, i])
            for i, (block, out) in enumerate(zip(blocks, outs))
        ]

    def step(n, carry):
        @pl.when(n >= 2)
        def _():
            for copy in leave(n - 2):
                copy.wait()

        slot = n % 2
        for u in range(24):
            two(n * 48 + 2 * u, 6 * MANY, fewer, blocks[0], slot, 2 * u)
            for v in range(3 * u, 3 * u + 3):
                w, h, b = v // 12, MANY + v // 6 % 2, v % 6
                index = index_ref[pl.ds(pl.multiple_of(n * 48 + 8 * b, 8), 8), :]
                blocks[1][slot, w * 2 + h - MANY, 8 * b : 8 * b + 8, :] = pick(w * HEADS + h, index)
        for u in range(3):
            two(WIN + n * 6 + 2 * u, ROWS, left, blocks[2], slot, 2 * u)
        for copy in leave(n):
            copy.start()
        return carry

    lax.fori_loop(0, 3, step, 0)
    for n in (1, 2):
        for copy in leave(n):
            copy.wait()


def pair_bias(table, index):
    return pl.pallas_call(
        bias_kernel,
        out_shape=(
            pltpu.HBM((WIN * 6 * MANY, 128), F32),
            pltpu.HBM((12, WIN, 128), F32),
            pltpu.HBM((18 * ROWS, 128), F32),
            jax.ShapeDtypeStruct((TILES, 128), jnp.int32),
        ),
        in_specs=[pl.BlockSpec(memory_space=pltpu.VMEM)] * 2,
        out_specs=(pl.BlockSpec(memory_space=pltpu.HBM),) * 3 + (pl.BlockSpec(memory_space=pltpu.VMEM),),
        scratch_shapes=[
            pltpu.VMEM((ROWS, HI * 256), F32),
            pltpu.VMEM((2, HI * ROWS, 256), F32),
            pltpu.VMEM((2, 48 * 6 * MANY, 128), F32),
            pltpu.VMEM((2, 12, 48, 128), F32),
            pltpu.VMEM((2, 6 * ROWS, 128), F32),
            pltpu.SemaphoreType.DMA((2, 3)),
        ],
        compiler_params=pltpu.CompilerParams(vmem_limit_bytes=20 << 20),
        cost_estimate=pl.CostEstimate(flops=10_000_000_000, bytes_accessed=4_000_000, transcendentals=0),
        name="pair_bias",
    )(table, index)


def pack(x, n, halfway, ref):
    ref[6 * n : 6 * n + 6, :] = x[:, :128]
    rest = x[:, 128:]
    at = 12 * halfway + 6 * (n % halfway)
    if n < halfway:
        ref[at : at + 6, :64] = rest
    else:
        ref[at : at + 6, 64:] = rest


def spare(ref, n, halfway):
    at = 12 * halfway + 6 * (n % halfway)
    return ref[at : at + 6, :64] if n < halfway else ref[at : at + 6, 64:]


def leaving_kernel(tok_ref, cot_ref, lon_out, lat_out, diag_out, lon_ref, lat_ref, diag_ref):
    for n, ref in enumerate((tok_ref, cot_ref)):
        for level in range(4):
            for row in range(18):
                x = ref[level, row].astype(F32)
                if row < 3:
                    pack(x[:6], level * 3 + row, 6, diag_ref)
                    pack(x[6:], level * 3 + row, 6, lat_ref)
                else:
                    pack(x[:6], level * 15 + row - 3, 30, lon_ref)
        lon_out[n] = lon_ref[...].astype(BF16)
        lat_out[n] = lat_ref[...].astype(BF16)
        diag_out[n] = diag_ref[...].astype(BF16)


def leaving(tokens, cotangent):
    vmem = pl.BlockSpec(memory_space=pltpu.VMEM)
    shapes = ((540, 128), (108, 128), (108, 128))
    return pl.pallas_call(
        leaving_kernel,
        out_shape=tuple(jax.ShapeDtypeStruct((2,) + shape, BF16) for shape in shapes),
        in_specs=[vmem] * 2,
        out_specs=(vmem,) * 3,
        scratch_shapes=[pltpu.VMEM(shape, F32) for shape in shapes],
        compiler_params=pltpu.CompilerParams(vmem_limit_bytes=14 << 20),
        name="leaving",
    )(tokens, cotangent)


def wide(x):
    return x[:, :128], jnp.concatenate([x[:, 128:WIN], jnp.zeros((x.shape[0], 112), x.dtype)], axis=1)


def turned(x):
    main, tail = wide(x)
    return jnp.concatenate([main.T, tail.T[:16]], axis=0)


def spread(xt, tail_mask):
    main, tail = wide(xt)
    for by in (16, 32, 64):
        tail = tail + pltpu.roll(tail, by, 1)
    tail = jnp.where(tail_mask, tail, 0.0).astype(BF16)
    main = main.astype(BF16)
    zero = jnp.zeros((32, 128), BF16)
    pairs = []
    for j in range(3):
        top = jnp.concatenate([main[64 * j : 64 * j + 32], zero], axis=1)
        low = jnp.concatenate([zero, main[64 * j + 32 : 64 * j + 64]], axis=1)
        pairs.append(jnp.concatenate([top, low], axis=0))
    return pairs, tail


def across(left, right, take):
    pairs, tail = right
    for j in range(3):
        part = nn(left[:, 64 * j : 64 * j + 64], pairs[j])
        yield
        take(2 * j, part[:, :128])
        yield
        take(2 * j + 1, part[:, 128:])
    part = nn(left, tail)
    yield
    take(HEADS, part)


def gather_heads(left, right):
    main = []
    for j in range(3):
        part = nn(left[64 * j : 64 * j + 64], right[:, 256 * j : 256 * j + 256])
        main += [part[:32, :128], part[32:, 128:]]
    tail = nn(left, right[:, 768:])
    tails = [tail[:32]] + [pltpu.roll(tail[32 * h : 32 * h + 32], 128 - 16 * h, 1) for h in range(1, HEADS)]
    return jnp.concatenate([jnp.concatenate(main, axis=0), jnp.concatenate(tails, axis=0)[:, :16]], axis=1)


def gather_keys(left, right):
    pairs, tail = left
    main = [nt(pairs[j], right[:, 256 * j : 256 * j + 256]) for j in range(3)]
    return jnp.concatenate(main, axis=0) + nt(tail, right[:, 768:])


def head_sum(x):
    sums = [jnp.sum(x[32 * h : 32 * h + 32], axis=0, keepdims=True) for h in range(HEADS)]
    return jnp.concatenate([jnp.broadcast_to(t, (32, WIN)) for t in sums], axis=0)


def column(row):
    return jnp.broadcast_to(row, (8, row.shape[1])).T[:, :1]


def unpacked(dense, levels, rows):
    n = levels * rows * 6
    rest = jnp.concatenate([dense[n:, :64], dense[n:, 64:]], axis=0)
    return jnp.concatenate([dense[:n], rest], axis=1).reshape(levels, rows, 6, 192)


def places():
    for w in range(6):
        aw, zw = w // 2, w % 2
        for i in range(2):
            level = (2 * zw + i + 1) % 4
            for j in range(6):
                yield w * WIN + (i * 6 + j) * 12, level, aw * 6 + j


def layer_kernel(
    tok_ref,
    cot_ref,
    lon_ref,
    lat_ref,
    diag_ref,
    label_ref,
    wqkv_ref,
    proj_ref,
    gain_ref,
    scale_ref,
    many_hbm,
    few_hbm,
    tail_hbm,
    grads_out,
    sums_out,
    pairs_out,
    lon_wide,
    lat_wide,
    diag_wide,
    x_ref,
    g_ref,
    grads_ref,
    grads_sems,
    wt_ref,
    projt_ref,
    sum_w_ref,
    sum_p_ref,
    sum_g_ref,
    sum_s_ref,
    many_ref,
    few_ref,
    tail_ref,
    bias_sems,
    *slots,
):
    arriving = [
        pltpu.make_async_copy(source, to, bias_sems.at[i])
        for i, (source, to) in enumerate(
            ((many_hbm, many_ref), (few_hbm, few_ref), (tail_hbm, tail_ref))
        )
    ]
    for copy in arriving:
        copy.start()

    for wide_ref, ref in ((lon_wide, lon_ref), (lat_wide, lat_ref), (diag_wide, diag_ref)):
        wide_ref[...] = ref[...].astype(F32)

    def place(ref, n, halfway, to, at):
        to[at : at + 6, :128] = ref[6 * n : 6 * n + 6, :]
        to[at : at + 6, 128:] = spare(ref, n, halfway)

    for base, level, row in places():
        for n, (own, to) in enumerate(((tok_ref, x_ref), (cot_ref, g_ref))):
            if row < 15:
                to[base : base + 6, :] = own[level, row + 3].astype(F32)[6:]
            else:
                place(lat_wide.at[n], level * 3 + row - 15, 6, to, base)
            if row < 15:
                place(lon_wide.at[n], level * 15 + row, 30, to, base + 6)
            else:
                place(diag_wide.at[n], level * 3 + row - 15, 6, to, base + 6)

    width = 192
    for n in range(3):
        wt_ref[width * n : width * n + width, :] = (
            wqkv_ref[:, width * n : width * n + width].astype(F32).T.astype(BF16)
        )
    projt_ref[...] = proj_ref[...].astype(F32).T.astype(BF16)
    for ref in (sum_w_ref, sum_p_ref, sum_g_ref, sum_s_ref):
        ref[...] = jnp.zeros_like(ref)
    gain = column(gain_ref[...])
    temper = jnp.exp(scale_ref[...])
    lanes = lax.broadcasted_iota(jnp.int32, (1, LANES), 1)
    lane_head = jnp.where(lanes < 768, lanes // 128, (lanes - 768) // 16)
    row_head = lax.broadcasted_iota(jnp.int32, (width, 128), 0) // 32
    tail_mask = row_head == lax.broadcasted_iota(jnp.int32, (width, 128), 1) // 16
    temper_row = jnp.zeros((1, LANES), F32)
    temper_col = jnp.zeros((width, 1), F32)
    for h in range(HEADS):
        temper_row = jnp.where(lane_head == h, temper[:, h : h + 1], temper_row)
        temper_col = jnp.where(row_head[:, :1] == h, temper[:, h : h + 1], temper_col)

    def leave(w):
        return pltpu.make_async_copy(grads_ref.at[w], grads_out.at[w], grads_sems.at[w])

    def window(n, slot):
        w = n * TOGETHER + slot
        cosine_ref, probs_ref, half_ref, column_ref = (ref.at[slot] for ref in slots)
        at = pl.ds(pl.multiple_of(w * WIN, 16), WIN)
        x = x_ref[at, :].astype(BF16)
        projected = nt(wt_ref[...], x).astype(BF16).astype(F32)
        yield
        query, key, value = (projected[width * n : width * n + width] for n in range(3))
        query_inv = lax.rsqrt(head_sum(query * query) + 1.0)
        key_inv = lax.rsqrt(head_sum(key * key) + 1.0)
        yield
        key_unit = (key * key_inv).astype(BF16).astype(F32)
        yield
        queries = spread((query * query_inv).astype(BF16).astype(F32), tail_mask)
        label = label_ref[w]
        tail = jnp.concatenate([label[:, 128:]] * 8, axis=1)
        label_col = jnp.concatenate([column(label[:, :128]), column(tail)[:16]], axis=0)
        column_ref[...] = jnp.broadcast_to(label_col, (WIN, 128))

        def soften(t, cosine):
            lane = slice(128 * t, 128 * t + 128)
            cosine_ref[:, lane] = cosine
            if t < MANY:
                bias = many_ref[pl.ds(w * MANY + t, WIN, stride=6 * MANY), :]
            elif t < HEADS:
                bias = few_ref[w * 2 + t - MANY]
            else:
                bias = []
                for n in range(18):
                    part = tail_ref[pl.ds(n * ROWS + w * HEADS, HEADS), :]
                    bias.append(swap_blocks(jnp.concatenate([part, jnp.zeros((2, 128), F32)], axis=0)))
                bias = jnp.concatenate(bias, axis=0)
            scores = cosine * temper_row[:, lane] + bias
            same = column_ref[...] == (label[:, :128] if t < HEADS else tail)
            scores = jnp.where(same, scores, NEG_FILL)
            weights = jnp.exp(scores - jnp.max(scores, axis=0, keepdims=True))
            probs = weights * (1.0 / jnp.sum(weights, axis=0, keepdims=True))
            probs_ref[:, lane] = probs
            half_ref[:, lane] = probs.astype(BF16)

        key_turned = turned(key_unit).astype(BF16)
        yield
        if slot == 0:

            @pl.when(n == 0)
            def _():
                for copy in arriving:
                    copy.wait()

        yield from across(key_turned, queries, soften)
        yield
        probs_half = half_ref[...]
        yield
        mixed = gather_heads(value.astype(BF16), probs_half).astype(BF16)
        yield
        att = nn(projt_ref[...], mixed).astype(BF16).astype(F32)
        yield
        center = att - jnp.sum(att, axis=0, keepdims=True) * (1.0 / width)
        inv_std = lax.rsqrt(jnp.sum(center * center, axis=0, keepdims=True) * (1.0 / width) + 1e-5)
        yield
        normed = center * inv_std
        yield
        grad = g_ref[at, :]
        grad = jnp.concatenate([grad[:128].T, jnp.concatenate([grad[128:], grad[:112]], axis=0).T[:, :16]], axis=1)
        yield
        sum_g_ref[...] += grad * normed
        grad = grad * gain
        yield
        grad_mean = jnp.sum(grad, axis=0, keepdims=True) * (1.0 / width)
        both_mean = jnp.sum(grad * normed, axis=0, keepdims=True) * (1.0 / width)
        grad_att = (inv_std * (grad - grad_mean - normed * both_mean)).astype(BF16)
        yield
        sum_p_ref[...] += nt(mixed, grad_att)
        yield
        grad_mixed = spread(nn(proj_ref[...], grad_att).astype(BF16).astype(F32), tail_mask)
        yield
        grad_value = gather_keys(grad_mixed, probs_half)

        def harden(t, grad_probs):
            lane = slice(128 * t, 128 * t + 128)
            probs = probs_ref[:, lane]
            along = jnp.sum(grad_probs * probs, axis=0, keepdims=True)
            grad_scores = probs * (grad_probs - along)
            sum_s_ref[:, lane] += jnp.sum(grad_scores * cosine_ref[:, lane], axis=0, keepdims=True)
            half_ref[:, lane] = grad_scores.astype(BF16)
            if t < HEADS:
                pairs_out[pl.ds(w * HEADS + t, WIN, stride=ROWS), :] = grad_scores
            else:
                for n in range(18):
                    block = swap_blocks(grad_scores[8 * n : 8 * n + 8])
                    pairs_out[pl.ds((WIN + n) * ROWS + w * HEADS, HEADS), :] = block[:HEADS]

        yield from across(turned(value).astype(BF16), grad_mixed, harden)
        yield
        scores_half = half_ref[...]
        grad_qunit = gather_heads(key_unit.astype(BF16), scores_half) * temper_col
        yield
        grad_kunit = gather_keys(queries, scores_half) * temper_col
        yield
        grad_query = query_inv * grad_qunit - query * (query_inv * query_inv * query_inv) * head_sum(
            query * grad_qunit
        )
        yield
        grad_key = key_inv * grad_kunit - key * (key_inv * key_inv * key_inv) * head_sum(key * grad_kunit)
        yield
        grad_all = jnp.concatenate([grad_query, grad_key, grad_value], axis=0).astype(BF16)
        yield
        sum_w_ref[...] += nn(grad_all, x)
        grads_ref[w] = grad_all
        leave(w).start()

    def group(n, carry):
        going = [window(n, slot) for slot in range(TOGETHER)]
        for slot, one in enumerate(going):
            for _ in range(LEAD * (TOGETHER - 1 - slot)):
                next(one)
        while going:
            going = [one for one in going if next(one, going) is None]
        return carry

    lax.fori_loop(0, 6 // TOGETHER, group, 0)

    grad_q, grad_k, grad_v = (sum_w_ref[width * n : width * n + width, :].T for n in range(3))
    grad_p = sum_p_ref[...]
    gain_sum = jnp.sum(sum_g_ref[...], axis=1, keepdims=True)
    gain_sum = jnp.broadcast_to(gain_sum, (width, 128)).T[:1]
    k_turned = pltpu.roll(jnp.concatenate([grad_k, jnp.zeros((width, 64), F32)], axis=1), 64, 1)
    p_end = pltpu.roll(jnp.concatenate([grad_p[:, 128:], jnp.zeros((width, 64), F32)], axis=1), 64, 1)
    zero = jnp.zeros((width, 64), F32)
    columns = [
        grad_q[:, :128],
        jnp.concatenate([grad_q[:, 128:], zero], axis=1) + jnp.concatenate([zero, k_turned[:, 64:128]], axis=1),
        k_turned[:, 128:256],
        grad_v[:, :128],
        jnp.concatenate([grad_v[:, 128:], zero], axis=1) + p_end,
        grad_p[:, :128],
    ]
    sums_out[...] = jnp.zeros_like(sums_out)
    for c, tiles in enumerate(columns):
        for n in range(24):
            sums_out[n * 6 + c] = tiles[8 * n : 8 * n + 8]
    lane = lax.broadcasted_iota(jnp.int32, (1, 128), 1)
    for w in range(6):
        leave(w).wait()
    scale_sum = sum_s_ref[...] * temper_row
    scale_row = jnp.zeros((1, 128), F32)
    for h in range(HEADS):
        main = jnp.sum(scale_sum[:, 128 * h : 128 * h + 128], axis=1, keepdims=True)
        tail = jnp.where((lane >= 16 * h) & (lane < 16 * h + 16), scale_sum[:, 768:], 0.0)
        total = main + jnp.sum(tail, axis=1, keepdims=True)
        scale_row = scale_row + jnp.where(lane == h, total, 0.0)
    rest = jnp.concatenate(
        [
            gain_sum[:, :128],
            jnp.concatenate([gain_sum[:, 128:], jnp.zeros((1, 64), F32)], axis=1),
            scale_row,
            jnp.zeros((5, 128), F32),
        ],
        axis=0,
    )
    high = rest.astype(BF16).astype(F32)
    sums_out[150] = high
    sums_out[151] = rest - high


def sublayer(*args):
    vmem = pl.BlockSpec(memory_space=pltpu.VMEM)
    tokens_n = 6 * WIN
    return pl.pallas_call(
        layer_kernel,
        out_shape=(
            pltpu.HBM((6, 576, WIN), BF16),
            jax.ShapeDtypeStruct((160, 8, 128), F32),
            jax.ShapeDtypeStruct((TILES * ROWS, 128), F32),
        ),
        in_specs=[vmem] * (len(args) - 3) + [pl.BlockSpec(memory_space=pltpu.HBM)] * 3,
        out_specs=(pl.BlockSpec(memory_space=pltpu.HBM), vmem, vmem),
        scratch_shapes=[pltpu.VMEM((2, 540, 128), F32)]
        + [pltpu.VMEM((2, 108, 128), F32)] * 2
        + [pltpu.VMEM((tokens_n, 192), F32)] * 2
        + [pltpu.VMEM((6, 576, WIN), BF16), pltpu.SemaphoreType.DMA((6,))]
        + [pltpu.VMEM((576, 192), BF16), pltpu.VMEM((192, 192), BF16)]
        + [pltpu.VMEM((576, 192), F32), pltpu.VMEM((192, 192), F32), pltpu.VMEM((192, WIN), F32), pltpu.VMEM((1, LANES), F32)]
        + [pltpu.VMEM((WIN * 6 * MANY, 128), F32), pltpu.VMEM((12, WIN, 128), F32)]
        + [pltpu.VMEM((18 * ROWS, 128), F32), pltpu.SemaphoreType.DMA((3,))]
        + [pltpu.VMEM((TOGETHER, WIN, LANES), F32)] * 2
        + [pltpu.VMEM((TOGETHER, WIN, LANES), BF16), pltpu.VMEM((TOGETHER, WIN, 128), F32)],
        compiler_params=pltpu.CompilerParams(vmem_limit_bytes=20 << 20),
        cost_estimate=pl.CostEstimate(flops=1_500_000_000, bytes_accessed=10_000_000, transcendentals=800_000),
        name="sublayer",
    )(*args)


def return_kernel(
    grads_ref, wqkv_ref, own_out, lon_out, lat_out, diag_out, gwin_ref, lon_ref32, lat_ref32, diag_ref32
):
    for w in range(6):
        gwin_ref[w * WIN : w * WIN + WIN, :] = turned(nn(wqkv_ref[...], grads_ref[w]))
    for base, level, row in places():
        left = gwin_ref[base : base + 6, :]
        right = gwin_ref[base + 6 : base + 12, :]
        if row < 15:
            own_out[level, row] = left.astype(BF16)
            pack(right, level * 15 + row, 30, lon_ref32)
        else:
            pack(left, level * 3 + row - 15, 6, lat_ref32)
            pack(right, level * 3 + row - 15, 6, diag_ref32)
    lon_out[...] = lon_ref32[...].astype(BF16)
    lat_out[...] = lat_ref32[...].astype(BF16)
    diag_out[...] = diag_ref32[...].astype(BF16)


def returns(grads, w_qkv):
    vmem = pl.BlockSpec(memory_space=pltpu.VMEM)
    return pl.pallas_call(
        return_kernel,
        out_shape=(
            jax.ShapeDtypeStruct((4, 15, 6, 192), BF16),
            jax.ShapeDtypeStruct((540, 128), BF16),
            jax.ShapeDtypeStruct((108, 128), BF16),
            jax.ShapeDtypeStruct((108, 128), BF16),
        ),
        in_specs=[vmem] * 2,
        out_specs=(vmem,) * 4,
        scratch_shapes=[pltpu.VMEM((6 * WIN, 192), F32), pltpu.VMEM((540, 128), F32)]
        + [pltpu.VMEM((108, 128), F32)] * 2,
        compiler_params=pltpu.CompilerParams(vmem_limit_bytes=14 << 20),
        cost_estimate=pl.CostEstimate(flops=2_000_000_000, bytes_accessed=3_000_000, transcendentals=0),
        name="returns",
    )(grads, w_qkv)


def entry_kernel(pairs_ref, index_ref, sums_ref, out_ref, acc_ref):
    acc_ref[...] = jnp.zeros_like(acc_ref)
    places = lax.broadcasted_iota(jnp.int32, (256, 128), 0)

    def step(n, carry):
        lefts, rights = [], []
        for t in range(54):
            tile = n * 54 + t
            index = index_ref[pl.ds(tile, 1), :]
            low, high = index & 255, index >> 8
            rights.append(jnp.where(places == low, 1.0, 0.0).astype(BF16))
            pairs = pairs_ref[pl.ds(pl.multiple_of(tile * ROWS, 8), ROWS), :]
            lefts.append(
                jnp.concatenate([jnp.where(high == k, pairs, 0.0) for k in range(HI)], axis=0).astype(BF16)
            )
        acc_ref[...] += nt(jnp.concatenate(lefts, axis=1), jnp.concatenate(rights, axis=1))
        return carry

    lax.fori_loop(0, TILES // 54, step, 0)
    rows = [acc_ref[k * ROWS : k * ROWS + 36, :] for k in range(HI)]
    rows = jnp.concatenate(rows + [jnp.zeros((44, 256), F32)], axis=0)
    for c in range(32):
        tiles = [sums_ref[5 * c + n] for n in range(5)]
        for n in range(2 * c, 2 * c + 2):
            tiles += [rows[8 * n : 8 * n + 8, :128], rows[8 * n : 8 * n + 8, 128:]]
        out_ref[c] = jnp.concatenate(tiles, axis=0).astype(BF16)


def by_entry(pairs, index, sums):
    vmem = pl.BlockSpec(memory_space=pltpu.VMEM)
    return pl.pallas_call(
        entry_kernel,
        out_shape=jax.ShapeDtypeStruct((32, 72, 128), BF16),
        in_specs=[vmem] * 3,
        out_specs=vmem,
        scratch_shapes=[pltpu.VMEM((HI * ROWS, 256), F32)],
        compiler_params=pltpu.CompilerParams(vmem_limit_bytes=20 << 20),
        cost_estimate=pl.CostEstimate(flops=5_000_000_000, bytes_accessed=4_000_000, transcendentals=0),
        name="by_entry",
    )(pairs, index, sums)


def unpack_kernel(got_ref, qkv_out, proj_out, bias_out, gain_out, scale_out, flat_ref):
    def tile(n, slots, at):
        return got_ref[n // slots, at + n % slots].astype(F32)

    for n in range(24):
        rows = pl.ds(8 * n, 8)
        for c in range(4):
            qkv_out[rows, 128 * c : 128 * c + 128] = tile(n * 6 + c, 5, 0)
        mid = tile(n * 6 + 4, 5, 0)
        qkv_out[rows, 512:576] = mid[:, :64]
        proj_out[rows, :128] = tile(n * 6 + 5, 5, 0)
        proj_out[rows, 128:192] = pltpu.roll(mid, 64, 1)[:, :64]
    for n in range(59):
        flat_ref[8 * n : 8 * n + 8, :] = tile(2 * n, 4, 5)
        flat_ref[472 + 8 * n : 480 + 8 * n, :] = tile(2 * n + 1, 4, 5)
    for k in range(2 * HI):
        size = min(128, 3312 - 128 * k)
        for aw in range(3):
            for h in range(HEADS):
                part = flat_ref[pl.ds(472 * (k % 2) + 36 * (k // 2) + 12 * aw + h, 2, stride=HEADS), :]
                bias_out[aw, h, :, 128 * k : 128 * k + size] = part[:, :size]
    rest = tile(150, 5, 0) + tile(151, 5, 0)
    gain_out[:, :128] = rest[0:1]
    gain_out[:, 128:192] = rest[1:2, :64]
    scale_out[...] = rest[2:3, :HEADS]


def unpack(got):
    vmem = pl.BlockSpec(memory_space=pltpu.VMEM)
    return pl.pallas_call(
        unpack_kernel,
        out_shape=(
            jax.ShapeDtypeStruct((192, 576), F32),
            jax.ShapeDtypeStruct((192, 192), F32),
            jax.ShapeDtypeStruct((3, HEADS, 2, 3312), F32),
            jax.ShapeDtypeStruct((1, 192), F32),
            jax.ShapeDtypeStruct((1, HEADS), F32),
        ),
        in_specs=[vmem],
        out_specs=(vmem,) * 5,
        scratch_shapes=[pltpu.VMEM((944, 128), F32)],
        compiler_params=pltpu.CompilerParams(vmem_limit_bytes=20 << 20),
        name="unpack",
    )(got)


def moved(value, lon_by, lat_by):
    lon_n, lat_n = 64, 4
    pairs = []
    for lon in range(lon_n):
        for lat in range(lat_n):
            to = (lon + lon_by) % lon_n * lat_n + (lat + lat_by) % lat_n
            pairs.append((lon * lat_n + lat, to))
    return lax.ppermute(value, AXES, pairs)


def half(x):
    return lax.reduce_precision(x, 8, 7)


def sum_everywhere(parts, leaving):
    parts = lax.all_to_all(parts, LAYER, 0, 0, tiled=True).astype(F32)
    mine = lax.axis_index(LAYER) == 30

    def rounded(x):
        both = x[:8] + x[8:16]
        high = half(both)
        split = jnp.concatenate([high, both - high, x[16:]], axis=0)
        return jnp.where(mine, split, x).astype(BF16)

    weights = jnp.sum(parts[:, :40], 0)
    bands = jnp.sum(parts[:, 40:].reshape(8, 4, 32, 128), 0).reshape(128, 128)
    layer = jnp.concatenate([rounded(weights), bands.astype(BF16)], axis=0)
    layer, leaving = lax.optimization_barrier((layer, leaving))
    layers = lax.all_to_all(jnp.broadcast_to(layer, (8, 168, 128)), "z", 0, 0, tiled=True)
    lon_out, lat_out, diag_out = leaving
    arrived = (moved(lon_out, 1, 0), moved(lat_out, 0, 1), moved(diag_out, 1, 1))
    layers, arrived = lax.optimization_barrier((layers, arrived))
    total = jnp.sum(layers.astype(F32), 0)
    weights = jnp.broadcast_to(rounded(total[:40]), (8, 4, 40, 128))
    bands = jnp.broadcast_to(total[40:].astype(BF16).reshape(4, 32, 128), (8, 4, 32, 128))
    parts = jnp.concatenate([weights, bands], axis=2).reshape(32, 72, 128)
    return lax.all_to_all(parts, LAYER, 0, 0, tiled=True), arrived


def on_device(tokens, cotangent, labels, w_qkv, w_proj, logit_scale, bias_table, bias_index, norm_gain):
    lon_in, lat_in, diag_in = leaving(tokens, cotangent)
    lat_in = moved(lat_in, 0, -1)
    lon_in = moved(lon_in, -1, 0)
    diag_in = moved(diag_in, -1, -1)

    *bias, index = pair_bias(bias_table.transpose(0, 2, 1, 3), bias_index)

    label_win = labels.reshape(2, 2, 3, 6, 12).transpose(2, 0, 1, 3, 4).reshape(6, 1, WIN).astype(F32)

    grads, sums, pairs = sublayer(
        tokens,
        cotangent,
        lon_in,
        lat_in,
        diag_in,
        label_win,
        w_qkv,
        w_proj,
        norm_gain[None],
        logit_scale[None],
        *(pltpu.with_memory_space_constraint(part, pltpu.HBM) for part in bias),
    )
    parts = by_entry(pairs, index, sums)
    own, *back = returns(grads, w_qkv)
    got, (lon_back, lat_back, diag_back) = sum_everywhere(parts, tuple(back))
    grad_qkv, grad_proj, grad_bias, grad_gain, grad_scale = unpack(got.reshape(32, 9, 8, 128))
    lon_back, lat_back, diag_back = unpacked(lon_back, 4, 15), unpacked(lat_back, 4, 3), unpacked(diag_back, 4, 3)
    returned = jnp.concatenate(
        [jnp.concatenate([diag_back, lat_back], axis=2), jnp.concatenate([lon_back, own], axis=2)], axis=1
    )
    grad_tokens = (cotangent.astype(F32) + returned.astype(F32)).astype(BF16)
    return (
        grad_tokens,
        grad_qkv,
        grad_proj,
        grad_scale[0],
        grad_bias.transpose(0, 2, 1, 3),
        grad_gain[0],
    )


def solution(mesh):
    fine = Mesh(mesh.devices.reshape(8, 4, 2, 2, 2), AXES)
    lon, lat = ("z", "y", "xl"), ("xh", "core")
    placed = (
        P(None, lat, lon, None),
        P(None, lat, lon, None),
        P(None, lat, lon),
        P(),
        P(),
        P(),
        P(lat, None, None, None),
        P(),
        P(),
    )
    return jax.shard_map(
        on_device,
        mesh=fine,
        in_specs=placed,
        out_specs=(P(None, lat, lon, None), P(), P(), P(), P(lat, None, None, None), P()),
        check_vma=False,
    )
```

```python
import jax
import jax.numpy as jnp
from jax import lax
from jax.experimental import pallas as pl
from jax.experimental.pallas import tpu as pltpu
from jax.sharding import Mesh
from jax.sharding import PartitionSpec as P


F32 = jnp.float32
BF16 = jnp.bfloat16
NEG_FILL = -1e30
HEADS = 6
WIN = 144
LANES = 896
CHUNKS = 26
HI = 13
ROWS = 40
LEAD = 2
TOGETHER = 3
MANY = 4
TILES = 162
AXES = ("z", "y", "xl", "xh", "core")
LAYER = ("y", "xl", "xh", "core")


def nt(left, right):
    return lax.dot_general(left, right, (((1,), (1,)), ((), ())), preferred_element_type=F32)


def tn(left, right):
    return lax.dot_general(left, right, (((0,), (0,)), ((), ())), preferred_element_type=F32)


def nn(left, right):
    return jnp.dot(left, right, preferred_element_type=F32)


def swap_blocks(x):
    sub = lax.broadcasted_iota(jnp.int32, x.shape, 0)
    block = lax.broadcasted_iota(jnp.int32, x.shape, 1) // 16
    for bit in (1, 2, 4):
        s_set = (sub & bit) != 0
        l_set = (block & bit) != 0
        up = pltpu.roll(pltpu.roll(x, bit, 0), 128 - 16 * bit, 1)
        down = pltpu.roll(pltpu.roll(x, 8 - bit, 0), 16 * bit, 1)
        x = jnp.where(s_set == l_set, x, jnp.where(s_set, up, down))
    return x


def bias_kernel(table_ref, given_ref, many_out, few_out, tail_out, index_ref, rows_ref, left_ref, *rest):
    given = given_ref[...].astype(F32)
    rest_q = jnp.concatenate([given[:, 128:], jnp.zeros((WIN, 112), F32)], axis=1)
    index_ref[:128, :] = given[:128, :128].T.astype(jnp.int32)
    index_ref[128:WIN, :] = rest_q[:128].T[:16].astype(jnp.int32)
    ends = jnp.concatenate([given[128:], jnp.zeros((112, WIN), F32)], axis=0)
    ends = jnp.concatenate(
        [ends[:, :128].T, jnp.concatenate([ends[:, 128:], jnp.zeros((128, 112), F32)], axis=1).T[:16]], axis=0
    )
    for by in (16, 32, 64):
        ends = ends + pltpu.roll(ends, by, 1)
    sub = lax.broadcasted_iota(jnp.int32, (WIN, 128), 0) % 8
    block = lax.broadcasted_iota(jnp.int32, (WIN, 128), 1) // 16
    ends = jnp.where(sub == block, ends, 0.0)
    for n in range(18):
        row = jnp.sum(ends[8 * n : 8 * n + 8], axis=0, keepdims=True)
        index_ref[WIN + n : WIN + n + 1, :] = row.astype(jnp.int32)
    blocks, sems = rest[:3], rest[3]
    entries = table_ref.shape[3]
    rows_ref[...] = jnp.zeros_like(rows_ref)
    for aw in range(3):
        for h in range(HEADS):
            for zw in range(2):
                row = (aw * 2 + zw) * HEADS + h
                rows_ref[row : row + 1, :entries] = table_ref[aw, h, zw : zw + 1, :]
    for k in range(HI):
        part = rows_ref[:, 256 * k : 256 * k + 256]
        high = part.astype(BF16).astype(F32)
        left_ref[0, k * ROWS : k * ROWS + ROWS, :] = high
        left_ref[1, k * ROWS : k * ROWS + ROWS, :] = part - high
    left = jnp.concatenate([left_ref[0], left_ref[1]], axis=0).astype(BF16)
    fewer = [
        left_ref[term, k * ROWS + HEADS * w : k * ROWS + HEADS * w + MANY, :]
        for term in range(2)
        for k in range(HI)
        for w in range(6)
    ]
    fewer = jnp.concatenate(fewer, axis=0).astype(BF16)
    places = lax.broadcasted_iota(jnp.int32, (256, 128), 0)

    def two(at, rows, left, block_ref, slot, to):
        index = [index_ref[pl.ds(at + t, 1), :] for t in range(2)]
        picks = jnp.concatenate(
            [jnp.where(places == (i & 255), 1.0, 0.0).astype(BF16) for i in index], axis=1
        )
        got = nn(left, picks)
        for t in range(2):
            high = index[t] >> 8
            lane = slice(128 * t, 128 * t + 128)
            total = None
            for k in range(HI):
                value = got[k * rows : k * rows + rows, lane] + got[(HI + k) * rows : (HI + k + 1) * rows, lane]
                total = value if total is None else jnp.where(high == k, value, total)
            block_ref[slot, (to + t) * rows : (to + t) * rows + rows, :] = total

    def pick(row, index):
        low = index & 127
        got = []
        for c in range(CHUNKS):
            source = jnp.broadcast_to(rows_ref[row : row + 1, c * 128 : c * 128 + 128], (8, 128))
            got.append(jnp.take_along_axis(source, low, axis=1, mode="promise_in_bounds"))
        bit = 128
        while len(got) > 1:
            odd = (index & bit) != 0
            got = [
                jnp.where(odd, got[i + 1], got[i]) if i + 1 < len(got) else got[i]
                for i in range(0, len(got), 2)
            ]
            bit *= 2
        return got[0]

    def leave(n):
        slot = n % 2
        outs = (
            many_out.at[pl.ds(pl.multiple_of(n * 48 * 6 * MANY, 8), 48 * 6 * MANY), :],
            few_out.at[:, pl.ds(pl.multiple_of(n * 48, 8), 48), :],
            tail_out.at[pl.ds(pl.multiple_of(n * 6 * ROWS, 8), 6 * ROWS), :],
        )
        return [
            pltpu.make_async_copy(block.at[slot], out, sems.at[slot, i])
            for i, (block, out) in enumerate(zip(blocks, outs))
        ]

    def step(n, carry):
        @pl.when(n >= 2)
        def _():
            for copy in leave(n - 2):
                copy.wait()

        slot = n % 2
        for u in range(24):
            two(n * 48 + 2 * u, 6 * MANY, fewer, blocks[0], slot, 2 * u)
            for v in range(3 * u, 3 * u + 3):
                w, h, b = v // 12, MANY + v // 6 % 2, v % 6
                index = index_ref[pl.ds(pl.multiple_of(n * 48 + 8 * b, 8), 8), :]
                blocks[1][slot, w * 2 + h - MANY, 8 * b : 8 * b + 8, :] = pick(w * HEADS + h, index)
        for u in range(3):
            two(WIN + n * 6 + 2 * u, ROWS, left, blocks[2], slot, 2 * u)
        for copy in leave(n):
            copy.start()
        return carry

    lax.fori_loop(0, 3, step, 0)
    for n in (1, 2):
        for copy in leave(n):
            copy.wait()


def pair_bias(table, index):
    return pl.pallas_call(
        bias_kernel,
        out_shape=(
            pltpu.HBM((WIN * 6 * MANY, 128), F32),
            pltpu.HBM((12, WIN, 128), F32),
            pltpu.HBM((18 * ROWS, 128), F32),
            jax.ShapeDtypeStruct((TILES, 128), jnp.int32),
        ),
        in_specs=[pl.BlockSpec(memory_space=pltpu.VMEM)] * 2,
        out_specs=(pl.BlockSpec(memory_space=pltpu.HBM),) * 3 + (pl.BlockSpec(memory_space=pltpu.VMEM),),
        scratch_shapes=[
            pltpu.VMEM((ROWS, HI * 256), F32),
            pltpu.VMEM((2, HI * ROWS, 256), F32),
            pltpu.VMEM((2, 48 * 6 * MANY, 128), F32),
            pltpu.VMEM((2, 12, 48, 128), F32),
            pltpu.VMEM((2, 6 * ROWS, 128), F32),
            pltpu.SemaphoreType.DMA((2, 3)),
        ],
        compiler_params=pltpu.CompilerParams(vmem_limit_bytes=20 << 20),
        cost_estimate=pl.CostEstimate(flops=10_000_000_000, bytes_accessed=4_000_000, transcendentals=0),
        name="pair_bias",
    )(table, index)


def pack(x, n, halfway, ref):
    ref[6 * n : 6 * n + 6, :] = x[:, :128]
    rest = x[:, 128:]
    at = 12 * halfway + 6 * (n % halfway)
    if n < halfway:
        ref[at : at + 6, :64] = rest
    else:
        ref[at : at + 6, 64:] = rest


def spare(ref, n, halfway):
    at = 12 * halfway + 6 * (n % halfway)
    return ref[at : at + 6, :64] if n < halfway else ref[at : at + 6, 64:]


def leaving_kernel(tok_ref, cot_ref, lon_out, lat_out, diag_out, lon_ref, lat_ref, diag_ref):
    for n, ref in enumerate((tok_ref, cot_ref)):
        for level in range(4):
            for row in range(18):
                x = ref[level, row].astype(F32)
                if row < 3:
                    pack(x[:6], level * 3 + row, 6, diag_ref)
                    pack(x[6:], level * 3 + row, 6, lat_ref)
                else:
                    pack(x[:6], level * 15 + row - 3, 30, lon_ref)
        lon_out[n] = lon_ref[...].astype(BF16)
        lat_out[n] = lat_ref[...].astype(BF16)
        diag_out[n] = diag_ref[...].astype(BF16)


def leaving(tokens, cotangent):
    vmem = pl.BlockSpec(memory_space=pltpu.VMEM)
    shapes = ((540, 128), (108, 128), (108, 128))
    return pl.pallas_call(
        leaving_kernel,
        out_shape=tuple(jax.ShapeDtypeStruct((2,) + shape, BF16) for shape in shapes),
        in_specs=[vmem] * 2,
        out_specs=(vmem,) * 3,
        scratch_shapes=[pltpu.VMEM(shape, F32) for shape in shapes],
        compiler_params=pltpu.CompilerParams(vmem_limit_bytes=14 << 20),
        name="leaving",
    )(tokens, cotangent)


def wide(x):
    return x[:, :128], jnp.concatenate([x[:, 128:WIN], jnp.zeros((x.shape[0], 112), x.dtype)], axis=1)


def turned(x):
    main, tail = wide(x)
    return jnp.concatenate([main.T, tail.T[:16]], axis=0)


def spread(xt, tail_mask):
    main, tail = wide(xt)
    for by in (16, 32, 64):
        tail = tail + pltpu.roll(tail, by, 1)
    tail = jnp.where(tail_mask, tail, 0.0).astype(BF16)
    main = main.astype(BF16)
    zero = jnp.zeros((32, 128), BF16)
    pairs = []
    for j in range(3):
        top = jnp.concatenate([main[64 * j : 64 * j + 32], zero], axis=1)
        low = jnp.concatenate([zero, main[64 * j + 32 : 64 * j + 64]], axis=1)
        pairs.append(jnp.concatenate([top, low], axis=0))
    return pairs, tail


def across(left, right, take):
    pairs, tail = right
    for j in range(3):
        part = nn(left[:, 64 * j : 64 * j + 64], pairs[j])
        yield
        take(2 * j, part[:, :128])
        yield
        take(2 * j + 1, part[:, 128:])
    part = nn(left, tail)
    yield
    take(HEADS, part)


def gather_heads(left, right):
    main = []
    for j in range(3):
        part = nn(left[64 * j : 64 * j + 64], right[:, 256 * j : 256 * j + 256])
        main += [part[:32, :128], part[32:, 128:]]
    tail = nn(left, right[:, 768:])
    tails = [tail[:32]] + [pltpu.roll(tail[32 * h : 32 * h + 32], 128 - 16 * h, 1) for h in range(1, HEADS)]
    return jnp.concatenate([jnp.concatenate(main, axis=0), jnp.concatenate(tails, axis=0)[:, :16]], axis=1)


def gather_keys(left, right):
    pairs, tail = left
    main = [nt(pairs[j], right[:, 256 * j : 256 * j + 256]) for j in range(3)]
    return jnp.concatenate(main, axis=0) + nt(tail, right[:, 768:])


def head_sum(x):
    sums = [jnp.sum(x[32 * h : 32 * h + 32], axis=0, keepdims=True) for h in range(HEADS)]
    return jnp.concatenate([jnp.broadcast_to(t, (32, WIN)) for t in sums], axis=0)


def column(row):
    return jnp.broadcast_to(row, (8, row.shape[1])).T[:, :1]


def unpacked(dense, levels, rows):
    n = levels * rows * 6
    rest = jnp.concatenate([dense[n:, :64], dense[n:, 64:]], axis=0)
    return jnp.concatenate([dense[:n], rest], axis=1).reshape(levels, rows, 6, 192)


def places():
    for w in range(6):
        aw, zw = w // 2, w % 2
        for i in range(2):
            level = (2 * zw + i + 1) % 4
            for j in range(6):
                yield w * WIN + (i * 6 + j) * 12, level, aw * 6 + j


def layer_kernel(
    tok_ref,
    cot_ref,
    lon_ref,
    lat_ref,
    diag_ref,
    label_ref,
    wqkv_ref,
    proj_ref,
    gain_ref,
    scale_ref,
    many_hbm,
    few_hbm,
    tail_hbm,
    grads_out,
    sums_out,
    pairs_out,
    lon_wide,
    lat_wide,
    diag_wide,
    x_ref,
    g_ref,
    grads_ref,
    grads_sems,
    wt_ref,
    projt_ref,
    sum_w_ref,
    sum_p_ref,
    sum_g_ref,
    sum_s_ref,
    many_ref,
    few_ref,
    tail_ref,
    bias_sems,
    *slots,
):
    arriving = [
        pltpu.make_async_copy(source, to, bias_sems.at[i])
        for i, (source, to) in enumerate(
            ((many_hbm, many_ref), (few_hbm, few_ref), (tail_hbm, tail_ref))
        )
    ]
    for copy in arriving:
        copy.start()

    for wide_ref, ref in ((lon_wide, lon_ref), (lat_wide, lat_ref), (diag_wide, diag_ref)):
        wide_ref[...] = ref[...].astype(F32)

    def place(ref, n, halfway, to, at):
        to[at : at + 6, :128] = ref[6 * n : 6 * n + 6, :]
        to[at : at + 6, 128:] = spare(ref, n, halfway)

    for base, level, row in places():
        for n, (own, to) in enumerate(((tok_ref, x_ref), (cot_ref, g_ref))):
            if row < 15:
                to[base : base + 6, :] = own[level, row + 3].astype(F32)[6:]
            else:
                place(lat_wide.at[n], level * 3 + row - 15, 6, to, base)
            if row < 15:
                place(lon_wide.at[n], level * 15 + row, 30, to, base + 6)
            else:
                place(diag_wide.at[n], level * 3 + row - 15, 6, to, base + 6)

    width = 192
    for n in range(3):
        wt_ref[width * n : width * n + width, :] = (
            wqkv_ref[:, width * n : width * n + width].astype(F32).T.astype(BF16)
        )
    projt_ref[...] = proj_ref[...].astype(F32).T.astype(BF16)
    for ref in (sum_w_ref, sum_p_ref, sum_g_ref, sum_s_ref):
        ref[...] = jnp.zeros_like(ref)
    gain = column(gain_ref[...])
    temper = jnp.exp(scale_ref[...])
    lanes = lax.broadcasted_iota(jnp.int32, (1, LANES), 1)
    lane_head = jnp.where(lanes < 768, lanes // 128, (lanes - 768) // 16)
    row_head = lax.broadcasted_iota(jnp.int32, (width, 128), 0) // 32
    tail_mask = row_head == lax.broadcasted_iota(jnp.int32, (width, 128), 1) // 16
    temper_row = jnp.zeros((1, LANES), F32)
    temper_col = jnp.zeros((width, 1), F32)
    for h in range(HEADS):
        temper_row = jnp.where(lane_head == h, temper[:, h : h + 1], temper_row)
        temper_col = jnp.where(row_head[:, :1] == h, temper[:, h : h + 1], temper_col)

    def leave(w):
        return pltpu.make_async_copy(grads_ref.at[w], grads_out.at[w], grads_sems.at[w])

    def window(n, slot):
        w = n * TOGETHER + slot
        cosine_ref, probs_ref, half_ref, column_ref = (ref.at[slot] for ref in slots)
        at = pl.ds(pl.multiple_of(w * WIN, 16), WIN)
        x = x_ref[at, :].astype(BF16)
        projected = nt(wt_ref[...], x).astype(BF16).astype(F32)
        yield
        query, key, value = (projected[width * n : width * n + width] for n in range(3))
        query_inv = lax.rsqrt(head_sum(query * query) + 1.0)
        key_inv = lax.rsqrt(head_sum(key * key) + 1.0)
        yield
        key_unit = (key * key_inv).astype(BF16).astype(F32)
        yield
        queries = spread((query * query_inv).astype(BF16).astype(F32), tail_mask)
        label = label_ref[w]
        tail = jnp.concatenate([label[:, 128:]] * 8, axis=1)
        label_col = jnp.concatenate([column(label[:, :128]), column(tail)[:16]], axis=0)
        column_ref[...] = jnp.broadcast_to(label_col, (WIN, 128))

        def soften(t, cosine):
            lane = slice(128 * t, 128 * t + 128)
            cosine_ref[:, lane] = cosine
            if t < MANY:
                bias = many_ref[pl.ds(w * MANY + t, WIN, stride=6 * MANY), :]
            elif t < HEADS:
                bias = few_ref[w * 2 + t - MANY]
            else:
                bias = []
                for n in range(18):
                    part = tail_ref[pl.ds(n * ROWS + w * HEADS, HEADS), :]
                    bias.append(swap_blocks(jnp.concatenate([part, jnp.zeros((2, 128), F32)], axis=0)))
                bias = jnp.concatenate(bias, axis=0)
            scores = cosine * temper_row[:, lane] + bias
            same = column_ref[...] == (label[:, :128] if t < HEADS else tail)
            scores = jnp.where(same, scores, NEG_FILL)
            weights = jnp.exp(scores - jnp.max(scores, axis=0, keepdims=True))
            probs = weights * (1.0 / jnp.sum(weights, axis=0, keepdims=True))
            probs_ref[:, lane] = probs
            half_ref[:, lane] = probs.astype(BF16)

        key_turned = turned(key_unit).astype(BF16)
        yield
        if slot == 0:

            @pl.when(n == 0)
            def _():
                for copy in arriving:
                    copy.wait()

        yield from across(key_turned, queries, soften)
        yield
        probs_half = half_ref[...]
        yield
        mixed = gather_heads(value.astype(BF16), probs_half).astype(BF16)
        yield
        att = nn(projt_ref[...], mixed).astype(BF16).astype(F32)
        yield
        center = att - jnp.sum(att, axis=0, keepdims=True) * (1.0 / width)
        inv_std = lax.rsqrt(jnp.sum(center * center, axis=0, keepdims=True) * (1.0 / width) + 1e-5)
        yield
        normed = center * inv_std
        yield
        grad = g_ref[at, :]
        grad = jnp.concatenate([grad[:128].T, jnp.concatenate([grad[128:], grad[:112]], axis=0).T[:, :16]], axis=1)
        yield
        sum_g_ref[...] += grad * normed
        grad = grad * gain
        yield
        grad_mean = jnp.sum(grad, axis=0, keepdims=True) * (1.0 / width)
        both_mean = jnp.sum(grad * normed, axis=0, keepdims=True) * (1.0 / width)
        grad_att = (inv_std * (grad - grad_mean - normed * both_mean)).astype(BF16)
        yield
        sum_p_ref[...] += nt(mixed, grad_att)
        yield
        grad_mixed = spread(nn(proj_ref[...], grad_att).astype(BF16).astype(F32), tail_mask)
        yield
        grad_value = gather_keys(grad_mixed, probs_half)

        def harden(t, grad_probs):
            lane = slice(128 * t, 128 * t + 128)
            probs = probs_ref[:, lane]
            along = jnp.sum(grad_probs * probs, axis=0, keepdims=True)
            grad_scores = probs * (grad_probs - along)
            sum_s_ref[:, lane] += jnp.sum(grad_scores * cosine_ref[:, lane], axis=0, keepdims=True)
            half_ref[:, lane] = grad_scores.astype(BF16)
            if t < HEADS:
                pairs_out[pl.ds(w * HEADS + t, WIN, stride=ROWS), :] = grad_scores
            else:
                for n in range(18):
                    block = swap_blocks(grad_scores[8 * n : 8 * n + 8])
                    pairs_out[pl.ds((WIN + n) * ROWS + w * HEADS, HEADS), :] = block[:HEADS]

        yield from across(turned(value).astype(BF16), grad_mixed, harden)
        yield
        scores_half = half_ref[...]
        grad_qunit = gather_heads(key_unit.astype(BF16), scores_half) * temper_col
        yield
        grad_kunit = gather_keys(queries, scores_half) * temper_col
        yield
        grad_query = query_inv * grad_qunit - query * (query_inv * query_inv * query_inv) * head_sum(
            query * grad_qunit
        )
        yield
        grad_key = key_inv * grad_kunit - key * (key_inv * key_inv * key_inv) * head_sum(key * grad_kunit)
        yield
        grad_all = jnp.concatenate([grad_query, grad_key, grad_value], axis=0).astype(BF16)
        yield
        sum_w_ref[...] += nn(grad_all, x)
        grads_ref[w] = grad_all
        leave(w).start()

    def group(n, carry):
        going = [window(n, slot) for slot in range(TOGETHER)]
        for slot, one in enumerate(going):
            for _ in range(LEAD * (TOGETHER - 1 - slot)):
                next(one)
        while going:
            going = [one for one in going if next(one, going) is None]
        return carry

    lax.fori_loop(0, 6 // TOGETHER, group, 0)

    grad_q, grad_k, grad_v = (sum_w_ref[width * n : width * n + width, :].T for n in range(3))
    grad_p = sum_p_ref[...]
    gain_sum = jnp.sum(sum_g_ref[...], axis=1, keepdims=True)
    gain_sum = jnp.broadcast_to(gain_sum, (width, 128)).T[:1]
    k_turned = pltpu.roll(jnp.concatenate([grad_k, jnp.zeros((width, 64), F32)], axis=1), 64, 1)
    p_end = pltpu.roll(jnp.concatenate([grad_p[:, 128:], jnp.zeros((width, 64), F32)], axis=1), 64, 1)
    zero = jnp.zeros((width, 64), F32)
    columns = [
        grad_q[:, :128],
        jnp.concatenate([grad_q[:, 128:], zero], axis=1) + jnp.concatenate([zero, k_turned[:, 64:128]], axis=1),
        k_turned[:, 128:256],
        grad_v[:, :128],
        jnp.concatenate([grad_v[:, 128:], zero], axis=1) + p_end,
        grad_p[:, :128],
    ]
    sums_out[...] = jnp.zeros_like(sums_out)
    for c, tiles in enumerate(columns):
        for n in range(24):
            sums_out[n * 6 + c] = tiles[8 * n : 8 * n + 8]
    lane = lax.broadcasted_iota(jnp.int32, (1, 128), 1)
    for w in range(6):
        leave(w).wait()
    scale_sum = sum_s_ref[...] * temper_row
    scale_row = jnp.zeros((1, 128), F32)
    for h in range(HEADS):
        main = jnp.sum(scale_sum[:, 128 * h : 128 * h + 128], axis=1, keepdims=True)
        tail = jnp.where((lane >= 16 * h) & (lane < 16 * h + 16), scale_sum[:, 768:], 0.0)
        total = main + jnp.sum(tail, axis=1, keepdims=True)
        scale_row = scale_row + jnp.where(lane == h, total, 0.0)
    rest = jnp.concatenate(
        [
            gain_sum[:, :128],
            jnp.concatenate([gain_sum[:, 128:], jnp.zeros((1, 64), F32)], axis=1),
            scale_row,
            jnp.zeros((5, 128), F32),
        ],
        axis=0,
    )
    high = rest.astype(BF16).astype(F32)
    sums_out[150] = high
    sums_out[151] = rest - high


def sublayer(*args):
    vmem = pl.BlockSpec(memory_space=pltpu.VMEM)
    tokens_n = 6 * WIN
    return pl.pallas_call(
        layer_kernel,
        out_shape=(
            pltpu.HBM((6, 576, WIN), BF16),
            jax.ShapeDtypeStruct((160, 8, 128), F32),
            jax.ShapeDtypeStruct((TILES * ROWS, 128), F32),
        ),
        in_specs=[vmem] * (len(args) - 3) + [pl.BlockSpec(memory_space=pltpu.HBM)] * 3,
        out_specs=(pl.BlockSpec(memory_space=pltpu.HBM), vmem, vmem),
        scratch_shapes=[pltpu.VMEM((2, 540, 128), F32)]
        + [pltpu.VMEM((2, 108, 128), F32)] * 2
        + [pltpu.VMEM((tokens_n, 192), F32)] * 2
        + [pltpu.VMEM((6, 576, WIN), BF16), pltpu.SemaphoreType.DMA((6,))]
        + [pltpu.VMEM((576, 192), BF16), pltpu.VMEM((192, 192), BF16)]
        + [pltpu.VMEM((576, 192), F32), pltpu.VMEM((192, 192), F32), pltpu.VMEM((192, WIN), F32), pltpu.VMEM((1, LANES), F32)]
        + [pltpu.VMEM((WIN * 6 * MANY, 128), F32), pltpu.VMEM((12, WIN, 128), F32)]
        + [pltpu.VMEM((18 * ROWS, 128), F32), pltpu.SemaphoreType.DMA((3,))]
        + [pltpu.VMEM((TOGETHER, WIN, LANES), F32)] * 2
        + [pltpu.VMEM((TOGETHER, WIN, LANES), BF16), pltpu.VMEM((TOGETHER, WIN, 128), F32)],
        compiler_params=pltpu.CompilerParams(vmem_limit_bytes=20 << 20),
        cost_estimate=pl.CostEstimate(flops=1_500_000_000, bytes_accessed=10_000_000, transcendentals=800_000),
        name="sublayer",
    )(*args)


def return_kernel(
    grads_ref, wqkv_ref, own_out, lon_out, lat_out, diag_out, gwin_ref, lon_ref32, lat_ref32, diag_ref32
):
    for w in range(6):
        gwin_ref[w * WIN : w * WIN + WIN, :] = turned(nn(wqkv_ref[...], grads_ref[w]))
    for base, level, row in places():
        left = gwin_ref[base : base + 6, :]
        right = gwin_ref[base + 6 : base + 12, :]
        if row < 15:
            own_out[level, row] = left.astype(BF16)
            pack(right, level * 15 + row, 30, lon_ref32)
        else:
            pack(left, level * 3 + row - 15, 6, lat_ref32)
            pack(right, level * 3 + row - 15, 6, diag_ref32)
    lon_out[...] = lon_ref32[...].astype(BF16)
    lat_out[...] = lat_ref32[...].astype(BF16)
    diag_out[...] = diag_ref32[...].astype(BF16)


def returns(grads, w_qkv):
    vmem = pl.BlockSpec(memory_space=pltpu.VMEM)
    return pl.pallas_call(
        return_kernel,
        out_shape=(
            jax.ShapeDtypeStruct((4, 15, 6, 192), BF16),
            jax.ShapeDtypeStruct((540, 128), BF16),
            jax.ShapeDtypeStruct((108, 128), BF16),
            jax.ShapeDtypeStruct((108, 128), BF16),
        ),
        in_specs=[vmem] * 2,
        out_specs=(vmem,) * 4,
        scratch_shapes=[pltpu.VMEM((6 * WIN, 192), F32), pltpu.VMEM((540, 128), F32)]
        + [pltpu.VMEM((108, 128), F32)] * 2,
        compiler_params=pltpu.CompilerParams(vmem_limit_bytes=14 << 20),
        cost_estimate=pl.CostEstimate(flops=2_000_000_000, bytes_accessed=3_000_000, transcendentals=0),
        name="returns",
    )(grads, w_qkv)


def entry_kernel(pairs_ref, index_ref, sums_ref, out_ref, acc_ref):
    acc_ref[...] = jnp.zeros_like(acc_ref)
    places = lax.broadcasted_iota(jnp.int32, (256, 128), 0)

    def step(n, carry):
        lefts, rights = [], []
        for t in range(81):
            tile = n * 81 + t
            index = index_ref[pl.ds(tile, 1), :]
            low, high = index & 255, index >> 8
            rights.append(jnp.where(places == low, 1.0, 0.0).astype(BF16))
            pairs = pairs_ref[pl.ds(pl.multiple_of(tile * ROWS, 8), ROWS), :]
            lefts.append(
                jnp.concatenate([jnp.where(high == k, pairs, 0.0) for k in range(HI)], axis=0).astype(BF16)
            )
        acc_ref[...] += nt(jnp.concatenate(lefts, axis=1), jnp.concatenate(rights, axis=1))
        return carry

    lax.fori_loop(0, TILES // 81, step, 0)
    rows = [acc_ref[k * ROWS : k * ROWS + 36, :] for k in range(HI)]
    rows = jnp.concatenate(rows + [jnp.zeros((44, 256), F32)], axis=0)
    for c in range(32):
        tiles = [sums_ref[5 * c + n] for n in range(5)]
        for n in range(2 * c, 2 * c + 2):
            tiles += [rows[8 * n : 8 * n + 8, :128], rows[8 * n : 8 * n + 8, 128:]]
        out_ref[c] = jnp.concatenate(tiles, axis=0).astype(BF16)


def by_entry(pairs, index, sums):
    vmem = pl.BlockSpec(memory_space=pltpu.VMEM)
    return pl.pallas_call(
        entry_kernel,
        out_shape=jax.ShapeDtypeStruct((32, 72, 128), BF16),
        in_specs=[vmem] * 3,
        out_specs=vmem,
        scratch_shapes=[pltpu.VMEM((HI * ROWS, 256), F32)],
        compiler_params=pltpu.CompilerParams(vmem_limit_bytes=20 << 20),
        cost_estimate=pl.CostEstimate(flops=5_000_000_000, bytes_accessed=4_000_000, transcendentals=0),
        name="by_entry",
    )(pairs, index, sums)


def unpack_kernel(got_ref, qkv_out, proj_out, bias_out, gain_out, scale_out, flat_ref):
    def tile(n, slots, at):
        return got_ref[n // slots, at + n % slots].astype(F32)

    for n in range(24):
        rows = pl.ds(8 * n, 8)
        for c in range(4):
            qkv_out[rows, 128 * c : 128 * c + 128] = tile(n * 6 + c, 5, 0)
        mid = tile(n * 6 + 4, 5, 0)
        qkv_out[rows, 512:576] = mid[:, :64]
        proj_out[rows, :128] = tile(n * 6 + 5, 5, 0)
        proj_out[rows, 128:192] = pltpu.roll(mid, 64, 1)[:, :64]
    for n in range(59):
        flat_ref[8 * n : 8 * n + 8, :] = tile(2 * n, 4, 5)
        flat_ref[472 + 8 * n : 480 + 8 * n, :] = tile(2 * n + 1, 4, 5)
    for k in range(2 * HI):
        size = min(128, 3312 - 128 * k)
        for aw in range(3):
            for h in range(HEADS):
                part = flat_ref[pl.ds(472 * (k % 2) + 36 * (k // 2) + 12 * aw + h, 2, stride=HEADS), :]
                bias_out[aw, h, :, 128 * k : 128 * k + size] = part[:, :size]
    rest = tile(150, 5, 0) + tile(151, 5, 0)
    gain_out[:, :128] = rest[0:1]
    gain_out[:, 128:192] = rest[1:2, :64]
    scale_out[...] = rest[2:3, :HEADS]


def unpack(got):
    vmem = pl.BlockSpec(memory_space=pltpu.VMEM)
    return pl.pallas_call(
        unpack_kernel,
        out_shape=(
            jax.ShapeDtypeStruct((192, 576), F32),
            jax.ShapeDtypeStruct((192, 192), F32),
            jax.ShapeDtypeStruct((3, HEADS, 2, 3312), F32),
            jax.ShapeDtypeStruct((1, 192), F32),
            jax.ShapeDtypeStruct((1, HEADS), F32),
        ),
        in_specs=[vmem],
        out_specs=(vmem,) * 5,
        scratch_shapes=[pltpu.VMEM((944, 128), F32)],
        compiler_params=pltpu.CompilerParams(vmem_limit_bytes=20 << 20),
        name="unpack",
    )(got)


def moved(value, lon_by, lat_by):
    lon_n, lat_n = 64, 4
    pairs = []
    for lon in range(lon_n):
        for lat in range(lat_n):
            to = (lon + lon_by) % lon_n * lat_n + (lat + lat_by) % lat_n
            pairs.append((lon * lat_n + lat, to))
    return lax.ppermute(value, AXES, pairs)


def half(x):
    return lax.reduce_precision(x, 8, 7)


def sum_everywhere(parts, leaving):
    parts = lax.all_to_all(parts, LAYER, 0, 0, tiled=True).astype(F32)
    mine = lax.axis_index(LAYER) == 30

    def rounded(x):
        both = x[:8] + x[8:16]
        high = half(both)
        split = jnp.concatenate([high, both - high, x[16:]], axis=0)
        return jnp.where(mine, split, x).astype(BF16)

    weights = jnp.sum(parts[:, :40], 0)
    bands = jnp.sum(parts[:, 40:].reshape(8, 4, 32, 128), 0).reshape(128, 128)
    layer = jnp.concatenate([rounded(weights), bands.astype(BF16)], axis=0)
    layer, leaving = lax.optimization_barrier((layer, leaving))
    layers = lax.all_to_all(jnp.broadcast_to(layer, (8, 168, 128)), "z", 0, 0, tiled=True)
    lon_out, lat_out, diag_out = leaving
    arrived = (moved(lon_out, 1, 0), moved(lat_out, 0, 1), moved(diag_out, 1, 1))
    layers, arrived = lax.optimization_barrier((layers, arrived))
    total = jnp.sum(layers.astype(F32), 0)
    weights = jnp.broadcast_to(rounded(total[:40]), (8, 4, 40, 128))
    bands = jnp.broadcast_to(total[40:].astype(BF16).reshape(4, 32, 128), (8, 4, 32, 128))
    parts = jnp.concatenate([weights, bands], axis=2).reshape(32, 72, 128)
    return lax.all_to_all(parts, LAYER, 0, 0, tiled=True), arrived


def on_device(tokens, cotangent, labels, w_qkv, w_proj, logit_scale, bias_table, bias_index, norm_gain):
    lon_in, lat_in, diag_in = leaving(tokens, cotangent)
    lat_in = moved(lat_in, 0, -1)
    lon_in = moved(lon_in, -1, 0)
    diag_in = moved(diag_in, -1, -1)

    *bias, index = pair_bias(bias_table.transpose(0, 2, 1, 3), bias_index)

    label_win = labels.reshape(2, 2, 3, 6, 12).transpose(2, 0, 1, 3, 4).reshape(6, 1, WIN).astype(F32)

    grads, sums, pairs = sublayer(
        tokens,
        cotangent,
        lon_in,
        lat_in,
        diag_in,
        label_win,
        w_qkv,
        w_proj,
        norm_gain[None],
        logit_scale[None],
        *(pltpu.with_memory_space_constraint(part, pltpu.HBM) for part in bias),
    )
    parts = by_entry(pairs, index, sums)
    own, *back = returns(grads, w_qkv)
    got, (lon_back, lat_back, diag_back) = sum_everywhere(parts, tuple(back))
    grad_qkv, grad_proj, grad_bias, grad_gain, grad_scale = unpack(got.reshape(32, 9, 8, 128))
    lon_back, lat_back, diag_back = unpacked(lon_back, 4, 15), unpacked(lat_back, 4, 3), unpacked(diag_back, 4, 3)
    returned = jnp.concatenate(
        [jnp.concatenate([diag_back, lat_back], axis=2), jnp.concatenate([lon_back, own], axis=2)], axis=1
    )
    grad_tokens = (cotangent.astype(F32) + returned.astype(F32)).astype(BF16)
    return (
        grad_tokens,
        grad_qkv,
        grad_proj,
        grad_scale[0],
        grad_bias.transpose(0, 2, 1, 3),
        grad_gain[0],
    )


def solution(mesh):
    fine = Mesh(mesh.devices.reshape(8, 4, 2, 2, 2), AXES)
    lon, lat = ("z", "y", "xl"), ("xh", "core")
    placed = (
        P(None, lat, lon, None),
        P(None, lat, lon, None),
        P(None, lat, lon),
        P(),
        P(),
        P(),
        P(lat, None, None, None),
        P(),
        P(),
    )
    return jax.shard_map(
        on_device,
        mesh=fine,
        in_specs=placed,
        out_specs=(P(None, lat, lon, None), P(), P(), P(), P(lat, None, None, None), P()),
        check_vma=False,
    )
```
